512 devices in a mesh: dp: 32 (over x, z_hi, core), mp: 16 (over y, z_lo).
Axes of the slice: x: 4, y: 4, z: 16 (z_hi: 4, z_lo: 4; z = z_hi * 4 + z_lo), core: 2. Of those that a mesh axis runs over, the one named last changes fastest.
Arguments:
- pool: bfloat16 [256, 32, 5120], P('dp', None, 'mp'), may hold values from -20 to 20
- send_table: int32 [32, 32], P('dp'), may hold values from -1 to 7, as said below
- slot_source: int32 [256], P('dp'), may hold values from 0 to 31, as said below
- multiplicity: int32 [256], P('dp'), may hold values from 1 to 4
- slot_weight: float32 [256], P('dp'), may hold values from 0.1 to 1
- cotangent: bfloat16 [256, 32, 4096], P('dp', None, 'mp'), may hold values from -6 to 6
- w_query: bfloat16 [5120, 4096], P(None, 'mp'), may hold values from -0.078125 to 0.078125
- w_key: bfloat16 [5120, 512], P('mp'), may hold values from -0.078125 to 0.078125
- w_value: bfloat16 [5120, 512], P('mp'), may hold values from -0.078125 to 0.078125
- query_gain: float32 [128], replicated, may hold values from 0.5 to 5
- key_gain: float32 [128], replicated, may hold values from 0.5 to 5
Outputs:
- attended: bfloat16 [256, 32, 4096], P('dp', None, 'mp')
- grad_query: float32 [5120, 4096], P('dp', 'mp')
- key_gradient: float32 [5120, 512], P('mp', 'dp')
- grad_value: float32 [5120, 512], P('mp', 'dp')
The draws below stay inside these ranges and needn't reach their ends.
Inputs may be any that keep to these rules, and one draw needn't show every extreme that they name: Entry [r, d] is the sequence of rank r's pool of 8 that data rank d receives from rank r, or -1 where rank d takes nothing from rank r; send_table[r, d] >= 0 exactly where r is among the sources of rank d's slots. `slot_source`: the 8 slots of data rank d (entries d * 8 to d * 8 + 7) name 8 different source ranks.
All inputs are finite; a program needn't handle non-finite values.
Results may differ from the reference program's by a relative error of at most 0.025.
The reference program's roundings to bfloat16 on the way count: a program that leaves them out, or rounds other values in their place, can miss the bound.
Values may be sent and summed in bfloat16 or wider, within the bound.
A program may use at most 64 MiB of HBM per device.

```python
import math
import jax
import jax.numpy as jnp
from jax import lax

D = 5120
HEAD_DIM = 128
HEADS = 32
KV_HEADS = 4
LENGTH = 32
SLOTS = 8
POOL = 8
SEQS = 256
SAMPLES = 256
N_DP = 32


def sample_plan(key):
    score_key, forced_key, pick_key, spot_key, popular_key = jax.random.split(key, 5)
    usage_frequency = jax.random.randint(popular_key, (N_DP,), 1, 9)
    random_jitter = jax.random.randint(score_key, (N_DP, N_DP), 0, 65536)
    pinned_choice = jax.random.permutation(forced_key, N_DP)
    source_index = jnp.arange(N_DP, dtype=jnp.int32)
    extra_reward = jnp.where(source_index[None, :] == pinned_choice[:, None], 1 << 20, 0)
    score_matrix = (random_jitter * usage_frequency[None, :] + extra_reward) * N_DP + source_index[None, :]
    ignored, sources = lax.top_k(score_matrix, SLOTS)
    picks = jax.random.randint(pick_key, (N_DP, SLOTS), 0, POOL)
    row_key, col_key = jax.random.split(spot_key)
    spot_row = jax.random.randint(row_key, (), 0, N_DP)
    spot_col = jax.random.randint(col_key, (), 0, SLOTS)
    picks = picks.at[spot_row, spot_col].set(POOL - 1)
    return (sources.astype(jnp.int32), picks.astype(jnp.int32))


def draw_send_table(key, part):
    sources, picks = sample_plan(key)
    columns = jnp.broadcast_to(jnp.arange(N_DP, dtype=jnp.int32)[:, None], (N_DP, SLOTS))
    table = jnp.full((N_DP, N_DP), -1, jnp.int32)
    return table.at[sources, columns].set(picks)


def draw_slot_source(key, part):
    sources, picks = sample_plan(key)
    return sources.reshape(-1).astype(jnp.int32)


def draw_pool(key, part):
    key = jax.random.fold_in(key, 5)
    first, second = jax.random.split(key)
    scale = jnp.exp(jax.random.uniform(first, (SEQS, LENGTH, 1), jnp.float32, -1.15, 1.15))
    values = jnp.clip(jax.random.normal(second, (SEQS, LENGTH, D), jnp.float32), -6.0, 6.0)
    return (scale * values).astype(jnp.bfloat16)


def gain_values(key, lower, upper):
    return jax.random.uniform(key, (HEAD_DIM,), jnp.float32, lower, upper)


def draw_query_gain(key, part):
    key = jax.random.fold_in(key, 3)
    return gain_values(key, 0.5, 1.5)


def draw_key_gain(key, part):
    key = jax.random.fold_in(key, 4)
    return gain_values(key, 0.5, 1.5)


def touch_ends(values, rng, smallest, top_value):
    dims = values.shape
    place = [jax.random.randint(jax.random.fold_in(rng, axis), (), 0, dims[axis]) for axis in range(len(dims))]
    values = values.at[tuple(place)].set(smallest)
    longest = dims.index(max(dims))
    place[longest] = (place[longest] + 1) % dims[longest]
    return values.at[tuple(place)].set(top_value)


def levels(rng, extent, cuts, low, high):
    loudness, own = 1.0, jax.random.fold_in(rng, 6)
    for dim, shards_of in cuts:
        draws = jnp.exp(jax.random.uniform(jax.random.fold_in(own, dim), (shards_of,), jnp.float32, low / len(cuts), high / len(cuts)))
        loudness = loudness * jnp.repeat(draws, extent[dim] // shards_of).reshape([-1 if axis == dim else 1 for axis in range(len(extent))])
    return loudness


def noise(own_key, dims, scale, bound, cuts=(), held_as=jnp.bfloat16):
    factor_of = levels(own_key, dims, cuts, -0.22, 0.18) if cuts else 1.0
    result = jax.random.normal(own_key, dims, jnp.float32) * scale * factor_of
    return jnp.minimum(jnp.maximum(result, -bound), bound).astype(held_as)


def setup_inputs(seed: int = 0) -> dict:
    arg_keys = jax.random.split(jax.random.key(seed), 12)
    pool = draw_pool(jax.random.fold_in(arg_keys[11], 71), 0)
    send_table = draw_send_table(jax.random.fold_in(arg_keys[11], 71), 0)
    slot_source = draw_slot_source(jax.random.fold_in(arg_keys[11], 71), 0)
    multiplicity = touch_ends(jax.random.randint(arg_keys[3], (SAMPLES,), 1, 5), jax.random.fold_in(arg_keys[3], 1), 1, 4).astype(jnp.int32)
    slot_weight = jnp.clip(jnp.exp(math.log(1.0) - 2.3025851 * jax.random.uniform(arg_keys[4], (SAMPLES,), jnp.float32) ** levels(arg_keys[4], (SAMPLES,), ((0, 32),), -0.2, 0.2)), 0.1, 1.0)
    cotangent = noise(arg_keys[5], (SAMPLES, LENGTH, HEADS * HEAD_DIM), 1.0, 6.0, ((0, 32), (2, 16)))
    w_query = noise(arg_keys[6], (D, HEADS * HEAD_DIM), D ** -0.5, 0.078125, ((1, 16),))
    w_key = noise(arg_keys[7], (D, KV_HEADS * HEAD_DIM), D ** -0.5, 0.078125, ((0, 16),))
    w_value = noise(arg_keys[8], (D, KV_HEADS * HEAD_DIM), D ** -0.5, 0.078125, ((0, 16),))
    query_gain = draw_query_gain(jax.random.fold_in(arg_keys[11], 71), 0)
    key_gain = draw_key_gain(jax.random.fold_in(arg_keys[11], 71), 0)
    return dict(pool=pool, send_table=send_table, slot_source=slot_source, multiplicity=multiplicity, slot_weight=slot_weight, cotangent=cotangent, w_query=w_query, w_key=w_key, w_value=w_value, query_gain=query_gain, key_gain=key_gain)


def rms_scale(values, gain):
    inverse = lax.rsqrt(lax.optimization_barrier(jnp.mean(values * values, axis=-1, keepdims=True)) + 1e-06)
    return (values * inverse * gain, inverse)

def rms_back(values, inverse, gain, grad_out):
    scaled = grad_out * gain
    inner = lax.optimization_barrier(jnp.mean(values * scaled, axis=-1, keepdims=True))
    return inverse * scaled - values * (inverse * inverse * inverse) * inner

def forward_core(query, key_sum, value_sum, query_gain, key_gain):
    scale = 1.0 / math.sqrt(query.shape[-1])
    q_norm, q_inverse = rms_scale(query, query_gain)
    k_norm, k_inverse = rms_scale(key_sum, key_gain)
    q_half = q_norm.astype(jnp.bfloat16)
    k_half = k_norm.astype(jnp.bfloat16)
    v_half = value_sum.astype(jnp.bfloat16)
    score_matrix = jnp.einsum('sqgph,skgh->sgpqk', q_half.astype(jnp.float32), k_half.astype(jnp.float32)) * scale
    length = query.shape[1]
    causal = lax.broadcasted_iota(jnp.int32, (length, length), 0) >= lax.broadcasted_iota(jnp.int32, (length, length), 1)
    score_matrix = jnp.where(causal, score_matrix, -1e+30)
    peak = lax.optimization_barrier(jnp.max(score_matrix, axis=-1, keepdims=True))
    raised = jnp.exp(score_matrix - peak)
    probs = raised / lax.optimization_barrier(jnp.sum(raised, axis=-1, keepdims=True))
    p_half = probs.astype(jnp.bfloat16)
    attended = jnp.einsum('sgpqk,skgh->sqgph', p_half.astype(jnp.float32), v_half.astype(jnp.float32))
    return (attended, (q_inverse, k_inverse, q_half, k_half, v_half, probs, p_half))

def backward_core(d_out, query, key_sum, query_gain, key_gain, saved):
    q_inverse, k_inverse, q_half, k_half, v_half, probs, p_half = saved
    scale = 1.0 / math.sqrt(query.shape[-1])
    out_half = d_out.astype(jnp.bfloat16).astype(jnp.float32)
    d_probs = jnp.einsum('sqgph,skgh->sgpqk', out_half, v_half.astype(jnp.float32))
    d_value = jnp.einsum('sgpqk,sqgph->skgh', p_half.astype(jnp.float32), out_half)
    d_scores = probs * (d_probs - lax.optimization_barrier(jnp.sum(d_probs * probs, axis=-1, keepdims=True))) * scale
    score_half = d_scores.astype(jnp.bfloat16).astype(jnp.float32)
    d_qnorm = jnp.einsum('sgpqk,skgh->sqgph', score_half, k_half.astype(jnp.float32))
    d_knorm = jnp.einsum('sgpqk,sqgph->skgh', score_half, q_half.astype(jnp.float32))
    d_query = rms_back(query, q_inverse, query_gain, d_qnorm)
    d_key = rms_back(key_sum, k_inverse, key_gain, d_knorm)
    return (d_query, d_key, d_value)

def rounded(term):
    half = lax.optimization_barrier(term.astype(jnp.bfloat16))
    return half.astype(jnp.float32)

def reference(pool, send_table, slot_source, multiplicity, slot_weight, cotangent, w_query, w_key, w_value, query_gain, key_gain):
    group_size = HEADS // KV_HEADS
    query_cols = HEADS * HEAD_DIM
    key_cols = KV_HEADS * HEAD_DIM
    token_count = SLOTS * LENGTH
    destination = (jnp.arange(SAMPLES, dtype=jnp.int32) // SLOTS).astype(jnp.int32)
    local_index = send_table[slot_source, destination]
    pool_row = (slot_source * POOL + local_index).astype(jnp.int32)
    factor = multiplicity.astype(jnp.float32) * slot_weight / LENGTH

    def rank_step(carry, inputs):
        grad_query, key_gradient, grad_value = carry
        row_index, cot_rank, factor_rank = inputs
        chosen = jnp.take(pool, row_index, axis=0)
        flat = chosen.reshape(token_count, D)
        query = jnp.dot(flat, w_query, preferred_element_type=jnp.float32).reshape(SLOTS, LENGTH, KV_HEADS, group_size, HEAD_DIM)
        key_sum = jnp.dot(flat, w_key, preferred_element_type=jnp.float32).reshape(SLOTS, LENGTH, KV_HEADS, HEAD_DIM)
        value_sum = jnp.dot(flat, w_value, preferred_element_type=jnp.float32).reshape(SLOTS, LENGTH, KV_HEADS, HEAD_DIM)
        attended, saved = forward_core(query, key_sum, value_sum, query_gain, key_gain)
        d_out = cot_rank.astype(jnp.float32).reshape(SLOTS, LENGTH, KV_HEADS, group_size, HEAD_DIM) * factor_rank[:, None, None, None, None]
        d_query, d_key, d_value = backward_core(d_out, query, key_sum, query_gain, key_gain, saved)
        query_rows = d_query.reshape(token_count, query_cols).astype(jnp.bfloat16)
        key_rows = d_key.reshape(token_count, key_cols).astype(jnp.bfloat16)
        value_rows = d_value.reshape(token_count, key_cols).astype(jnp.bfloat16)
        grad_query = grad_query + rounded(jnp.dot(flat.T, query_rows, preferred_element_type=jnp.float32))
        key_gradient = key_gradient + rounded(jnp.dot(flat.T, key_rows, preferred_element_type=jnp.float32))
        grad_value = grad_value + rounded(jnp.dot(flat.T, value_rows, preferred_element_type=jnp.float32))
        return ((grad_query, key_gradient, grad_value), attended.reshape(SLOTS, LENGTH, query_cols).astype(jnp.bfloat16))
    start = (jnp.zeros((D, query_cols), jnp.float32), jnp.zeros((D, key_cols), jnp.float32), jnp.zeros((D, key_cols), jnp.float32))
    scanned = (pool_row.reshape(N_DP, SLOTS), cotangent.reshape(N_DP, SLOTS, LENGTH, query_cols), factor.reshape(N_DP, SLOTS))
    (grad_query, key_gradient, grad_value), attended = lax.scan(rank_step, start, scanned)
    return (attended.reshape(SAMPLES, LENGTH, query_cols), grad_query, key_gradient, grad_value)
```

```python
import functools
import math

import jax
import jax.numpy as jnp
from jax import lax
from jax.experimental import pallas as pl
from jax.experimental.pallas import tpu as pltpu
from jax.sharding import PartitionSpec as P

F32, BF16 = jnp.float32, jnp.bfloat16
MESH = pl.DeviceIdType.MESH

N_X, N_ZH, N_CORE, N_Y, N_ZL = 4, 4, 2, 4, 4
N_DP, N_MP = N_X * N_ZH * N_CORE, N_Y * N_ZL
SEQS, LENGTH, WIDTH = 8, 32, 320
TOKENS = SEQS * LENGTH
HEAD, COLS = 128, 256
PADDED = 384
SHARE = WIDTH // N_X
HALF = WIDTH // 2
EPS = 1e-6
SCALE = 1.0 / math.sqrt(HEAD)


def dot_nn(a, b):
    return lax.dot_general(a, b, (((1,), (0,)), ((), ())), preferred_element_type=F32)


def dot_tn(a, b):
    return lax.dot_general(a, b, (((0,), (0,)), ((), ())), preferred_element_type=F32)


def dot_nt(a, b):
    return lax.dot_general(a, b, (((1,), (1,)), ((), ())), preferred_element_type=F32)


def rms_back(values, inverse, gain, grad_out):
    scaled = grad_out * gain
    inner = jnp.mean(values * scaled, axis=0, keepdims=True)
    return inverse * scaled - values * (inverse * inverse * inverse) * inner


def kernel(
    table,
    source,
    x_ref,
    w_mine,
    w_query,
    d_out,
    target,
    q_gain,
    k_gain,
    att_out,
    gq_out,
    gkv_out,
    piece,
    w_kv,
    d_send,
    d_slots,
    acc_q,
    acc_kv,
    att,
    att_send,
    att_slots,
    d_query,
    g_send,
    g_recv,
    g_keep,
    x_recv,
    z_send,
    z_recv,
    dkv,
    dkv_recv,
    dkv_all,
    kv_part,
    kv_recv,
    kv_sum,
    kv_x,
    kv_zs,
    kv_z,
    tz_s,
    tz_r,
    ty_s,
    ty_r,
    tf_s,
    tf_r,
    w1_s,
    w1_r,
    w2_s,
    w2_r,
    w3_s,
    w3_r,
    co_s,
    co_r,
    at_s,
    at_r,
    k1_s,
    k1_r,
    k2_s,
    k2_r,
    k3_s,
    k3_r,
    gc_s,
    gc_r,
    gx_s,
    gx_r,
    gz_s,
    gz_r,
    vc_s,
    vc_r,
    vx_s,
    vx_r,
    vz_s,
    vz_r,
):
    dp, mp = lax.axis_index("dp"), lax.axis_index("mp")
    x, zh, core = dp // (N_ZH * N_CORE), (dp // N_CORE) % N_ZH, dp % N_CORE
    y, zl = mp // N_ZL, mp % N_ZL
    other = 1 - core

    def at_dp(step):
        return lax.rem(dp + step, N_DP), mp

    def at_mp(step):
        return dp, lax.rem(mp + step, N_MP)

    def at_x(step):
        return lax.rem(dp + step * (N_ZH * N_CORE), N_DP), mp

    def at_zh(step):
        return x * (N_ZH * N_CORE) + lax.rem(zh + step, N_ZH) * N_CORE + core, mp

    def at_y(step):
        return dp, lax.rem(mp + step * N_ZL, N_MP)

    def at_zl(step):
        return dp, y * N_ZL + lax.rem(zl + step, N_ZL)

    sibling = (dp + 1 - 2 * core, mp)

    def copy(src, dst, send, recv, device):
        return pltpu.make_async_remote_copy(
            src_ref=src,
            dst_ref=dst,
            send_sem=send,
            recv_sem=recv,
            device_id=device,
            device_id_type=MESH,
        )

    sends = []

    def start(*args):
        made = copy(*args)
        made.start()
        sends.append(made)

    barrier = pltpu.get_barrier_semaphore()
    for step in range(1, N_DP):
        pl.semaphore_signal(barrier, inc=1, device_id=at_dp(step), device_id_type=MESH)
    for step in range(1, N_MP):
        pl.semaphore_signal(barrier, inc=1, device_id=at_mp(step), device_id_type=MESH)
    pl.semaphore_wait(barrier, N_DP - 1 + N_MP - 1)

    def block(step_y, step_z):
        return lax.rem(y + step_y, N_Y) * N_ZL + lax.rem(zl + step_z, N_ZL)

    def mine(step):
        return block(0, N_ZL - step)

    def near(k, way):
        return block(N_Y - 1 if way == 0 else 1, N_ZL - k if k else 0)

    piece[mp] = x_ref[:WIDTH]
    tokens = x_ref.at[pl.ds(0, WIDTH)]
    for k in (1, 2, 3):
        start(tokens, piece.at[mp], tz_s.at[k], tz_r.at[k], at_zl(k))
    for way, step in ((0, 1), (1, N_Y - 1)):
        start(tokens, piece.at[mp], ty_s.at[0, way], ty_r.at[0, way], at_y(step))

    rows = pl.ds(pl.multiple_of(x * SHARE, 16), SHARE)
    w_kv[core, mp, rows] = w_mine[y]
    for step in range(1, N_MP):
        dest = at_mp(step)
        start(w_mine.at[dest[1] // N_ZL], w_kv.at[core, mp, rows], w1_s, w1_r, dest)

    for k in range(N_DP):
        wanted = lax.rem(dp + k, N_DP)
        slot = jnp.int32(SEQS)
        for s in range(SEQS):
            slot = jnp.where(source[s] == wanted, jnp.int32(s), slot)
        d_send[k] = d_out[slot]
        if k:
            start(d_send.at[k], d_slots.at[k], co_s, co_r, at_dp(k))
    d_slots[0] = d_send[0]

    acc_q[...] = jnp.zeros_like(acc_q)

    def project(j):
        place = pl.ds(pl.multiple_of(j * WIDTH, WIDTH), WIDTH)
        acc_q[...] += dot_tn(w_query[place], piece[j])

    def wait_near(k, way):
        spot = piece.at[near(k, way)]
        copy(spot, spot, ty_s.at[k, way], ty_r.at[k, way], at_y(1)).wait_recv()

    def pass_on(k):
        for way, step in ((0, 1), (1, N_Y - 1)):
            wait_near(k, way)
            half = piece.at[near(k, way), pl.ds(way * HALF, HALF)]
            start(half, half, tf_s.at[k, way], tf_r.at[k, way], at_y(step))

    def take(k):
        spot = piece.at[mine(k)]
        copy(spot, spot, tz_s.at[k], tz_r.at[k], at_zl(1)).wait_recv()
        for way, step in ((0, 1), (1, N_Y - 1)):
            start(spot, spot, ty_s.at[k, way], ty_r.at[k, way], at_y(step))

    project(mp)
    take(1)
    project(mine(1))
    pass_on(0)
    take(2)
    project(mine(2))
    take(3)
    project(mine(3))
    got = w_kv.at[0, pl.ds(0, N_MP - 1), pl.ds(0, SHARE)]
    copy(got, got, w1_s, w1_r, at_mp(1)).wait_recv()
    part = w_kv.at[core, :, rows]
    for k in (1, 2, 3):
        start(part, part, w2_s.at[k], w2_r.at[k], at_x(k))
    for way in (0, 1):
        project(near(0, way))
    for k in (1, 2, 3):
        pass_on(k)
        for way in (0, 1):
            project(near(k, way))
    for k in (1, 2, 3):
        copy(part, part, w2_s.at[k], w2_r.at[k], at_x(k)).wait_recv()
    start(w_kv.at[core], w_kv.at[core], w3_s, w3_r, sibling)
    for k in range(N_ZL):
        far = block(2, N_ZL - k if k else 0)
        for way in (0, 1):
            half = piece.at[far, pl.ds(way * HALF, HALF)]
            copy(half, half, tf_s.at[k, way], tf_r.at[k, way], at_y(1)).wait_recv()
        project(far)
    copy(w_kv.at[other], w_kv.at[other], w3_s, w3_r, sibling).wait_recv()
    acc_kv[...] = jnp.zeros_like(acc_kv)

    def project_kv(j, carry):
        for half in (0, 1):
            acc_kv[half] += dot_tn(w_kv[half, j], piece[j])
        return carry

    lax.fori_loop(0, N_MP, project_kv, 0)

    gain_q, gain_k = q_gain[...], k_gain[...]
    key_sum = acc_kv[0]
    k_inverse = lax.rsqrt(jnp.mean(key_sum * key_sum, axis=0, keepdims=True) + EPS)
    k_norm = (key_sum * k_inverse * gain_k).astype(BF16)
    value = acc_kv[1].astype(BF16)
    at_key = lax.broadcasted_iota(jnp.int32, (TOKENS, TOKENS), 0)
    at_query = lax.broadcasted_iota(jnp.int32, (TOKENS, TOKENS), 1)
    seen = ((at_key >> 5) == (at_query >> 5)) & (at_key <= at_query)
    saved = []
    for h in range(COLS // HEAD):
        query = acc_q[h * HEAD : (h + 1) * HEAD]
        inverse = lax.rsqrt(jnp.mean(query * query, axis=0, keepdims=True) + EPS)
        q_norm = (query * inverse * gain_q).astype(BF16)
        scores = jnp.where(seen, dot_tn(k_norm, q_norm) * SCALE, -1e30)
        raised = jnp.exp(scores - jnp.max(scores, axis=0, keepdims=True))
        probs = raised / jnp.sum(raised, axis=0, keepdims=True)
        p_half = probs.astype(BF16)
        out = dot_nn(value, p_half).T.astype(BF16)
        att[:, :, h * HEAD : (h + 1) * HEAD] = out.reshape(SEQS, LENGTH, HEAD)
        saved.append((query, inverse, q_norm, probs, p_half))
    for k in range(N_DP):
        spot = table[0, lax.rem(dp + k, N_DP)]
        att_send[k] = att[jnp.maximum(spot, 0)]
        if k:
            start(att_send.at[k], att_slots.at[k], at_s, at_r, at_dp(k))
    att_slots[0] = att_send[0]

    got = d_slots.at[pl.ds(1, N_DP - 1)]
    copy(got, got, co_s, co_r, at_dp(1)).wait_recv()
    place = lax.broadcasted_iota(jnp.int32, (TOKENS, N_DP * LENGTH), 0)
    chosen = jnp.where(place == target[...], 1.0, 0.0).astype(BF16)
    d_rows = dot_nn(chosen, d_slots[...].reshape(N_DP * LENGTH, COLS))
    d_cols = d_rows.T.astype(BF16)
    d_knorm = jnp.zeros((HEAD, TOKENS), F32)
    d_value = jnp.zeros((HEAD, TOKENS), F32)
    d_queries = []
    for h in range(COLS // HEAD):
        query, inverse, q_norm, probs, p_half = saved[h]
        out_half = d_cols[h * HEAD : (h + 1) * HEAD]
        d_probs = dot_tn(value, out_half)
        d_value += dot_nt(out_half, p_half)
        centred = d_probs - jnp.sum(d_probs * probs, axis=0, keepdims=True)
        score_half = (probs * centred * SCALE).astype(BF16)
        d_qnorm = dot_nn(k_norm, score_half)
        d_knorm += dot_nt(q_norm, score_half)
        d_queries.append(rms_back(query, inverse, gain_q, d_qnorm))
    for h in range(COLS // HEAD):
        d_query[:, h * HEAD : (h + 1) * HEAD] = d_queries[h].T.astype(BF16)
    d_key = rms_back(key_sum, k_inverse, gain_k, d_knorm).astype(BF16)
    d_value = d_value.astype(BF16)
    for q in (0, 1):
        dkv[q] = d_key[q * 64 : (q + 1) * 64]
        dkv[2 + q] = d_value[q * 64 : (q + 1) * 64]

    for k in (1, 2, 3):
        start(
            dkv.at[lax.rem(zl + k, N_ZL)],
            dkv_recv.at[k],
            k1_s.at[k],
            k1_r.at[k],
            at_zl(k),
        )

    def partial_rows(to, into, which):
        def one(i, carry):
            rows = pl.ds(pl.multiple_of(which * HALF, 16), HALF)
            total = dot_nn(piece[to * N_ZH + i, rows], d_query[...])
            into[to, i] = total.astype(BF16)
            return carry

        lax.fori_loop(0, N_ZH, one, 0)

    def x_at(step):
        return lax.rem(x + step, N_X)

    order = (2, 1, 3, 0)
    for k in order:
        to = x_at(k)
        partial_rows(to, g_send, other)
        start(g_send.at[to], g_recv.at[to], gc_s.at[k], gc_r.at[k], sibling)
    for k in order:
        partial_rows(x_at(k), g_keep, core)

    for k in (1, 2, 3):
        copy(
            dkv.at[0], dkv_recv.at[k], k1_s.at[k], k1_r.at[k], at_zl(k)
        ).wait_recv()
    total = dkv[zl].astype(F32)
    for k in (1, 2, 3):
        total += dkv_recv[k].astype(F32)
    dkv_all[y, zl] = total.astype(BF16)
    spot = dkv_all.at[y, zl]
    for k in (1, 2, 3):
        start(spot, spot, k2_s.at[k], k2_r.at[k], at_zl(k))

    for k in order:
        to = x_at(k)
        copy(
            g_send.at[to], g_recv.at[to], gc_s.at[k], gc_r.at[k], sibling
        ).wait_recv()
        both = g_keep[to].astype(F32) + g_recv[to].astype(F32)
        g_keep[to] = both.astype(BF16)
        if k:
            for kz in order:
                to_z = lax.rem(zh + kz, N_ZH)
                start(
                    g_keep.at[to, to_z],
                    x_recv.at[k, to_z],
                    gx_s.at[k, kz],
                    gx_r.at[k, kz],
                    at_x(k),
                )

    for k in (1, 2, 3):
        copy(spot, spot, k2_s.at[k], k2_r.at[k], at_zl(k)).wait_recv()
    group = dkv_all.at[y]
    for k in (1, 2, 3):
        start(group, group, k3_s.at[k], k3_r.at[k], at_y(k))
    for k in (1, 2, 3):
        copy(group, group, k3_s.at[k], k3_r.at[k], at_y(k)).wait_recv()

    def kv_rows(g, carry):
        rows = dkv_all[g].reshape(2 * HEAD, TOKENS)
        product = dot_nt(rows, x_ref[...]).astype(BF16)
        for half in range(2):
            for i in range(N_ZH):
                for c in range(N_CORE):
                    first = half * HEAD + i * 32 + c * 16
                    kv_part[c, g, i, half] = product[first : first + 16]
        return carry

    lax.fori_loop(0, N_X, kv_rows, 0)
    start(kv_part.at[other], kv_recv, vc_s, vc_r, sibling)

    for kz in order:
        to_z = lax.rem(zh + kz, N_ZH)
        total = g_keep[x, to_z].astype(F32)
        for k in (1, 2, 3):
            spot = x_recv.at[k, to_z]
            copy(spot, spot, gx_s.at[k, kz], gx_r.at[k, kz], at_x(k)).wait_recv()
            total += x_recv[k, to_z].astype(F32)
        z_send[to_z] = total.astype(BF16)
        if kz:
            start(
                z_send.at[to_z], z_recv.at[kz], gz_s.at[kz], gz_r.at[kz], at_zh(kz)
            )

    copy(kv_part.at[other], kv_recv, vc_s, vc_r, sibling).wait_recv()
    kv_sum[...] = (kv_part[core].astype(F32) + kv_recv[...].astype(F32)).astype(BF16)
    for k in (1, 2, 3):
        start(kv_sum.at[x_at(k)], kv_x.at[k], vx_s.at[k], vx_r.at[k], at_x(k))
    total = kv_sum[x].astype(F32)
    for k in (1, 2, 3):
        copy(kv_sum.at[0], kv_x.at[k], vx_s.at[k], vx_r.at[k], at_x(k)).wait_recv()
        total += kv_x[k].astype(F32)
    kv_zs[...] = total.astype(BF16)
    for k in (1, 2, 3):
        to_z = lax.rem(zh + k, N_ZH)
        start(kv_zs.at[to_z], kv_z.at[k], vz_s.at[k], vz_r.at[k], at_zh(k))

    total = z_send[zh].astype(F32)
    for k in (1, 2, 3):
        copy(z_send.at[0], z_recv.at[k], gz_s.at[k], gz_r.at[k], at_zh(k)).wait_recv()
        total += z_recv[k].astype(F32)
    gq_out[...] = total

    total = kv_zs[zh].astype(F32)
    for k in (1, 2, 3):
        copy(kv_zs.at[0], kv_z.at[k], vz_s.at[k], vz_r.at[k], at_zh(k)).wait_recv()
        total += kv_z[k].astype(F32)
    gkv_out[...] = total

    got = att_slots.at[pl.ds(1, N_DP - 1)]
    copy(got, got, at_s, at_r, at_dp(1)).wait_recv()
    for s in range(SEQS):
        att_out[s] = att_slots[lax.rem(dp + N_DP - source[s], N_DP)]

    for made in sends:
        made.wait_send()


def local(
    pool,
    send_table,
    slot_source,
    multiplicity,
    slot_weight,
    cotangent,
    w_query,
    w_key,
    w_value,
    query_gain,
    key_gain,
):
    dp = lax.axis_index("dp")
    rank_x, core = dp // (N_ZH * N_CORE), dp % N_CORE
    rows = pool.reshape(TOKENS, WIDTH).T
    rows = jnp.pad(rows, ((0, PADDED - WIDTH), (0, 0)))
    weights = jnp.where(core == 0, w_key, w_value)
    weights = lax.dynamic_slice_in_dim(weights, rank_x * SHARE, SHARE, 0)
    weights = weights.reshape(SHARE, N_Y, HEAD).transpose(1, 0, 2)
    factor = multiplicity.astype(F32) * slot_weight / LENGTH
    d_out = (cotangent.astype(F32) * factor[:, None, None]).astype(BF16)
    d_out = jnp.pad(d_out, ((0, 1), (0, 0), (0, 0)))
    entry = send_table[0, (dp + N_DP - jnp.arange(N_DP)) % N_DP]
    target = jnp.where(
        entry[:, None] >= 0, entry[:, None] * LENGTH + jnp.arange(LENGTH)[None, :], -1
    ).reshape(1, N_DP * LENGTH)

    dma = pltpu.SemaphoreType.DMA
    smem = pl.BlockSpec(memory_space=pltpu.SMEM)
    vmem = pl.BlockSpec(memory_space=pltpu.VMEM)
    attended, grad_query, grad_kv = pl.pallas_call(
        kernel,
        out_shape=(
            jax.ShapeDtypeStruct((SEQS, LENGTH, COLS), BF16),
            jax.ShapeDtypeStruct((HALF, COLS), F32),
            jax.ShapeDtypeStruct((2, 16, PADDED), F32),
        ),
        in_specs=[smem, smem] + [vmem] * 7,
        out_specs=(vmem, vmem, vmem),
        scratch_shapes=[
            pltpu.VMEM((N_MP, WIDTH, TOKENS), BF16),
            pltpu.VMEM((2, N_MP, WIDTH, HEAD), BF16),
            pltpu.VMEM((N_DP, LENGTH, COLS), BF16),
            pltpu.VMEM((N_DP, LENGTH, COLS), BF16),
            pltpu.VMEM((COLS, TOKENS), F32),
            pltpu.VMEM((2, HEAD, TOKENS), F32),
            pltpu.VMEM((SEQS, LENGTH, COLS), BF16),
            pltpu.VMEM((N_DP, LENGTH, COLS), BF16),
            pltpu.VMEM((N_DP, LENGTH, COLS), BF16),
            pltpu.VMEM((TOKENS, COLS), BF16),
            pltpu.VMEM((N_X, N_ZH, HALF, COLS), BF16),
            pltpu.VMEM((N_X, N_ZH, HALF, COLS), BF16),
            pltpu.VMEM((N_X, N_ZH, HALF, COLS), BF16),
            pltpu.VMEM((N_X, N_ZH, HALF, COLS), BF16),
            pltpu.VMEM((N_ZH, HALF, COLS), BF16),
            pltpu.VMEM((N_ZH, HALF, COLS), BF16),
            pltpu.VMEM((N_ZL, 64, TOKENS), BF16),
            pltpu.VMEM((N_ZL, 64, TOKENS), BF16),
            pltpu.VMEM((N_Y, N_ZL, 64, TOKENS), BF16),
            pltpu.VMEM((N_CORE, N_X, N_ZH, 2, 16, PADDED), BF16),
            pltpu.VMEM((N_X, N_ZH, 2, 16, PADDED), BF16),
            pltpu.VMEM((N_X, N_ZH, 2, 16, PADDED), BF16),
            pltpu.VMEM((N_X, N_ZH, 2, 16, PADDED), BF16),
            pltpu.VMEM((N_ZH, 2, 16, PADDED), BF16),
            pltpu.VMEM((N_ZH, 2, 16, PADDED), BF16),
            dma((4,)),
            dma((4,)),
            dma((4, 2)),
            dma((4, 2)),
            dma((4, 2)),
            dma((4, 2)),
            dma,
            dma,
            dma((4,)),
            dma((4,)),
            dma,
            dma,
            dma,
            dma,
            dma,
            dma,
            dma((4,)),
            dma((4,)),
            dma((4,)),
            dma((4,)),
            dma((4,)),
            dma((4,)),
            dma((4,)),
            dma((4,)),
            dma((4, 4)),
            dma((4, 4)),
            dma((4,)),
            dma((4,)),
            dma,
            dma,
            dma((4,)),
            dma((4,)),
            dma((4,)),
            dma((4,)),
        ],
        compiler_params=pltpu.CompilerParams(
            collective_id=0, has_side_effects=True, vmem_limit_bytes=48 * 1024 * 1024
        ),
        name="train_step",
    )(
        send_table,
        slot_source,
        rows,
        weights,
        w_query,
        d_out,
        target,
        query_gain[:, None],
        key_gain[:, None],
    )
    key_gradient, grad_value = grad_kv[0, :, :WIDTH].T, grad_kv[1, :, :WIDTH].T
    return attended, grad_query, key_gradient, grad_value


def solution(mesh):
    return jax.shard_map(
        local,
        mesh=mesh,
        in_specs=(
            P("dp", None, "mp"),
            P("dp", None),
            P("dp"),
            P("dp"),
            P("dp"),
            P("dp", None, "mp"),
            P(None, "mp"),
            P("mp", None),
            P("mp", None),
            P(),
            P(),
        ),
        out_specs=(P("dp", None, "mp"), P("dp", "mp"), P("mp", "dp"), P("mp", "dp")),
        check_vma=False,
    )
```

```python
import functools
import math

import jax
import jax.numpy as jnp
from jax import lax
from jax.experimental import pallas as pl
from jax.experimental.pallas import tpu as pltpu
from jax.sharding import PartitionSpec as P

F32, BF16 = jnp.float32, jnp.bfloat16
MESH = pl.DeviceIdType.MESH

N_X, N_ZH, N_CORE, N_Y, N_ZL = 4, 4, 2, 4, 4
N_DP, N_MP = N_X * N_ZH * N_CORE, N_Y * N_ZL
SEQS, LENGTH, WIDTH = 8, 32, 320
TOKENS = SEQS * LENGTH
HEAD, COLS = 128, 256
PADDED = 384
SHARE = WIDTH // N_X
HALF = WIDTH // 2
EPS = 1e-6
PAIRS = ((0, 1), (1, 0), (1, 1), (2, 0), (2, 1), (3, 0), (3, 1))
SCALE = 1.0 / math.sqrt(HEAD)


def dot_nn(a, b):
    return lax.dot_general(a, b, (((1,), (0,)), ((), ())), preferred_element_type=F32)


def dot_tn(a, b):
    return lax.dot_general(a, b, (((0,), (0,)), ((), ())), preferred_element_type=F32)


def dot_nt(a, b):
    return lax.dot_general(a, b, (((1,), (1,)), ((), ())), preferred_element_type=F32)


def rms_back(values, inverse, gain, grad_out):
    scaled = grad_out * gain
    inner = jnp.mean(values * scaled, axis=0, keepdims=True)
    return inverse * scaled - values * (inverse * inverse * inverse) * inner


def kernel(
    table_in,
    source_in,
    drawn_in,
    weight_in,
    pool_in,
    cotangent_in,
    w_query_in,
    w_key_in,
    w_value_in,
    q_gain_in,
    k_gain_in,
    att_out,
    gq_out,
    gk_out,
    gv_out,
    table,
    source,
    drawn,
    weight,
    pool,
    cotangent,
    w_query,
    w_key,
    w_value,
    q_gain,
    k_gain,
    load_s,
    table_row,
    source_row,
    tables,
    sources,
    near_tables,
    near_sources,
    ts_s,
    ts_r,
    x_ref,
    w_mine,
    piece,
    w_kv,
    d_all_0,
    d_all_1,
    d_all_2,
    d_all_3,
    d_send,
    d_slots,
    acc_q,
    acc_kv,
    att_all_0,
    att_all_1,
    att_all_2,
    att_all_3,
    att_send,
    att_slots,
    d_query,
    g_send,
    g_recv,
    g_keep,
    x_recv,
    z_send,
    z_recv,
    dkv,
    dkv_recv,
    dkv_all,
    kv_part,
    kv_recv,
    kv_sum,
    kv_x,
    kv_zs,
    kv_z,
    tz_s,
    tz_r,
    ty_s,
    ty_r,
    tf_s,
    tf_r,
    w1_s,
    w1_r,
    w2_s,
    w2_r,
    w3_s,
    w3_r,
    c1_s,
    c1_r,
    cf_s,
    cf_r,
    c2_s,
    c2_r,
    a1_s,
    a1_r,
    af_s,
    af_r,
    a2_s,
    a2_r,
    k1_s,
    k1_r,
    k2_s,
    k2_r,
    k3_s,
    k3_r,
    gc_s,
    gc_r,
    gx_s,
    gx_r,
    gz_s,
    gz_r,
    vc_s,
    vc_r,
    vx_s,
    vx_r,
    vz_s,
    vz_r,
):
    dp, mp = lax.axis_index("dp"), lax.axis_index("mp")
    x, zh, core = dp // (N_ZH * N_CORE), (dp // N_CORE) % N_ZH, dp % N_CORE
    y, zl = mp // N_ZL, mp % N_ZL
    other = 1 - core

    def pair(step, flip):
        return lax.rem(x + step, N_X) * (N_ZH * N_CORE) + zh * N_CORE + (
            other if flip else core
        )

    def at_mp(step):
        return dp, lax.rem(mp + step, N_MP)

    def at_x(step):
        return lax.rem(dp + step * (N_ZH * N_CORE), N_DP), mp

    def at_zh(step):
        return x * (N_ZH * N_CORE) + lax.rem(zh + step, N_ZH) * N_CORE + core, mp

    def at_y(step):
        return dp, lax.rem(mp + step * N_ZL, N_MP)

    def at_zl(step):
        return dp, y * N_ZL + lax.rem(zl + step, N_ZL)

    sibling = (dp + 1 - 2 * core, mp)
    d_all = (d_all_0, d_all_1, d_all_2, d_all_3)
    att_all = (att_all_0, att_all_1, att_all_2, att_all_3)

    def copy(src, dst, send, recv, device):
        return pltpu.make_async_remote_copy(
            src_ref=src,
            dst_ref=dst,
            send_sem=send,
            recv_sem=recv,
            device_id=device,
            device_id_type=MESH,
        )

    sends = []

    def start(*args):
        made = copy(*args)
        made.start()
        sends.append(made)

    barrier = pltpu.get_barrier_semaphore()
    partners = [at_mp(step) for step in range(1, N_MP)]
    partners += [at_zh(step) for step in range(1, N_ZH)]
    partners += [(pair(step, flip), mp) for step, flip in PAIRS]
    for device in partners:
        pl.semaphore_signal(barrier, inc=1, device_id=device, device_id_type=MESH)

    loads = {}
    for i, (name, src, dst) in enumerate(
        (
            ("pool", pool_in, pool),
            ("w_key", w_key_in, w_key),
            ("w_value", w_value_in, w_value),
            ("table_row", table_in, table_row),
            ("source_row", source_in, source_row),
            ("table", table_in, table),
            ("source", source_in, source),
            ("drawn", drawn_in, drawn),
            ("weight", weight_in, weight),
            ("cotangent", cotangent_in, cotangent),
            ("w_query", w_query_in, w_query),
            ("q_gain", q_gain_in, q_gain),
            ("k_gain", k_gain_in, k_gain),
        )
    ):
        loads[name] = pltpu.make_async_copy(src, dst, load_s.at[i])
        loads[name].start()

    for name in ("pool", "w_key", "w_value"):
        loads[name].wait()
    rows = pool[...].reshape(TOKENS, WIDTH).astype(F32)
    x_ref[:COLS] = rows[:, :COLS].T.astype(BF16)
    rest = [rows[:, COLS:], jnp.zeros((TOKENS, PADDED - WIDTH), F32)]
    x_ref[COLS:] = jnp.concatenate(rest, axis=1).T.astype(BF16)
    rows = pl.ds(pl.multiple_of(x * SHARE, 16), SHARE)
    for which, w_ref in ((0, w_key), (1, w_value)):

        @pl.when(core == which)
        def _():
            for g in range(N_Y):
                w_mine[g] = w_ref[rows, g * HEAD : (g + 1) * HEAD]

    loads["table_row"].wait()
    loads["source_row"].wait()
    pl.semaphore_wait(barrier, len(partners))

    def block(step_y, step_z):
        return lax.rem(y + step_y, N_Y) * N_ZL + lax.rem(zl + step_z, N_ZL)

    def mine(step):
        return block(0, N_ZL - step)

    def near(k, way):
        return block(N_Y - 1 if way == 0 else 1, N_ZL - k if k else 0)

    piece[mp] = x_ref[:WIDTH]
    tokens = x_ref.at[pl.ds(0, WIDTH)]
    for k in (1, 2, 3):
        start(tokens, piece.at[mp], tz_s.at[k], tz_r.at[k], at_zl(k))
    for way, step in ((0, 1), (1, N_Y - 1)):
        start(tokens, piece.at[mp], ty_s.at[0, way], ty_r.at[0, way], at_y(step))

    w_kv[core, mp, rows] = w_mine[y]
    for step in range(1, N_MP):
        dest = at_mp(step)
        start(w_mine.at[dest[1] // N_ZL], w_kv.at[core, mp, rows], w1_s, w1_r, dest)

    for k in (1, 2, 3):
        start(table_row, tables.at[k], ts_s.at[k, 0], ts_r.at[k, 0], at_zh(N_ZH - k))
        start(source_row, sources.at[k], ts_s.at[k, 1], ts_r.at[k, 1], at_zh(N_ZH - k))

    def line_send(buf, send, recv):
        for way, step in ((0, 1), (1, N_ZH - 1)):
            start(
                buf[0].at[pl.ds(0, SEQS)],
                buf[N_ZH - 1 if way == 0 else 1].at[pl.ds(0, SEQS)],
                send.at[way],
                recv.at[way],
                at_zh(step),
            )

    def line_pass(buf, send, recv, send_on, recv_on):
        for way, step in ((0, 1), (1, N_ZH - 1)):
            k = N_ZH - 1 if way == 0 else 1
            spot = buf[k].at[pl.ds(0, SEQS)]
            copy(spot, spot, send.at[way], recv.at[way], at_zh(step)).wait_recv()
            some = pl.ds(way * (SEQS // 2), SEQS // 2)
            start(
                buf[k].at[some],
                buf[2].at[some],
                send_on.at[way],
                recv_on.at[way],
                at_zh(step),
            )

    def line_end(buf, send_on, recv_on):
        for way in (0, 1):
            spot = buf[2].at[pl.ds(way * (SEQS // 2), SEQS // 2)]
            copy(spot, spot, send_on.at[way], recv_on.at[way], at_zh(1)).wait_recv()

    def deal(buf, k, pick, out, into, send, recv):
        for i, (step, flip) in enumerate(PAIRS):
            to = pair(step, flip)
            out[i, k] = buf[k][pick(k, to)]
            start(out.at[i, k], into.at[i, k], send, recv, (to, mp))
        into[len(PAIRS), k] = buf[k][pick(k, dp)]

    def dealt(into, send, recv):
        spot = into.at[pl.ds(0, len(PAIRS))]
        copy(spot, spot, send, recv, sibling).wait_recv()

    for name in ("drawn", "weight", "cotangent", "table", "source"):
        loads[name].wait()
    for s in range(SEQS):
        factor = drawn[s].astype(F32) * weight[s] * (1.0 / LENGTH)
        d_all[0][s] = (cotangent[s].astype(F32) * factor).astype(BF16)
    for k in range(N_ZH):
        d_all[k][SEQS] = jnp.zeros((LENGTH, COLS), BF16)

    def slot_of(k, rank):
        found = jnp.int32(SEQS)
        for s in range(SEQS):
            have = source[s] if k == 0 else near_sources[k, s]
            found = jnp.where(have == rank, jnp.int32(s), found)
        return found

    deal(d_all, 0, slot_of, d_send, d_slots, c2_s, c2_r)

    acc_q[...] = jnp.zeros_like(acc_q)

    def project(j):
        place = pl.ds(pl.multiple_of(j * WIDTH, WIDTH), WIDTH)
        acc_q[...] += dot_tn(w_query[place], piece[j])

    def wait_near(k, way):
        spot = piece.at[near(k, way)]
        copy(spot, spot, ty_s.at[k, way], ty_r.at[k, way], at_y(1)).wait_recv()

    def pass_on(k):
        for way, step in ((0, 1), (1, N_Y - 1)):
            wait_near(k, way)
            half = piece.at[near(k, way), pl.ds(way * HALF, HALF)]
            start(half, half, tf_s.at[k, way], tf_r.at[k, way], at_y(step))

    def take(k):
        spot = piece.at[mine(k)]
        copy(spot, spot, tz_s.at[k], tz_r.at[k], at_zl(1)).wait_recv()
        for way, step in ((0, 1), (1, N_Y - 1)):
            start(spot, spot, ty_s.at[k, way], ty_r.at[k, way], at_y(step))

    loads["w_query"].wait()
    def w_rows(step):
        at = lax.rem(x + step, N_X) * SHARE
        return w_kv.at[core, :, pl.ds(pl.multiple_of(at, 16), SHARE)]

    def w_across(step):
        spot = w_rows(step)
        start(spot, spot, w3_s.at[step], w3_r.at[step], sibling)

    def w_arrived(step):
        spot = w_rows(N_X - step)
        copy(spot, spot, w2_s.at[step], w2_r.at[step], at_x(step)).wait_recv()
        w_across(N_X - step)

    project(mp)
    take(1)
    project(mine(1))
    got = w_kv.at[0, pl.ds(0, N_MP - 1), pl.ds(0, SHARE)]
    copy(got, got, w1_s, w1_r, at_mp(1)).wait_recv()
    for k in (1, 3, 2):
        start(w_rows(0), w_rows(0), w2_s.at[k], w2_r.at[k], at_x(k))
    w_across(0)
    pass_on(0)
    take(2)
    project(mine(2))
    take(3)
    line_send(d_all, c1_s, c1_r)
    project(mine(3))
    for way in (0, 1):
        project(near(0, way))
    pass_on(1)
    w_arrived(1)
    w_arrived(3)
    pass_on(2)
    w_arrived(2)
    pass_on(3)
    for k in (1, 2, 3):
        for way in (0, 1):
            project(near(k, way))
    for k in (1, 2, 3):
        for i, row, rows in ((0, table_row, tables), (1, source_row, sources)):
            copy(
                row, rows.at[k], ts_s.at[k, i], ts_r.at[k, i], at_zh(k)
            ).wait_recv()
    fetch = pltpu.make_async_copy(tables, near_tables, load_s.at[13])
    fetch.start()
    fetch.wait()
    fetch = pltpu.make_async_copy(sources, near_sources, load_s.at[14])
    fetch.start()
    fetch.wait()
    line_pass(d_all, c1_s, c1_r, cf_s, cf_r)
    for k in (1, 3):
        deal(d_all, k, slot_of, d_send, d_slots, c2_s, c2_r)
    for k in range(N_ZL):
        far = block(2, N_ZL - k if k else 0)
        for way in (0, 1):
            half = piece.at[far, pl.ds(way * HALF, HALF)]
            copy(half, half, tf_s.at[k, way], tf_r.at[k, way], at_y(1)).wait_recv()
        project(far)
    for k in range(N_X):
        at = lax.rem(x + k, N_X) * SHARE
        spot = w_kv.at[other, :, pl.ds(pl.multiple_of(at, 16), SHARE)]
        copy(spot, spot, w3_s.at[k], w3_r.at[k], sibling).wait_recv()
    gathered = piece[...].reshape(N_MP * WIDTH, TOKENS)
    for half in (0, 1):
        w_half = w_kv[half].reshape(N_MP * WIDTH, HEAD)
        acc_kv[half] = dot_tn(w_half, gathered)

    loads["q_gain"].wait()
    loads["k_gain"].wait()
    gain_q, gain_k = (
        jnp.broadcast_to(gain[...], (HEAD, HEAD)).T[:, :1] for gain in (q_gain, k_gain)
    )
    key_sum = acc_kv[0]
    k_inverse = lax.rsqrt(jnp.mean(key_sum * key_sum, axis=0, keepdims=True) + EPS)
    k_norm = (key_sum * k_inverse * gain_k).astype(BF16)
    value = acc_kv[1].astype(BF16)
    at_key = lax.broadcasted_iota(jnp.int32, (TOKENS, TOKENS), 0)
    at_query = lax.broadcasted_iota(jnp.int32, (TOKENS, TOKENS), 1)
    seen = ((at_key >> 5) == (at_query >> 5)) & (at_key <= at_query)
    saved = []
    for h in range(COLS // HEAD):
        query = acc_q[h * HEAD : (h + 1) * HEAD]
        inverse = lax.rsqrt(jnp.mean(query * query, axis=0, keepdims=True) + EPS)
        q_norm = (query * inverse * gain_q).astype(BF16)
        scores = jnp.where(seen, dot_tn(k_norm, q_norm) * SCALE, -1e30)
        raised = jnp.exp(scores - jnp.max(scores, axis=0, keepdims=True))
        probs = raised / jnp.sum(raised, axis=0, keepdims=True)
        p_half = probs.astype(BF16)
        out = dot_nn(value, p_half).T.astype(BF16)
        att_all[0][:, :, h * HEAD : (h + 1) * HEAD] = out.reshape(SEQS, LENGTH, HEAD)
        saved.append((query, inverse, q_norm, probs, p_half))
    def sent_to(k, rank):
        have = table[0, rank] if k == 0 else near_tables[k, 0, rank]
        return jnp.maximum(have, 0)

    line_send(att_all, a1_s, a1_r)
    deal(att_all, 0, sent_to, att_send, att_slots, a2_s, a2_r)

    line_end(d_all, cf_s, cf_r)
    deal(d_all, 2, slot_of, d_send, d_slots, c2_s, c2_r)
    dealt(d_slots, c2_s, c2_r)
    lane = lax.broadcasted_iota(jnp.int32, (1, N_DP * LENGTH), 1)
    target = jnp.zeros_like(lane)

    def sender(step, flip, k):
        of_x = lax.rem(x + N_X - step, N_X)
        of_core = other if flip else core
        return of_x * (N_ZH * N_CORE) + lax.rem(zh + k, N_ZH) * N_CORE + of_core

    for i, (step, flip) in enumerate(PAIRS + ((0, 0),)):
        for k in range(N_ZH):
            entry = table[0, sender(step, flip, k)]
            here = (lane >> 5) == i * N_ZH + k
            target = jnp.where(here, entry * LENGTH, target)
    target = jnp.where(target < 0, -1, target + (lane & (LENGTH - 1)))
    place = lax.broadcasted_iota(jnp.int32, (TOKENS, N_DP * LENGTH), 0)
    chosen = jnp.where(place == target, 1.0, 0.0).astype(BF16)
    d_rows = dot_nn(chosen, d_slots[...].reshape(N_DP * LENGTH, COLS))
    d_cols = d_rows.T.astype(BF16)
    d_knorm = jnp.zeros((HEAD, TOKENS), F32)
    d_value = jnp.zeros((HEAD, TOKENS), F32)
    d_queries = []
    for h in range(COLS // HEAD):
        query, inverse, q_norm, probs, p_half = saved[h]
        out_half = d_cols[h * HEAD : (h + 1) * HEAD]
        d_probs = dot_tn(value, out_half)
        d_value += dot_nt(out_half, p_half)
        centred = d_probs - jnp.sum(d_probs * probs, axis=0, keepdims=True)
        score_half = (probs * centred * SCALE).astype(BF16)
        d_qnorm = dot_nn(k_norm, score_half)
        d_knorm += dot_nt(q_norm, score_half)
        d_queries.append(rms_back(query, inverse, gain_q, d_qnorm))
    for h in range(COLS // HEAD):
        d_query[:, h * HEAD : (h + 1) * HEAD] = d_queries[h].T.astype(BF16)
    d_key = rms_back(key_sum, k_inverse, gain_k, d_knorm).astype(BF16)
    d_value = d_value.astype(BF16)
    for q in (0, 1):
        dkv[q] = d_key[q * 64 : (q + 1) * 64]
        dkv[2 + q] = d_value[q * 64 : (q + 1) * 64]

    for k in (1, 2, 3):
        start(
            dkv.at[lax.rem(zl + k, N_ZL)],
            dkv_recv.at[k],
            k1_s.at[k],
            k1_r.at[k],
            at_zl(k),
        )

    def partial_rows(to, into, which):
        rows = pl.ds(pl.multiple_of(which * HALF, 16), HALF)
        found = piece[pl.ds(to * N_ZH, N_ZH), rows].reshape(N_ZH * HALF, TOKENS)
        total = dot_nn(found, d_query[...]).astype(BF16)
        into[to] = total.reshape(N_ZH, HALF, COLS)

    def x_at(step):
        return lax.rem(x + step, N_X)

    order = (2, 1, 3, 0)
    for k in order:
        to = x_at(k)
        partial_rows(to, g_send, other)
        start(g_send.at[to], g_recv.at[to], gc_s.at[k], gc_r.at[k], sibling)
    for k in order:
        partial_rows(x_at(k), g_keep, core)

    for k in (1, 2, 3):
        copy(
            dkv.at[0], dkv_recv.at[k], k1_s.at[k], k1_r.at[k], at_zl(k)
        ).wait_recv()
    total = dkv[zl].astype(F32)
    for k in (1, 2, 3):
        total += dkv_recv[k].astype(F32)
    dkv_all[y, zl] = total.astype(BF16)
    spot = dkv_all.at[y, zl]
    for k in (1, 2, 3):
        start(spot, spot, k2_s.at[k], k2_r.at[k], at_zl(k))

    for k in order:
        to = x_at(k)
        copy(
            g_send.at[to], g_recv.at[to], gc_s.at[k], gc_r.at[k], sibling
        ).wait_recv()
        both = g_keep[to].astype(F32) + g_recv[to].astype(F32)
        g_keep[to] = both.astype(BF16)
        if k:
            for kz in order:
                to_z = lax.rem(zh + kz, N_ZH)
                start(
                    g_keep.at[to, to_z],
                    x_recv.at[k, to_z],
                    gx_s.at[k, kz],
                    gx_r.at[k, kz],
                    at_x(k),
                )

    line_pass(att_all, a1_s, a1_r, af_s, af_r)
    for k in (1, 3):
        deal(att_all, k, sent_to, att_send, att_slots, a2_s, a2_r)

    for k in (1, 2, 3):
        copy(spot, spot, k2_s.at[k], k2_r.at[k], at_zl(k)).wait_recv()
    group = dkv_all.at[y]
    for k in (1, 2, 3):
        start(group, group, k3_s.at[k], k3_r.at[k], at_y(k))
    for k in (1, 2, 3):
        copy(group, group, k3_s.at[k], k3_r.at[k], at_y(k)).wait_recv()

    for g in range(N_X):
        rows = dkv_all[g].reshape(2 * HEAD, TOKENS)
        product = dot_nt(rows, x_ref[...]).astype(BF16)
        for half in range(2):
            for i in range(N_ZH):
                for c in range(N_CORE):
                    first = half * HEAD + i * 32 + c * 16
                    kv_part[c, g, i, half] = product[first : first + 16]
    start(kv_part.at[other], kv_recv, vc_s, vc_r, sibling)

    for kz in order:
        to_z = lax.rem(zh + kz, N_ZH)
        total = g_keep[x, to_z].astype(F32)
        for k in (1, 2, 3):
            spot = x_recv.at[k, to_z]
            copy(spot, spot, gx_s.at[k, kz], gx_r.at[k, kz], at_x(k)).wait_recv()
            total += x_recv[k, to_z].astype(F32)
        z_send[to_z] = total.astype(BF16)
        if kz:
            start(
                z_send.at[to_z], z_recv.at[kz], gz_s.at[kz], gz_r.at[kz], at_zh(kz)
            )

    line_end(att_all, af_s, af_r)
    deal(att_all, 2, sent_to, att_send, att_slots, a2_s, a2_r)
    copy(kv_part.at[other], kv_recv, vc_s, vc_r, sibling).wait_recv()
    kv_sum[...] = (kv_part[core].astype(F32) + kv_recv[...].astype(F32)).astype(BF16)
    for k in (1, 2, 3):
        start(kv_sum.at[x_at(k)], kv_x.at[k], vx_s.at[k], vx_r.at[k], at_x(k))
    total = kv_sum[x].astype(F32)
    for k in (1, 2, 3):
        copy(kv_sum.at[0], kv_x.at[k], vx_s.at[k], vx_r.at[k], at_x(k)).wait_recv()
        total += kv_x[k].astype(F32)
    kv_zs[...] = total.astype(BF16)
    for k in (1, 2, 3):
        to_z = lax.rem(zh + k, N_ZH)
        start(kv_zs.at[to_z], kv_z.at[k], vz_s.at[k], vz_r.at[k], at_zh(k))

    total = z_send[zh].astype(F32)
    for k in (1, 2, 3):
        copy(z_send.at[0], z_recv.at[k], gz_s.at[k], gz_r.at[k], at_zh(k)).wait_recv()
        total += z_recv[k].astype(F32)
    gq_out[...] = total

    total = kv_zs[zh].astype(F32)
    for k in (1, 2, 3):
        copy(kv_zs.at[0], kv_z.at[k], vz_s.at[k], vz_r.at[k], at_zh(k)).wait_recv()
        total += kv_z[k].astype(F32)
    gk_out[...] = total[0][:, :WIDTH]
    gv_out[...] = total[1][:, :WIDTH]

    dealt(att_slots, a2_s, a2_r)
    for s in range(SEQS):
        rank = source[s]
        step = lax.rem(x + N_X - rank // (N_ZH * N_CORE), N_X)
        flip = lax.rem(rank + core, N_CORE)
        k = lax.rem((rank // N_CORE) % N_ZH + N_ZH - zh, N_ZH)
        place = lax.rem(step * N_CORE + flip + len(PAIRS), len(PAIRS) + 1)
        att_out[s] = att_slots[place, k]
    for made in sends:
        made.wait_send()


def local(
    pool,
    send_table,
    slot_source,
    multiplicity,
    slot_weight,
    cotangent,
    w_query,
    w_key,
    w_value,
    query_gain,
    key_gain,
):
    dma = pltpu.SemaphoreType.DMA
    vmem = pl.BlockSpec(memory_space=pltpu.VMEM)
    attended, grad_query, grad_key, grad_value = pl.pallas_call(
        kernel,
        out_shape=(
            jax.ShapeDtypeStruct((SEQS, LENGTH, COLS), BF16),
            jax.ShapeDtypeStruct((HALF, COLS), F32),
            jax.ShapeDtypeStruct((16, WIDTH), F32),
            jax.ShapeDtypeStruct((16, WIDTH), F32),
        ),
        in_specs=[pl.BlockSpec(memory_space=pl.ANY)] * 11,
        out_specs=(vmem,) * 4,
        scratch_shapes=[
            pltpu.SMEM((1, N_DP), jnp.int32),
            pltpu.SMEM((SEQS,), jnp.int32),
            pltpu.SMEM((SEQS,), jnp.int32),
            pltpu.SMEM((SEQS,), F32),
            pltpu.VMEM((SEQS, LENGTH, WIDTH), BF16),
            pltpu.VMEM((SEQS, LENGTH, COLS), BF16),
            pltpu.VMEM((N_MP * WIDTH, COLS), BF16),
            pltpu.VMEM((WIDTH, N_Y * HEAD), BF16),
            pltpu.VMEM((WIDTH, N_Y * HEAD), BF16),
            pltpu.VMEM((1, HEAD), F32),
            pltpu.VMEM((1, HEAD), F32),
            dma((15,)),
            pltpu.VMEM((1, N_DP), jnp.int32),
            pltpu.VMEM((SEQS,), jnp.int32),
            pltpu.VMEM((N_ZH, 1, N_DP), jnp.int32),
            pltpu.VMEM((N_ZH, SEQS), jnp.int32),
            pltpu.SMEM((N_ZH, 1, N_DP), jnp.int32),
            pltpu.SMEM((N_ZH, SEQS), jnp.int32),
            dma((4, 2)),
            dma((4, 2)),
            pltpu.VMEM((PADDED, TOKENS), BF16),
            pltpu.VMEM((N_Y, SHARE, HEAD), BF16),
            pltpu.VMEM((N_MP, WIDTH, TOKENS), BF16),
            pltpu.VMEM((2, N_MP, WIDTH, HEAD), BF16),
            *[pltpu.VMEM((SEQS + 1, LENGTH, COLS), BF16)] * N_ZH,
            pltpu.VMEM((len(PAIRS), N_ZH, LENGTH, COLS), BF16),
            pltpu.VMEM((len(PAIRS) + 1, N_ZH, LENGTH, COLS), BF16),
            pltpu.VMEM((COLS, TOKENS), F32),
            pltpu.VMEM((2, HEAD, TOKENS), F32),
            *[pltpu.VMEM((SEQS, LENGTH, COLS), BF16)] * N_ZH,
            pltpu.VMEM((len(PAIRS), N_ZH, LENGTH, COLS), BF16),
            pltpu.VMEM((len(PAIRS) + 1, N_ZH, LENGTH, COLS), BF16),
            pltpu.VMEM((TOKENS, COLS), BF16),
            pltpu.VMEM((N_X, N_ZH, HALF, COLS), BF16),
            pltpu.VMEM((N_X, N_ZH, HALF, COLS), BF16),
            pltpu.VMEM((N_X, N_ZH, HALF, COLS), BF16),
            pltpu.VMEM((N_X, N_ZH, HALF, COLS), BF16),
            pltpu.VMEM((N_ZH, HALF, COLS), BF16),
            pltpu.VMEM((N_ZH, HALF, COLS), BF16),
            pltpu.VMEM((N_ZL, 64, TOKENS), BF16),
            pltpu.VMEM((N_ZL, 64, TOKENS), BF16),
            pltpu.VMEM((N_Y, N_ZL, 64, TOKENS), BF16),
            pltpu.VMEM((N_CORE, N_X, N_ZH, 2, 16, PADDED), BF16),
            pltpu.VMEM((N_X, N_ZH, 2, 16, PADDED), BF16),
            pltpu.VMEM((N_X, N_ZH, 2, 16, PADDED), BF16),
            pltpu.VMEM((N_X, N_ZH, 2, 16, PADDED), BF16),
            pltpu.VMEM((N_ZH, 2, 16, PADDED), BF16),
            pltpu.VMEM((N_ZH, 2, 16, PADDED), BF16),
            dma((4,)),
            dma((4,)),
            dma((4, 2)),
            dma((4, 2)),
            dma((4, 2)),
            dma((4, 2)),
            dma,
            dma,
            dma((4,)),
            dma((4,)),
            dma((4,)),
            dma((4,)),
            dma((2,)),
            dma((2,)),
            dma((2,)),
            dma((2,)),
            dma,
            dma,
            dma((2,)),
            dma((2,)),
            dma((2,)),
            dma((2,)),
            dma,
            dma,
            dma((4,)),
            dma((4,)),
            dma((4,)),
            dma((4,)),
            dma((4,)),
            dma((4,)),
            dma((4,)),
            dma((4,)),
            dma((4, 4)),
            dma((4, 4)),
            dma((4,)),
            dma((4,)),
            dma,
            dma,
            dma((4,)),
            dma((4,)),
            dma((4,)),
            dma((4,)),
        ],
        compiler_params=pltpu.CompilerParams(
            collective_id=0, has_side_effects=True, vmem_limit_bytes=60 * 1024 * 1024
        ),
        name="train_step",
    )(
        send_table,
        slot_source,
        multiplicity,
        slot_weight,
        pool,
        cotangent,
        w_query,
        w_key,
        w_value,
        query_gain.reshape(1, HEAD),
        key_gain.reshape(1, HEAD),
    )
    return attended, grad_query, grad_key.T, grad_value.T


def solution(mesh):
    return jax.shard_map(
        local,
        mesh=mesh,
        in_specs=(
            P("dp", None, "mp"),
            P("dp", None),
            P("dp"),
            P("dp"),
            P("dp"),
            P("dp", None, "mp"),
            P(None, "mp"),
            P("mp", None),
            P("mp", None),
            P(),
            P(),
        ),
        out_specs=(P("dp", None, "mp"), P("dp", "mp"), P("mp", "dp"), P("mp", "dp")),
        check_vma=False,
    )
```

```python
import functools
import math

import jax
import jax.numpy as jnp
from jax import lax
from jax.experimental import pallas as pl
from jax.experimental.pallas import tpu as pltpu
from jax.sharding import PartitionSpec as P

F32, BF16 = jnp.float32, jnp.bfloat16
MESH = pl.DeviceIdType.MESH

N_X, N_ZH, N_CORE, N_Y, N_ZL = 4, 4, 2, 4, 4
N_DP, N_MP = N_X * N_ZH * N_CORE, N_Y * N_ZL
SEQS, LENGTH, WIDTH = 8, 32, 320
TOKENS = SEQS * LENGTH
HEAD, COLS = 128, 256
PADDED = 384
SHARE = WIDTH // N_X
HALF = WIDTH // 2
EPS = 1e-6
PAIRS = ((0, 1), (1, 0), (1, 1), (2, 0), (2, 1), (3, 0), (3, 1))
SCALE = 1.0 / math.sqrt(HEAD)


def dot_nn(a, b):
    return lax.dot_general(a, b, (((1,), (0,)), ((), ())), preferred_element_type=F32)


def dot_tn(a, b):
    return lax.dot_general(a, b, (((0,), (0,)), ((), ())), preferred_element_type=F32)


def dot_nt(a, b):
    return lax.dot_general(a, b, (((1,), (1,)), ((), ())), preferred_element_type=F32)


def rms_back(values, inverse, gain, grad_out):
    scaled = grad_out * gain
    inner = jnp.mean(values * scaled, axis=0, keepdims=True)
    return inverse * scaled - values * (inverse * inverse * inverse) * inner


def kernel(
    table_in,
    source_in,
    drawn_in,
    weight_in,
    pool_in,
    cotangent_in,
    w_query_in,
    w_key_in,
    w_value_in,
    q_gain_in,
    k_gain_in,
    att_out,
    gq_out,
    gk_out,
    gv_out,
    table,
    source,
    drawn,
    weight,
    pool,
    cotangent,
    w_query,
    w_key,
    w_value,
    q_gain,
    k_gain,
    load_s,
    table_row,
    source_row,
    tables,
    sources,
    near_tables,
    near_sources,
    ts_s,
    ts_r,
    x_ref,
    w_mine,
    piece,
    w_kv,
    d_all_0,
    d_all_1,
    d_all_2,
    d_all_3,
    d_send,
    d_slots,
    acc_q,
    acc_kv,
    att_all_0,
    att_all_1,
    att_all_2,
    att_all_3,
    att_send,
    att_slots,
    d_query,
    g_send,
    g_recv,
    g_keep,
    x_recv,
    z_send,
    z_recv,
    dkv,
    dkv_recv,
    dkv_all,
    kv_part,
    kv_recv,
    kv_sum,
    kv_x,
    kv_zs,
    kv_z,
    tz_s,
    tz_r,
    ty_s,
    ty_r,
    tf_s,
    tf_r,
    w1_s,
    w1_r,
    w2_s,
    w2_r,
    w3_s,
    w3_r,
    c1_s,
    c1_r,
    cf_s,
    cf_r,
    c2_s,
    c2_r,
    a1_s,
    a1_r,
    af_s,
    af_r,
    a2_s,
    a2_r,
    k1_s,
    k1_r,
    k2_s,
    k2_r,
    k3_s,
    k3_r,
    gc_s,
    gc_r,
    gx_s,
    gx_r,
    gz_s,
    gz_r,
    vc_s,
    vc_r,
    vx_s,
    vx_r,
    vz_s,
    vz_r,
):
    dp, mp = lax.axis_index("dp"), lax.axis_index("mp")
    x, zh, core = dp // (N_ZH * N_CORE), (dp // N_CORE) % N_ZH, dp % N_CORE
    y, zl = mp // N_ZL, mp % N_ZL
    other = 1 - core

    def pair(step, flip):
        return lax.rem(x + step, N_X) * (N_ZH * N_CORE) + zh * N_CORE + (
            other if flip else core
        )

    def at_mp(step):
        return dp, lax.rem(mp + step, N_MP)

    def at_x(step):
        return lax.rem(dp + step * (N_ZH * N_CORE), N_DP), mp

    def at_zh(step):
        return x * (N_ZH * N_CORE) + lax.rem(zh + step, N_ZH) * N_CORE + core, mp

    def at_y(step):
        return dp, lax.rem(mp + step * N_ZL, N_MP)

    def at_zl(step):
        return dp, y * N_ZL + lax.rem(zl + step, N_ZL)

    sibling = (dp + 1 - 2 * core, mp)
    d_all = (d_all_0, d_all_1, d_all_2, d_all_3)
    att_all = (att_all_0, att_all_1, att_all_2, att_all_3)

    def copy(src, dst, send, recv, device):
        return pltpu.make_async_remote_copy(
            src_ref=src,
            dst_ref=dst,
            send_sem=send,
            recv_sem=recv,
            device_id=device,
            device_id_type=MESH,
        )

    sends = []

    def start(*args):
        made = copy(*args)
        made.start()
        sends.append(made)

    barrier = pltpu.get_barrier_semaphore()
    partners = [at_mp(step) for step in range(1, N_MP)]
    partners += [at_zh(step) for step in range(1, N_ZH)]
    partners += [(pair(step, flip), mp) for step, flip in PAIRS]
    for device in partners:
        pl.semaphore_signal(barrier, inc=1, device_id=device, device_id_type=MESH)

    loads = {}
    for i, (name, src, dst) in enumerate(
        (
            ("pool", pool_in, pool),
            ("w_key", w_key_in, w_key),
            ("w_value", w_value_in, w_value),
            ("table_row", table_in, table_row),
            ("source_row", source_in, source_row),
            ("table", table_in, table),
            ("source", source_in, source),
            ("drawn", drawn_in, drawn),
            ("weight", weight_in, weight),
            ("cotangent", cotangent_in, cotangent),
            ("w_query", w_query_in, w_query),
            ("q_gain", q_gain_in, q_gain),
            ("k_gain", k_gain_in, k_gain),
        )
    ):
        loads[name] = pltpu.make_async_copy(src, dst, load_s.at[i])
        loads[name].start()

    for name in ("pool", "w_key", "w_value"):
        loads[name].wait()
    rows = pool[...].reshape(TOKENS, WIDTH).astype(F32)
    x_ref[:COLS] = rows[:, :COLS].T.astype(BF16)
    rest = [rows[:, COLS:], jnp.zeros((TOKENS, PADDED - WIDTH), F32)]
    x_ref[COLS:] = jnp.concatenate(rest, axis=1).T.astype(BF16)
    rows = pl.ds(pl.multiple_of(x * SHARE, 16), SHARE)
    for which, w_ref in ((0, w_key), (1, w_value)):

        @pl.when(core == which)
        def _():
            for g in range(N_Y):
                w_mine[g] = w_ref[rows, g * HEAD : (g + 1) * HEAD]

    loads["table_row"].wait()
    loads["source_row"].wait()
    pl.semaphore_wait(barrier, len(partners))

    fellow = zl + 1 - 2 * (zl % 2)
    across = N_ZL - 1 - zl
    inner = (zl == 1) | (zl == 2)
    line_of = (
        zl,
        fellow,
        jnp.where(zl < 2, jnp.int32(2), jnp.int32(1)),
        jnp.where(zl < 2, jnp.int32(3), jnp.int32(0)),
    )

    def mine(k):
        return y * N_ZL + line_of[k]

    def near(k, way):
        return lax.rem(y + (N_Y - 1 if way == 0 else 1), N_Y) * N_ZL + line_of[k]

    inner_sends = []

    def start_inner(*args):
        inner_sends.append(args)

        @pl.when(inner)
        def _():
            copy(*args).start()

    def along_y(k):
        spot = piece.at[mine(k)]
        for way, step in ((0, 1), (1, N_Y - 1)):
            start(spot, spot, ty_s.at[k, way], ty_r.at[k, way], at_y(step))

    piece[mp] = x_ref[:WIDTH]
    w_kv[core, mp, rows] = w_mine[y]
    for step in range(1, N_MP):
        dest = at_mp(step)
        start(w_mine.at[dest[1] // N_ZL], w_kv.at[core, mp, rows], w1_s, w1_r, dest)
    tokens = piece.at[mp]
    start(tokens, tokens, tz_s.at[0], tz_r.at[1], (dp, y * N_ZL + fellow))
    start_inner(tokens, tokens, tz_s.at[1], tz_r.at[2], (dp, y * N_ZL + across))
    along_y(0)

    for k in (1, 2, 3):
        start(table_row, tables.at[k], ts_s.at[k, 0], ts_r.at[k, 0], at_zh(N_ZH - k))
        start(source_row, sources.at[k], ts_s.at[k, 1], ts_r.at[k, 1], at_zh(N_ZH - k))

    half_slots = SEQS // 2

    def line_send(buf, send, recv):
        for part in (0, 1):
            for way, step in ((0, 1), (1, N_ZH - 1)):
                some = pl.ds((way ^ part) * half_slots, half_slots)
                start(
                    buf[0].at[some],
                    buf[N_ZH - 1 if way == 0 else 1].at[some],
                    send.at[way, part],
                    recv.at[way, part],
                    at_zh(step),
                )

    def line_pass(buf, send, recv, send_on, recv_on):
        for part in (0, 1):
            for way, step in ((0, 1), (1, N_ZH - 1)):
                some = pl.ds((way ^ part) * half_slots, half_slots)
                spot = buf[N_ZH - 1 if way == 0 else 1].at[some]
                copy(
                    spot, spot, send.at[way, part], recv.at[way, part], at_zh(step)
                ).wait_recv()
                if part == 0:
                    start(
                        spot,
                        buf[2].at[some],
                        send_on.at[way],
                        recv_on.at[way],
                        at_zh(step),
                    )

    def line_end(buf, send_on, recv_on):
        for way in (0, 1):
            spot = buf[2].at[pl.ds(way * (SEQS // 2), SEQS // 2)]
            copy(spot, spot, send_on.at[way], recv_on.at[way], at_zh(1)).wait_recv()

    def deal(buf, k, pick, out, into, send, recv):
        for i, (step, flip) in enumerate(PAIRS):
            to = pair(step, flip)
            out[i, k] = buf[k][pick(k, to)]
            start(out.at[i, k], into.at[i, k], send, recv, (to, mp))
        into[len(PAIRS), k] = buf[k][pick(k, dp)]

    def dealt(into, send, recv):
        spot = into.at[pl.ds(0, len(PAIRS))]
        copy(spot, spot, send, recv, sibling).wait_recv()

    for name in ("drawn", "weight", "cotangent", "table", "source"):
        loads[name].wait()
    for s in range(SEQS):
        factor = drawn[s].astype(F32) * weight[s] * (1.0 / LENGTH)
        d_all[0][s] = (cotangent[s].astype(F32) * factor).astype(BF16)
    for k in range(N_ZH):
        d_all[k][SEQS] = jnp.zeros((LENGTH, COLS), BF16)

    def slot_of(k, rank):
        found = jnp.int32(SEQS)
        for s in range(SEQS):
            have = source[s] if k == 0 else near_sources[k, s]
            found = jnp.where(have == rank, jnp.int32(s), found)
        return found

    deal(d_all, 0, slot_of, d_send, d_slots, c2_s, c2_r)

    acc_q[...] = jnp.zeros_like(acc_q)

    def project(j):
        place = pl.ds(pl.multiple_of(j * WIDTH, WIDTH), WIDTH)
        acc_q[...] += dot_tn(w_query[place], piece[j])

    def wait_near(k, way):
        spot = piece.at[near(k, way)]
        copy(spot, spot, ty_s.at[k, way], ty_r.at[k, way], at_y(1)).wait_recv()

    def pass_on(k):
        for way, step in ((0, 1), (1, N_Y - 1)):
            wait_near(k, way)
            half = piece.at[near(k, way), pl.ds(way * HALF, HALF)]
            start(half, half, tf_s.at[k, way], tf_r.at[k, way], at_y(step))

    def take(k):
        spot = piece.at[mine(k)]
        copy(spot, spot, tz_s.at[k], tz_r.at[k], at_y(1)).wait_recv()
        to = across if k == 1 else fellow
        start_inner(
            spot, spot, tz_s.at[k + 1], tz_r.at[3 if k == 1 else k], (dp, y * N_ZL + to)
        )
        along_y(k)

    def w_rows(step):
        at = lax.rem(x + step, N_X) * SHARE
        return w_kv.at[core, :, pl.ds(pl.multiple_of(at, 16), SHARE)]

    def w_across(step):
        spot = w_rows(step)
        start(spot, spot, w3_s.at[step], w3_r.at[step], sibling)

    def w_arrived(step):
        spot = w_rows(N_X - step)
        copy(spot, spot, w2_s.at[step], w2_r.at[step], at_x(step)).wait_recv()
        w_across(N_X - step)

    def far_arrived(k):
        far = lax.rem(y + 2, N_Y) * N_ZL + line_of[k]
        for way in (0, 1):
            half = piece.at[far, pl.ds(way * HALF, HALF)]
            copy(half, half, tf_s.at[k, way], tf_r.at[k, way], at_y(1)).wait_recv()
        project(far)

    loads["w_query"].wait()
    project(mp)
    take(1)
    pass_on(0)
    got = w_kv.at[0, pl.ds(0, N_MP - 1), pl.ds(0, SHARE)]
    copy(got, got, w1_s, w1_r, at_mp(1)).wait_recv()
    for k in (1, 3, 2):
        start(w_rows(0), w_rows(0), w2_s.at[k], w2_r.at[k], at_x(k))
    w_across(0)
    project(mine(1))
    for way in (0, 1):
        project(near(0, way))
    take(2)
    line_send(d_all, c1_s, c1_r)
    project(mine(2))
    pass_on(1)
    take(3)
    project(mine(3))
    far_arrived(0)
    pass_on(2)
    w_arrived(1)
    w_arrived(3)
    for k in (1, 2):
        for way in (0, 1):
            project(near(k, way))
    pass_on(3)
    w_arrived(2)
    for way in (0, 1):
        project(near(3, way))
    far_arrived(1)
    far_arrived(2)
    for k in (1, 2, 3):
        for i, row, rows in ((0, table_row, tables), (1, source_row, sources)):
            copy(
                row, rows.at[k], ts_s.at[k, i], ts_r.at[k, i], at_zh(k)
            ).wait_recv()
    fetches = [
        pltpu.make_async_copy(tables, near_tables, load_s.at[13]),
        pltpu.make_async_copy(sources, near_sources, load_s.at[14]),
    ]
    for fetch in fetches:
        fetch.start()
    for fetch in fetches:
        fetch.wait()
    line_pass(d_all, c1_s, c1_r, cf_s, cf_r)
    for k in (1, 3):
        deal(d_all, k, slot_of, d_send, d_slots, c2_s, c2_r)
    far_arrived(3)
    for k in range(N_X):
        at = lax.rem(x + k, N_X) * SHARE
        spot = w_kv.at[other, :, pl.ds(pl.multiple_of(at, 16), SHARE)]
        copy(spot, spot, w3_s.at[k], w3_r.at[k], sibling).wait_recv()
    gathered = piece[...].reshape(N_MP * WIDTH, TOKENS)
    for half in (0, 1):
        w_half = w_kv[half].reshape(N_MP * WIDTH, HEAD)
        acc_kv[half] = dot_tn(w_half, gathered)

    loads["q_gain"].wait()
    loads["k_gain"].wait()
    gain_q, gain_k = (
        jnp.broadcast_to(gain[...], (HEAD, HEAD)).T[:, :1] for gain in (q_gain, k_gain)
    )
    key_sum = acc_kv[0]
    k_inverse = lax.rsqrt(jnp.mean(key_sum * key_sum, axis=0, keepdims=True) + EPS)
    k_norm = (key_sum * k_inverse * gain_k).astype(BF16)
    value = acc_kv[1].astype(BF16)
    at_key = lax.broadcasted_iota(jnp.int32, (TOKENS, TOKENS), 0)
    at_query = lax.broadcasted_iota(jnp.int32, (TOKENS, TOKENS), 1)
    seen = ((at_key >> 5) == (at_query >> 5)) & (at_key <= at_query)
    saved = []
    for h in range(COLS // HEAD):
        query = acc_q[h * HEAD : (h + 1) * HEAD]
        inverse = lax.rsqrt(jnp.mean(query * query, axis=0, keepdims=True) + EPS)
        q_norm = (query * inverse * gain_q).astype(BF16)
        scores = jnp.where(seen, dot_tn(k_norm, q_norm) * SCALE, -1e30)
        raised = jnp.exp(scores - jnp.max(scores, axis=0, keepdims=True))
        probs = raised / jnp.sum(raised, axis=0, keepdims=True)
        p_half = probs.astype(BF16)
        out = dot_nn(value, p_half).T.astype(BF16)
        att_all[0][:, :, h * HEAD : (h + 1) * HEAD] = out.reshape(SEQS, LENGTH, HEAD)
        saved.append((query, inverse, q_norm, probs, p_half))
    def sent_to(k, rank):
        have = table[0, rank] if k == 0 else near_tables[k, 0, rank]
        return jnp.maximum(have, 0)

    line_send(att_all, a1_s, a1_r)
    deal(att_all, 0, sent_to, att_send, att_slots, a2_s, a2_r)

    line_end(d_all, cf_s, cf_r)
    deal(d_all, 2, slot_of, d_send, d_slots, c2_s, c2_r)
    dealt(d_slots, c2_s, c2_r)
    lane = lax.broadcasted_iota(jnp.int32, (1, N_DP * LENGTH), 1)
    target = jnp.zeros_like(lane)

    def sender(step, flip, k):
        of_x = lax.rem(x + N_X - step, N_X)
        of_core = other if flip else core
        return of_x * (N_ZH * N_CORE) + lax.rem(zh + k, N_ZH) * N_CORE + of_core

    for i, (step, flip) in enumerate(PAIRS + ((0, 0),)):
        for k in range(N_ZH):
            entry = table[0, sender(step, flip, k)]
            here = (lane >> 5) == i * N_ZH + k
            target = jnp.where(here, entry * LENGTH, target)
    target = jnp.where(target < 0, -1, target + (lane & (LENGTH - 1)))
    place = lax.broadcasted_iota(jnp.int32, (TOKENS, N_DP * LENGTH), 0)
    chosen = jnp.where(place == target, 1.0, 0.0).astype(BF16)
    d_rows = dot_nn(chosen, d_slots[...].reshape(N_DP * LENGTH, COLS))
    d_cols = d_rows.T.astype(BF16)
    d_knorm = jnp.zeros((HEAD, TOKENS), F32)
    d_value = jnp.zeros((HEAD, TOKENS), F32)
    d_queries = []
    for h in range(COLS // HEAD):
        query, inverse, q_norm, probs, p_half = saved[h]
        out_half = d_cols[h * HEAD : (h + 1) * HEAD]
        d_probs = dot_tn(value, out_half)
        d_value += dot_nt(out_half, p_half)
        centred = d_probs - jnp.sum(d_probs * probs, axis=0, keepdims=True)
        score_half = (probs * centred * SCALE).astype(BF16)
        d_qnorm = dot_nn(k_norm, score_half)
        d_knorm += dot_nt(q_norm, score_half)
        d_queries.append(rms_back(query, inverse, gain_q, d_qnorm))
    for h in range(COLS // HEAD):
        d_query[:, h * HEAD : (h + 1) * HEAD] = d_queries[h].T.astype(BF16)
    d_key = rms_back(key_sum, k_inverse, gain_k, d_knorm).astype(BF16)
    d_value = d_value.astype(BF16)
    for q in (0, 1):
        dkv[q] = d_key[q * 64 : (q + 1) * 64]
        dkv[2 + q] = d_value[q * 64 : (q + 1) * 64]

    for k in (1, 2, 3):
        start(
            dkv.at[lax.rem(zl + k, N_ZL)],
            dkv_recv.at[k],
            k1_s.at[k],
            k1_r.at[k],
            at_zl(k),
        )

    def x_at(step):
        return lax.rem(x + step, N_X)

    def zh_at(step):
        return lax.rem(zh + step, N_ZH)

    def partial_rows(to, into, which):
        rows = pl.ds(pl.multiple_of(which * HALF, 16), HALF)
        for i in range(N_X):
            total = dot_nn(piece[i * N_ZH + to, rows], d_query[...])
            into[to, i] = total.astype(BF16)

    def core_step(kz):
        to = zh_at(kz)
        copy(
            g_send.at[to], g_recv.at[to], gc_s.at[kz], gc_r.at[kz], sibling
        ).wait_recv()
        both = g_keep[to].astype(F32) + g_recv[to].astype(F32)
        g_keep[to] = both.astype(BF16)
        for k in (2, 1, 3):
            start(
                g_keep.at[to, x_at(k)],
                x_recv.at[to, k],
                gx_s.at[k, kz],
                gx_r.at[k, kz],
                at_x(k),
            )

    def x_step(kz):
        to = zh_at(kz)
        total = g_keep[to, x].astype(F32)
        for k in (1, 2, 3):
            spot = x_recv.at[to, k]
            copy(spot, spot, gx_s.at[k, kz], gx_r.at[k, kz], at_x(k)).wait_recv()
            total += x_recv[to, k].astype(F32)
        z_send[to] = total.astype(BF16)
        if kz:
            start(z_send.at[to], z_recv.at[kz], gz_s.at[kz], gz_r.at[kz], at_zh(kz))

    order = (2, 1, 3, 0)

    def kv_place(i):
        step = lax.rem(i + N_ZH - zh, N_ZH)
        return jnp.where(
            step == 0, 3, jnp.where(step == 1, 1, jnp.where(step == 2, 0, 2))
        )

    def kv_core_step(part):
        some = pl.ds(2 * part, 2)
        copy(
            kv_part.at[other, some],
            kv_recv.at[some],
            vc_s.at[part],
            vc_r.at[part],
            sibling,
        ).wait_recv()
        both = kv_part[core, some].astype(F32) + kv_recv[some].astype(F32)
        both = both.astype(BF16)
        for g in range(N_X):
            kv_sum[g, some] = both[:, g]
        for k in (2, 1, 3):
            start(
                kv_sum.at[x_at(k), some],
                kv_x.at[k, some],
                vx_s.at[k, part],
                vx_r.at[k, part],
                at_x(k),
            )

    def kv_x_step(part):
        some = pl.ds(2 * part, 2)
        total = kv_sum[x, some].astype(F32)
        for k in (1, 2, 3):
            spot = kv_x.at[k, some]
            copy(
                spot, spot, vx_s.at[k, part], vx_r.at[k, part], at_x(k)
            ).wait_recv()
            total += kv_x[k, some].astype(F32)
        kv_zs[some] = total.astype(BF16)
        for p in (0, 1):
            k = order[2 * part + p]
            if k:
                start(
                    kv_zs.at[2 * part + p],
                    kv_z.at[k],
                    vz_s.at[k],
                    vz_r.at[k],
                    at_zh(k),
                )

    for kz in order:
        to = zh_at(kz)
        partial_rows(to, g_send, other)
        start(g_send.at[to], g_recv.at[to], gc_s.at[kz], gc_r.at[kz], sibling)
    for kz in order:
        partial_rows(zh_at(kz), g_keep, core)
    for k in (1, 2, 3):
        copy(
            dkv.at[0], dkv_recv.at[k], k1_s.at[k], k1_r.at[k], at_zl(k)
        ).wait_recv()
    total = dkv[zl].astype(F32)
    for k in (1, 2, 3):
        total += dkv_recv[k].astype(F32)
    dkv_all[y, zl] = total.astype(BF16)

    def quarter(step_y, k):
        of_y = lax.rem(y + N_Y - step_y, N_Y)
        return dkv_all.at[of_y, lax.rem(zl + N_ZL - k, N_ZL)]

    def quarter_along_y(k):
        spot = quarter(0, k)
        for step in (2, 1, 3):
            start(spot, spot, k3_s.at[k, step], k3_r.at[k, step], at_y(step))

    for k in (1, 2, 3):
        spot = quarter(0, 0)
        start(spot, spot, k2_s.at[k], k2_r.at[k], at_zl(k))
    quarter_along_y(0)
    core_step(2)
    core_step(1)
    for k in (1, 2, 3):
        spot = quarter(0, k)
        copy(spot, spot, k2_s.at[k], k2_r.at[k], at_zl(k)).wait_recv()
        quarter_along_y(k)
    core_step(3)
    core_step(0)
    line_pass(att_all, a1_s, a1_r, af_s, af_r)
    for k in (1, 3):
        deal(att_all, k, sent_to, att_send, att_slots, a2_s, a2_r)
    for k in range(N_ZL):
        for step in (1, 2, 3):
            spot = quarter(step, k)
            copy(
                spot, spot, k3_s.at[k, step], k3_r.at[k, step], at_y(step)
            ).wait_recv()
    for g in range(N_X):
        rows = dkv_all[g].reshape(2 * HEAD, TOKENS)
        product = dot_nt(rows, x_ref[...]).astype(BF16)
        for half in range(2):
            for i in range(N_ZH):
                for c in range(N_CORE):
                    first = half * HEAD + i * 32 + c * 16
                    kv_part[c, kv_place(i), g, half] = product[first : first + 16]
    for part in (0, 1):
        some = pl.ds(2 * part, 2)
        start(
            kv_part.at[other, some],
            kv_recv.at[some],
            vc_s.at[part],
            vc_r.at[part],
            sibling,
        )
    x_step(2)
    kv_core_step(0)
    kv_core_step(1)
    x_step(1)
    kv_x_step(0)
    x_step(3)
    line_end(att_all, af_s, af_r)
    deal(att_all, 2, sent_to, att_send, att_slots, a2_s, a2_r)
    kv_x_step(1)
    x_step(0)
    total = z_send[zh].astype(F32)
    for k in (1, 2, 3):
        copy(z_send.at[0], z_recv.at[k], gz_s.at[k], gz_r.at[k], at_zh(k)).wait_recv()
        total += z_recv[k].astype(F32)
    gq_out[...] = total

    total = kv_zs[3].astype(F32)
    for k in (1, 2, 3):
        copy(kv_zs.at[0], kv_z.at[k], vz_s.at[k], vz_r.at[k], at_zh(k)).wait_recv()
        total += kv_z[k].astype(F32)
    gk_out[...] = total[0][:, :WIDTH]
    gv_out[...] = total[1][:, :WIDTH]

    dealt(att_slots, a2_s, a2_r)
    for s in range(SEQS):
        rank = source[s]
        step = lax.rem(x + N_X - rank // (N_ZH * N_CORE), N_X)
        flip = lax.rem(rank + core, N_CORE)
        k = lax.rem((rank // N_CORE) % N_ZH + N_ZH - zh, N_ZH)
        place = lax.rem(step * N_CORE + flip + len(PAIRS), len(PAIRS) + 1)
        att_out[s] = att_slots[place, k]
    for made in sends:
        made.wait_send()

    @pl.when(inner)
    def _():
        for args in inner_sends:
            copy(*args).wait_send()


def finish(*refs):
    for src, dst in zip(refs[:4], refs[4:]):
        dst[...] = src[...]


def local(
    pool,
    send_table,
    slot_source,
    multiplicity,
    slot_weight,
    cotangent,
    w_query,
    w_key,
    w_value,
    query_gain,
    key_gain,
):
    dma = pltpu.SemaphoreType.DMA
    vmem = pl.BlockSpec(memory_space=pltpu.VMEM)
    out_shape = (
        jax.ShapeDtypeStruct((SEQS, LENGTH, COLS), BF16),
        jax.ShapeDtypeStruct((HALF, COLS), F32),
        jax.ShapeDtypeStruct((16, WIDTH), F32),
        jax.ShapeDtypeStruct((16, WIDTH), F32),
    )
    results = pl.pallas_call(
        kernel,
        out_shape=out_shape,
        in_specs=[pl.BlockSpec(memory_space=pl.ANY)] * 11,
        out_specs=(vmem,) * 4,
        scratch_shapes=[
            pltpu.SMEM((1, N_DP), jnp.int32),
            pltpu.SMEM((SEQS,), jnp.int32),
            pltpu.SMEM((SEQS,), jnp.int32),
            pltpu.SMEM((SEQS,), F32),
            pltpu.VMEM((SEQS, LENGTH, WIDTH), BF16),
            pltpu.VMEM((SEQS, LENGTH, COLS), BF16),
            pltpu.VMEM((N_MP * WIDTH, COLS), BF16),
            pltpu.VMEM((WIDTH, N_Y * HEAD), BF16),
            pltpu.VMEM((WIDTH, N_Y * HEAD), BF16),
            pltpu.VMEM((1, HEAD), F32),
            pltpu.VMEM((1, HEAD), F32),
            dma((15,)),
            pltpu.VMEM((1, N_DP), jnp.int32),
            pltpu.VMEM((SEQS,), jnp.int32),
            pltpu.VMEM((N_ZH, 1, N_DP), jnp.int32),
            pltpu.VMEM((N_ZH, SEQS), jnp.int32),
            pltpu.SMEM((N_ZH, 1, N_DP), jnp.int32),
            pltpu.SMEM((N_ZH, SEQS), jnp.int32),
            dma((4, 2)),
            dma((4, 2)),
            pltpu.VMEM((PADDED, TOKENS), BF16),
            pltpu.VMEM((N_Y, SHARE, HEAD), BF16),
            pltpu.VMEM((N_MP, WIDTH, TOKENS), BF16),
            pltpu.VMEM((2, N_MP, WIDTH, HEAD), BF16),
            *[pltpu.VMEM((SEQS + 1, LENGTH, COLS), BF16)] * N_ZH,
            pltpu.VMEM((len(PAIRS), N_ZH, LENGTH, COLS), BF16),
            pltpu.VMEM((len(PAIRS) + 1, N_ZH, LENGTH, COLS), BF16),
            pltpu.VMEM((COLS, TOKENS), F32),
            pltpu.VMEM((2, HEAD, TOKENS), F32),
            *[pltpu.VMEM((SEQS, LENGTH, COLS), BF16)] * N_ZH,
            pltpu.VMEM((len(PAIRS), N_ZH, LENGTH, COLS), BF16),
            pltpu.VMEM((len(PAIRS) + 1, N_ZH, LENGTH, COLS), BF16),
            pltpu.VMEM((TOKENS, COLS), BF16),
            pltpu.VMEM((N_X, N_ZH, HALF, COLS), BF16),
            pltpu.VMEM((N_X, N_ZH, HALF, COLS), BF16),
            pltpu.VMEM((N_X, N_ZH, HALF, COLS), BF16),
            pltpu.VMEM((N_X, N_ZH, HALF, COLS), BF16),
            pltpu.VMEM((N_ZH, HALF, COLS), BF16),
            pltpu.VMEM((N_ZH, HALF, COLS), BF16),
            pltpu.VMEM((N_ZL, 64, TOKENS), BF16),
            pltpu.VMEM((N_ZL, 64, TOKENS), BF16),
            pltpu.VMEM((N_Y, N_ZL, 64, TOKENS), BF16),
            pltpu.VMEM((N_CORE, N_ZH, N_X, 2, 16, PADDED), BF16),
            pltpu.VMEM((N_ZH, N_X, 2, 16, PADDED), BF16),
            pltpu.VMEM((N_X, N_ZH, 2, 16, PADDED), BF16),
            pltpu.VMEM((N_X, N_ZH, 2, 16, PADDED), BF16),
            pltpu.VMEM((N_ZH, 2, 16, PADDED), BF16),
            pltpu.VMEM((N_ZH, 2, 16, PADDED), BF16),
            dma((5,)),
            dma((4,)),
            dma((4, 2)),
            dma((4, 2)),
            dma((4, 2)),
            dma((4, 2)),
            dma,
            dma,
            dma((4,)),
            dma((4,)),
            dma((4,)),
            dma((4,)),
            dma((2, 2)),
            dma((2, 2)),
            dma((2,)),
            dma((2,)),
            dma,
            dma,
            dma((2, 2)),
            dma((2, 2)),
            dma((2,)),
            dma((2,)),
            dma,
            dma,
            dma((4,)),
            dma((4,)),
            dma((4,)),
            dma((4,)),
            dma((4, 4)),
            dma((4, 4)),
            dma((4,)),
            dma((4,)),
            dma((4, 4)),
            dma((4, 4)),
            dma((4,)),
            dma((4,)),
            dma((2,)),
            dma((2,)),
            dma((4, 2)),
            dma((4, 2)),
            dma((4,)),
            dma((4,)),
        ],
        compiler_params=pltpu.CompilerParams(
            collective_id=0, has_side_effects=True, vmem_limit_bytes=60 * 1024 * 1024
        ),
        name="train_step",
    )(
        send_table,
        slot_source,
        multiplicity,
        slot_weight,
        pool,
        cotangent,
        w_query,
        w_key,
        w_value,
        query_gain.reshape(1, HEAD),
        key_gain.reshape(1, HEAD),
    )
    attended, grad_query, grad_key, grad_value = pl.pallas_call(
        finish,
        out_shape=out_shape,
        in_specs=[vmem] * 4,
        out_specs=[vmem] * 4,
        compiler_params=pltpu.CompilerParams(vmem_limit_bytes=60 * 1024 * 1024),
        name="results",
    )(*results)
    return attended, grad_query, grad_key.T, grad_value.T


def solution(mesh):
    return jax.shard_map(
        local,
        mesh=mesh,
        in_specs=(
            P("dp", None, "mp"),
            P("dp", None),
            P("dp"),
            P("dp"),
            P("dp"),
            P("dp", None, "mp"),
            P(None, "mp"),
            P("mp", None),
            P("mp", None),
            P(),
            P(),
        ),
        out_specs=(P("dp", None, "mp"), P("dp", "mp"), P("mp", "dp"), P("mp", "dp")),
        check_vma=False,
    )
```

```python
import functools
import math

import jax
import jax.numpy as jnp
from jax import lax
from jax.experimental import pallas as pl
from jax.experimental.pallas import tpu as pltpu
from jax.sharding import PartitionSpec as P

F32, BF16 = jnp.float32, jnp.bfloat16
MESH = pl.DeviceIdType.MESH

N_X, N_ZH, N_CORE, N_Y, N_ZL = 4, 4, 2, 4, 4
N_DP, N_MP = N_X * N_ZH * N_CORE, N_Y * N_ZL
SEQS, LENGTH, WIDTH = 8, 32, 320
TOKENS = SEQS * LENGTH
HEAD, COLS = 128, 256
PADDED = 384
SHARE = WIDTH // N_X
HALF = WIDTH // 2
EPS = 1e-6
PAIRS = ((0, 1), (1, 0), (1, 1), (2, 0), (2, 1), (3, 0), (3, 1))
SCALE = 1.0 / math.sqrt(HEAD)


def dot_nn(a, b):
    return lax.dot_general(a, b, (((1,), (0,)), ((), ())), preferred_element_type=F32)


def dot_tn(a, b):
    return lax.dot_general(a, b, (((0,), (0,)), ((), ())), preferred_element_type=F32)


def dot_nt(a, b):
    return lax.dot_general(a, b, (((1,), (1,)), ((), ())), preferred_element_type=F32)


def rms_back(values, inverse, gain, grad_out):
    scaled = grad_out * gain
    inner = jnp.mean(values * scaled, axis=0, keepdims=True)
    return inverse * scaled - values * (inverse * inverse * inverse) * inner


def kernel(
    table_in,
    source_in,
    drawn_in,
    weight_in,
    pool_in,
    cotangent_in,
    w_query_in,
    w_key_in,
    w_value_in,
    q_gain_in,
    k_gain_in,
    att_out,
    gq_out,
    gk_out,
    gv_out,
    table,
    source,
    drawn,
    weight,
    pool,
    cotangent,
    w_query,
    w_key,
    w_value,
    q_gain,
    k_gain,
    load_s,
    table_row,
    source_row,
    tables,
    sources,
    near_tables,
    near_sources,
    ts_s,
    ts_r,
    x_ref,
    w_mine,
    piece,
    w_kv,
    d_all_0,
    d_all_1,
    d_all_2,
    d_all_3,
    d_send,
    d_slots,
    acc_q,
    acc_kv,
    att_all_0,
    att_all_1,
    att_all_2,
    att_all_3,
    att_send,
    att_slots,
    d_query,
    g_send,
    g_recv,
    g_keep,
    x_recv,
    z_send,
    z_recv,
    dkv,
    dkv_recv,
    dkv_all,
    kv_part,
    kv_recv,
    kv_sum,
    kv_x,
    kv_zs,
    kv_z,
    tz_s,
    tz_r,
    ty_s,
    ty_r,
    tf_s,
    tf_r,
    w1_s,
    w1_r,
    w2_s,
    w2_r,
    w3_s,
    w3_r,
    c1_s,
    c1_r,
    cf_s,
    cf_r,
    c2_s,
    c2_r,
    a1_s,
    a1_r,
    af_s,
    af_r,
    a2_s,
    a2_r,
    k1_s,
    k1_r,
    k2_s,
    k2_r,
    k3_s,
    k3_r,
    gc_s,
    gc_r,
    gx_s,
    gx_r,
    gz_s,
    gz_r,
    vc_s,
    vc_r,
    vx_s,
    vx_r,
    vz_s,
    vz_r,
):
    dp, mp = lax.axis_index("dp"), lax.axis_index("mp")
    x, zh, core = dp // (N_ZH * N_CORE), (dp // N_CORE) % N_ZH, dp % N_CORE
    y, zl = mp // N_ZL, mp % N_ZL
    other = 1 - core

    def pair(step, flip):
        return lax.rem(x + step, N_X) * (N_ZH * N_CORE) + zh * N_CORE + (
            other if flip else core
        )

    def at_mp(step):
        return dp, lax.rem(mp + step, N_MP)

    def at_x(step):
        return lax.rem(dp + step * (N_ZH * N_CORE), N_DP), mp

    def at_zh(step):
        return x * (N_ZH * N_CORE) + lax.rem(zh + step, N_ZH) * N_CORE + core, mp

    def at_y(step):
        return dp, lax.rem(mp + step * N_ZL, N_MP)

    def at_zl(step):
        return dp, y * N_ZL + lax.rem(zl + step, N_ZL)

    sibling = (dp + 1 - 2 * core, mp)
    d_all = (d_all_0, d_all_1, d_all_2, d_all_3)
    att_all = (att_all_0, att_all_1, att_all_2, att_all_3)

    def copy(src, dst, send, recv, device):
        return pltpu.make_async_remote_copy(
            src_ref=src,
            dst_ref=dst,
            send_sem=send,
            recv_sem=recv,
            device_id=device,
            device_id_type=MESH,
        )

    sends = []

    def start(*args):
        made = copy(*args)
        made.start()
        sends.append(made)

    barrier = pltpu.get_barrier_semaphore()
    partners = [at_mp(step) for step in range(1, N_MP)]
    partners += [at_zh(step) for step in range(1, N_ZH)]
    partners += [(pair(step, flip), mp) for step, flip in PAIRS]
    for device in partners:
        pl.semaphore_signal(barrier, inc=1, device_id=device, device_id_type=MESH)

    loads = {}
    for i, (name, src, dst) in enumerate(
        (
            ("pool", pool_in, pool),
            ("w_key", w_key_in, w_key),
            ("w_value", w_value_in, w_value),
            ("table_row", table_in, table_row),
            ("source_row", source_in, source_row),
            ("table", table_in, table),
            ("source", source_in, source),
            ("drawn", drawn_in, drawn),
            ("weight", weight_in, weight),
            ("cotangent", cotangent_in, cotangent),
            ("w_query", w_query_in, w_query),
            ("q_gain", q_gain_in, q_gain),
            ("k_gain", k_gain_in, k_gain),
        )
    ):
        loads[name] = pltpu.make_async_copy(src, dst, load_s.at[i])
        loads[name].start()

    for name in ("pool", "w_key", "w_value"):
        loads[name].wait()
    rows = pool[...].reshape(TOKENS, WIDTH).astype(F32)
    x_ref[:COLS] = rows[:, :COLS].T.astype(BF16)
    rest = [rows[:, COLS:], jnp.zeros((TOKENS, PADDED - WIDTH), F32)]
    x_ref[COLS:] = jnp.concatenate(rest, axis=1).T.astype(BF16)
    rows = pl.ds(pl.multiple_of(x * SHARE, 16), SHARE)
    for which, w_ref in ((0, w_key), (1, w_value)):

        @pl.when(core == which)
        def _():
            for g in range(N_Y):
                w_mine[g] = w_ref[rows, g * HEAD : (g + 1) * HEAD]

    loads["table_row"].wait()
    loads["source_row"].wait()
    pl.semaphore_wait(barrier, len(partners))

    fellow = zl + 1 - 2 * (zl % 2)
    across = N_ZL - 1 - zl
    inner = (zl == 1) | (zl == 2)
    line_of = (
        zl,
        fellow,
        jnp.where(zl < 2, jnp.int32(2), jnp.int32(1)),
        jnp.where(zl < 2, jnp.int32(3), jnp.int32(0)),
    )

    def mine(k):
        return y * N_ZL + line_of[k]

    def near(k, way):
        return lax.rem(y + (N_Y - 1 if way == 0 else 1), N_Y) * N_ZL + line_of[k]

    inner_sends = []

    def start_inner(*args):
        inner_sends.append(args)

        @pl.when(inner)
        def _():
            copy(*args).start()

    def along_y(k):
        spot = piece.at[mine(k)]
        for way, step in ((0, 1), (1, N_Y - 1)):
            start(spot, spot, ty_s.at[k, way], ty_r.at[k, way], at_y(step))

    piece[mp] = x_ref[:WIDTH]
    w_kv[core, mp, rows] = w_mine[y]
    for step in range(1, N_MP):
        dest = at_mp(step)
        start(w_mine.at[dest[1] // N_ZL], w_kv.at[core, mp, rows], w1_s, w1_r, dest)
    tokens = piece.at[mp]
    start(tokens, tokens, tz_s.at[0], tz_r.at[1], (dp, y * N_ZL + fellow))
    start_inner(tokens, tokens, tz_s.at[1], tz_r.at[2], (dp, y * N_ZL + across))
    along_y(0)

    for k in (1, 2, 3):
        start(table_row, tables.at[k], ts_s.at[k, 0], ts_r.at[k, 0], at_zh(N_ZH - k))
        start(source_row, sources.at[k], ts_s.at[k, 1], ts_r.at[k, 1], at_zh(N_ZH - k))

    half_slots = SEQS // 2

    def line_send(buf, send, recv):
        for part in (0, 1):
            for way, step in ((0, 1), (1, N_ZH - 1)):
                some = pl.ds((way ^ part) * half_slots, half_slots)
                start(
                    buf[0].at[some],
                    buf[N_ZH - 1 if way == 0 else 1].at[some],
                    send.at[way, part],
                    recv.at[way, part],
                    at_zh(step),
                )

    def line_wait(buf, send, recv, part, then):
        for way, step in ((0, 1), (1, N_ZH - 1)):
            some = pl.ds((way ^ part) * half_slots, half_slots)
            spot = buf[N_ZH - 1 if way == 0 else 1].at[some]
            copy(
                spot, spot, send.at[way, part], recv.at[way, part], at_zh(step)
            ).wait_recv()
            then(way, step, some, spot)

    def line_pass(buf, send, recv, send_on, recv_on):
        def on(way, step, some, spot):
            start(spot, buf[2].at[some], send_on.at[way], recv_on.at[way], at_zh(step))

        line_wait(buf, send, recv, 0, on)

    def line_rest(buf, send, recv):
        line_wait(buf, send, recv, 1, lambda *args: None)

    def line_end(buf, send_on, recv_on):
        for way in (0, 1):
            spot = buf[2].at[pl.ds(way * (SEQS // 2), SEQS // 2)]
            copy(spot, spot, send_on.at[way], recv_on.at[way], at_zh(1)).wait_recv()

    def deal(buf, k, pick, out, into, send, recv):
        for i, (step, flip) in enumerate(PAIRS):
            to = pair(step, flip)
            out[i, k] = buf[k][pick(k, to)]
            start(out.at[i, k], into.at[i, k], send, recv, (to, mp))
        into[len(PAIRS), k] = buf[k][pick(k, dp)]

    def dealt(into, send, recv):
        spot = into.at[pl.ds(0, len(PAIRS))]
        copy(spot, spot, send, recv, sibling).wait_recv()

    for name in ("drawn", "weight", "cotangent", "table", "source"):
        loads[name].wait()
    for s in range(SEQS):
        factor = drawn[s].astype(F32) * weight[s] * (1.0 / LENGTH)
        d_all[0][s] = (cotangent[s].astype(F32) * factor).astype(BF16)
    for k in range(N_ZH):
        d_all[k][SEQS] = jnp.zeros((LENGTH, COLS), BF16)

    def slot_of(k, rank):
        found = jnp.int32(SEQS)
        for s in range(SEQS):
            have = source[s] if k == 0 else near_sources[k, s]
            found = jnp.where(have == rank, jnp.int32(s), found)
        return found

    deal(d_all, 0, slot_of, d_send, d_slots, c2_s, c2_r)

    acc_q[...] = jnp.zeros_like(acc_q)

    def project(j):
        place = pl.ds(pl.multiple_of(j * WIDTH, WIDTH), WIDTH)
        acc_q[...] += dot_tn(w_query[place], piece[j])

    def wait_near(k, way):
        spot = piece.at[near(k, way)]
        copy(spot, spot, ty_s.at[k, way], ty_r.at[k, way], at_y(1)).wait_recv()

    def pass_on(k):
        for way, step in ((0, 1), (1, N_Y - 1)):
            wait_near(k, way)
            half = piece.at[near(k, way), pl.ds(way * HALF, HALF)]
            start(half, half, tf_s.at[k, way], tf_r.at[k, way], at_y(step))

    def take(k):
        spot = piece.at[mine(k)]
        copy(spot, spot, tz_s.at[k], tz_r.at[k], at_y(1)).wait_recv()
        to = across if k == 1 else fellow
        start_inner(
            spot, spot, tz_s.at[k + 1], tz_r.at[3 if k == 1 else k], (dp, y * N_ZL + to)
        )
        along_y(k)

    def w_rows(step):
        at = lax.rem(x + step, N_X) * SHARE
        return w_kv.at[core, :, pl.ds(pl.multiple_of(at, 16), SHARE)]

    def w_across(step):
        spot = w_rows(step)
        start(spot, spot, w3_s.at[step], w3_r.at[step], sibling)

    def w_arrived(step):
        spot = w_rows(N_X - step)
        copy(spot, spot, w2_s.at[step], w2_r.at[step], at_x(step)).wait_recv()
        w_across(N_X - step)

    def far_arrived(k):
        far = lax.rem(y + 2, N_Y) * N_ZL + line_of[k]
        for way in (0, 1):
            half = piece.at[far, pl.ds(way * HALF, HALF)]
            copy(half, half, tf_s.at[k, way], tf_r.at[k, way], at_y(1)).wait_recv()
        project(far)

    loads["w_query"].wait()
    project(mp)
    take(1)
    pass_on(0)
    got = w_kv.at[0, pl.ds(0, N_MP - 1), pl.ds(0, SHARE)]
    copy(got, got, w1_s, w1_r, at_mp(1)).wait_recv()
    for k in (1, 3, 2):
        start(w_rows(0), w_rows(0), w2_s.at[k], w2_r.at[k], at_x(k))
    w_across(0)
    project(mine(1))
    for way in (0, 1):
        project(near(0, way))
    take(2)
    line_send(d_all, c1_s, c1_r)
    project(mine(2))
    pass_on(1)
    take(3)
    project(mine(3))
    far_arrived(0)
    pass_on(2)
    for k in (1, 2, 3):
        for i, row, rows in ((0, table_row, tables), (1, source_row, sources)):
            copy(
                row, rows.at[k], ts_s.at[k, i], ts_r.at[k, i], at_zh(k)
            ).wait_recv()
    fetches = [
        pltpu.make_async_copy(tables, near_tables, load_s.at[13]),
        pltpu.make_async_copy(sources, near_sources, load_s.at[14]),
    ]
    for fetch in fetches:
        fetch.start()
    for fetch in fetches:
        fetch.wait()
    w_arrived(1)
    w_arrived(3)
    for way in (0, 1):
        project(near(1, way))
    for way in (0, 1):
        project(near(2, way))
    line_pass(d_all, c1_s, c1_r, cf_s, cf_r)
    pass_on(3)
    w_arrived(2)
    for way in (0, 1):
        project(near(3, way))
    far_arrived(1)
    far_arrived(2)
    line_rest(d_all, c1_s, c1_r)
    for k in (1, 3):
        deal(d_all, k, slot_of, d_send, d_slots, c2_s, c2_r)
    far_arrived(3)
    line_end(d_all, cf_s, cf_r)
    deal(d_all, 2, slot_of, d_send, d_slots, c2_s, c2_r)
    for k in range(N_X):
        at = lax.rem(x + k, N_X) * SHARE
        spot = w_kv.at[other, :, pl.ds(pl.multiple_of(at, 16), SHARE)]
        copy(spot, spot, w3_s.at[k], w3_r.at[k], sibling).wait_recv()
    gathered = piece[...].reshape(N_MP * WIDTH, TOKENS)
    for half in (0, 1):
        w_half = w_kv[half].reshape(N_MP * WIDTH, HEAD)
        acc_kv[half] = dot_tn(w_half, gathered)

    loads["q_gain"].wait()
    loads["k_gain"].wait()
    gain_q, gain_k = (
        jnp.broadcast_to(gain[...], (HEAD, HEAD)).T[:, :1] for gain in (q_gain, k_gain)
    )
    key_sum = acc_kv[0]
    k_inverse = lax.rsqrt(jnp.mean(key_sum * key_sum, axis=0, keepdims=True) + EPS)
    k_norm = (key_sum * k_inverse * gain_k).astype(BF16)
    value = acc_kv[1].astype(BF16)
    at_key = lax.broadcasted_iota(jnp.int32, (TOKENS, TOKENS), 0)
    at_query = lax.broadcasted_iota(jnp.int32, (TOKENS, TOKENS), 1)
    seen = ((at_key >> 5) == (at_query >> 5)) & (at_key <= at_query)
    saved = []
    for h in range(COLS // HEAD):
        query = acc_q[h * HEAD : (h + 1) * HEAD]
        inverse = lax.rsqrt(jnp.mean(query * query, axis=0, keepdims=True) + EPS)
        q_norm = (query * inverse * gain_q).astype(BF16)
        scores = jnp.where(seen, dot_tn(k_norm, q_norm) * SCALE, -1e30)
        raised = jnp.exp(scores - jnp.max(scores, axis=0, keepdims=True))
        probs = raised / jnp.sum(raised, axis=0, keepdims=True)
        p_half = probs.astype(BF16)
        out = dot_nn(value, p_half).T.astype(BF16)
        att_all[0][:, :, h * HEAD : (h + 1) * HEAD] = out.reshape(SEQS, LENGTH, HEAD)
        saved.append((query, inverse, q_norm, probs, p_half))
    def sent_to(k, rank):
        have = table[0, rank] if k == 0 else near_tables[k, 0, rank]
        return jnp.maximum(have, 0)

    line_send(att_all, a1_s, a1_r)
    deal(att_all, 0, sent_to, att_send, att_slots, a2_s, a2_r)

    dealt(d_slots, c2_s, c2_r)
    lane = lax.broadcasted_iota(jnp.int32, (1, N_DP * LENGTH), 1)
    target = jnp.zeros_like(lane)

    def sender(step, flip, k):
        of_x = lax.rem(x + N_X - step, N_X)
        of_core = other if flip else core
        return of_x * (N_ZH * N_CORE) + lax.rem(zh + k, N_ZH) * N_CORE + of_core

    for i, (step, flip) in enumerate(PAIRS + ((0, 0),)):
        for k in range(N_ZH):
            entry = table[0, sender(step, flip, k)]
            here = (lane >> 5) == i * N_ZH + k
            target = jnp.where(here, entry * LENGTH, target)
    target = jnp.where(target < 0, -1, target + (lane & (LENGTH - 1)))
    place = lax.broadcasted_iota(jnp.int32, (TOKENS, N_DP * LENGTH), 0)
    chosen = jnp.where(place == target, 1.0, 0.0).astype(BF16)
    d_rows = dot_nn(chosen, d_slots[...].reshape(N_DP * LENGTH, COLS))
    d_cols = d_rows.T.astype(BF16)
    d_knorm = jnp.zeros((HEAD, TOKENS), F32)
    d_value = jnp.zeros((HEAD, TOKENS), F32)
    d_queries = []
    for h in range(COLS // HEAD):
        query, inverse, q_norm, probs, p_half = saved[h]
        out_half = d_cols[h * HEAD : (h + 1) * HEAD]
        d_probs = dot_tn(value, out_half)
        d_value += dot_nt(out_half, p_half)
        centred = d_probs - jnp.sum(d_probs * probs, axis=0, keepdims=True)
        score_half = (probs * centred * SCALE).astype(BF16)
        d_qnorm = dot_nn(k_norm, score_half)
        d_knorm += dot_nt(q_norm, score_half)
        d_queries.append((query, inverse, gain_q, d_qnorm))
    d_key = rms_back(key_sum, k_inverse, gain_k, d_knorm).astype(BF16)
    d_value = d_value.astype(BF16)
    for q in (0, 1):
        dkv[q] = d_key[q * 64 : (q + 1) * 64]
        dkv[2 + q] = d_value[q * 64 : (q + 1) * 64]

    for k in (1, 2, 3):
        start(
            dkv.at[lax.rem(zl + k, N_ZL)],
            dkv_recv.at[k],
            k1_s.at[k],
            k1_r.at[k],
            at_zl(k),
        )

    for h in range(COLS // HEAD):
        d_query[:, h * HEAD : (h + 1) * HEAD] = rms_back(*d_queries[h]).T.astype(BF16)

    def x_at(step):
        return lax.rem(x + step, N_X)

    def zh_at(step):
        return lax.rem(zh + step, N_ZH)

    def partial_rows(to, into, which):
        rows = pl.ds(pl.multiple_of(which * HALF, 16), HALF)
        for i in range(N_X):
            total = dot_nn(piece[i * N_ZH + to, rows], d_query[...])
            into[to, i] = total.astype(BF16)

    def core_step(kz):
        to = zh_at(kz)
        copy(
            g_send.at[to], g_recv.at[to], gc_s.at[kz], gc_r.at[kz], sibling
        ).wait_recv()
        both = g_keep[to].astype(F32) + g_recv[to].astype(F32)
        g_keep[to] = both.astype(BF16)
        for k in (2, 1, 3):
            start(
                g_keep.at[to, x_at(k)],
                x_recv.at[to, k],
                gx_s.at[k, kz],
                gx_r.at[k, kz],
                at_x(k),
            )

    def x_step(kz):
        to = zh_at(kz)
        total = g_keep[to, x].astype(F32)
        for k in (1, 2, 3):
            spot = x_recv.at[to, k]
            copy(spot, spot, gx_s.at[k, kz], gx_r.at[k, kz], at_x(k)).wait_recv()
            total += x_recv[to, k].astype(F32)
        z_send[to] = total.astype(BF16)
        if kz:
            start(z_send.at[to], z_recv.at[kz], gz_s.at[kz], gz_r.at[kz], at_zh(kz))

    order = (2, 1, 3, 0)

    def kv_place(i):
        step = lax.rem(i + N_ZH - zh, N_ZH)
        return jnp.where(
            step == 0, 3, jnp.where(step == 1, 1, jnp.where(step == 2, 0, 2))
        )

    def kv_core_step(k):
        copy(
            kv_part.at[other, k], kv_recv.at[k], vc_s.at[k], vc_r.at[k], sibling
        ).wait_recv()
        both = kv_part[core, k].astype(F32) + kv_recv[k].astype(F32)
        kv_sum[k] = both.astype(BF16)
        for part in (0, 1) if k else ():
            some = pl.ds(2 * part, 2)
            start(
                kv_sum.at[k, some],
                kv_x.at[k, some],
                vx_s.at[k, part],
                vx_r.at[k, part],
                at_x(k),
            )

    def kv_x_step(part):
        some = pl.ds(2 * part, 2)
        total = kv_sum[0, some].astype(F32)
        for k in (1, 2, 3):
            spot = kv_x.at[k, some]
            copy(
                spot, spot, vx_s.at[k, part], vx_r.at[k, part], at_x(k)
            ).wait_recv()
            total += kv_x[k, some].astype(F32)
        kv_zs[some] = total.astype(BF16)
        for p in (0, 1):
            k = order[2 * part + p]
            if k:
                start(
                    kv_zs.at[2 * part + p],
                    kv_z.at[k],
                    vz_s.at[k],
                    vz_r.at[k],
                    at_zh(k),
                )

    for kz in order:
        to = zh_at(kz)
        partial_rows(to, g_send, other)
        start(g_send.at[to], g_recv.at[to], gc_s.at[kz], gc_r.at[kz], sibling)
    for kz in order:
        partial_rows(zh_at(kz), g_keep, core)
    for k in (1, 2, 3):
        copy(
            dkv.at[0], dkv_recv.at[k], k1_s.at[k], k1_r.at[k], at_zl(k)
        ).wait_recv()
    total = dkv[zl].astype(F32)
    for k in (1, 2, 3):
        total += dkv_recv[k].astype(F32)
    dkv_all[y, zl] = total.astype(BF16)

    def quarter(step_y, k):
        of_y = lax.rem(y + N_Y - step_y, N_Y)
        return dkv_all.at[of_y, lax.rem(zl + N_ZL - k, N_ZL)]

    def quarter_along_y(k):
        spot = quarter(0, k)
        for step in (2, 1, 3):
            start(spot, spot, k3_s.at[k, step], k3_r.at[k, step], at_y(step))

    for k in (1, 2, 3):
        spot = quarter(0, 0)
        start(spot, spot, k2_s.at[k], k2_r.at[k], at_zl(k))
    quarter_along_y(0)
    core_step(2)
    core_step(1)
    for k in (1, 2, 3):
        spot = quarter(0, k)
        copy(spot, spot, k2_s.at[k], k2_r.at[k], at_zl(k)).wait_recv()
        quarter_along_y(k)
    line_pass(att_all, a1_s, a1_r, af_s, af_r)
    core_step(3)
    core_step(0)
    x_step(2)
    for k in range(N_ZL):
        for step in (1, 2, 3):
            spot = quarter(step, k)
            copy(
                spot, spot, k3_s.at[k, step], k3_r.at[k, step], at_y(step)
            ).wait_recv()
    for step in order:
        rows = dkv_all[x_at(step)].reshape(2 * HEAD, TOKENS)
        product = dot_nt(rows, x_ref[...]).astype(BF16)
        for half in range(2):
            for i in range(N_ZH):
                for c in range(N_CORE):
                    first = half * HEAD + i * 32 + c * 16
                    kv_part[c, step, kv_place(i), half] = product[first : first + 16]
        start(
            kv_part.at[other, step],
            kv_recv.at[step],
            vc_s.at[step],
            vc_r.at[step],
            sibling,
        )
    line_rest(att_all, a1_s, a1_r)
    for k in (1, 3):
        deal(att_all, k, sent_to, att_send, att_slots, a2_s, a2_r)
    for k in order:
        kv_core_step(k)
    x_step(1)
    line_end(att_all, af_s, af_r)
    deal(att_all, 2, sent_to, att_send, att_slots, a2_s, a2_r)
    x_step(3)
    kv_x_step(0)
    kv_x_step(1)
    x_step(0)
    total = z_send[zh].astype(F32)
    for k in (1, 2, 3):
        copy(z_send.at[0], z_recv.at[k], gz_s.at[k], gz_r.at[k], at_zh(k)).wait_recv()
        total += z_recv[k].astype(F32)
    gq_out[...] = total

    total = kv_zs[3].astype(F32)
    for k in (1, 2, 3):
        copy(kv_zs.at[0], kv_z.at[k], vz_s.at[k], vz_r.at[k], at_zh(k)).wait_recv()
        total += kv_z[k].astype(F32)
    gk_out[...] = total[0][:, :WIDTH]
    gv_out[...] = total[1][:, :WIDTH]

    dealt(att_slots, a2_s, a2_r)
    for s in range(SEQS):
        rank = source[s]
        step = lax.rem(x + N_X - rank // (N_ZH * N_CORE), N_X)
        flip = lax.rem(rank + core, N_CORE)
        k = lax.rem((rank // N_CORE) % N_ZH + N_ZH - zh, N_ZH)
        place = lax.rem(step * N_CORE + flip + len(PAIRS), len(PAIRS) + 1)
        att_out[s] = att_slots[place, k]
    for made in sends:
        made.wait_send()

    @pl.when(inner)
    def _():
        for args in inner_sends:
            copy(*args).wait_send()


def finish(*refs):
    for src, dst in zip(refs[:4], refs[4:]):
        dst[...] = src[...]


def local(
    pool,
    send_table,
    slot_source,
    multiplicity,
    slot_weight,
    cotangent,
    w_query,
    w_key,
    w_value,
    query_gain,
    key_gain,
):
    dma = pltpu.SemaphoreType.DMA
    vmem = pl.BlockSpec(memory_space=pltpu.VMEM)
    out_shape = (
        jax.ShapeDtypeStruct((SEQS, LENGTH, COLS), BF16),
        jax.ShapeDtypeStruct((HALF, COLS), F32),
        jax.ShapeDtypeStruct((16, WIDTH), F32),
        jax.ShapeDtypeStruct((16, WIDTH), F32),
    )
    results = pl.pallas_call(
        kernel,
        out_shape=out_shape,
        in_specs=[pl.BlockSpec(memory_space=pl.ANY)] * 11,
        out_specs=(vmem,) * 4,
        scratch_shapes=[
            pltpu.SMEM((1, N_DP), jnp.int32),
            pltpu.SMEM((SEQS,), jnp.int32),
            pltpu.SMEM((SEQS,), jnp.int32),
            pltpu.SMEM((SEQS,), F32),
            pltpu.VMEM((SEQS, LENGTH, WIDTH), BF16),
            pltpu.VMEM((SEQS, LENGTH, COLS), BF16),
            pltpu.VMEM((N_MP * WIDTH, COLS), BF16),
            pltpu.VMEM((WIDTH, N_Y * HEAD), BF16),
            pltpu.VMEM((WIDTH, N_Y * HEAD), BF16),
            pltpu.VMEM((1, HEAD), F32),
            pltpu.VMEM((1, HEAD), F32),
            dma((15,)),
            pltpu.VMEM((1, N_DP), jnp.int32),
            pltpu.VMEM((SEQS,), jnp.int32),
            pltpu.VMEM((N_ZH, 1, N_DP), jnp.int32),
            pltpu.VMEM((N_ZH, SEQS), jnp.int32),
            pltpu.SMEM((N_ZH, 1, N_DP), jnp.int32),
            pltpu.SMEM((N_ZH, SEQS), jnp.int32),
            dma((4, 2)),
            dma((4, 2)),
            pltpu.VMEM((PADDED, TOKENS), BF16),
            pltpu.VMEM((N_Y, SHARE, HEAD), BF16),
            pltpu.VMEM((N_MP, WIDTH, TOKENS), BF16),
            pltpu.VMEM((2, N_MP, WIDTH, HEAD), BF16),
            *[pltpu.VMEM((SEQS + 1, LENGTH, COLS), BF16)] * N_ZH,
            pltpu.VMEM((len(PAIRS), N_ZH, LENGTH, COLS), BF16),
            pltpu.VMEM((len(PAIRS) + 1, N_ZH, LENGTH, COLS), BF16),
            pltpu.VMEM((COLS, TOKENS), F32),
            pltpu.VMEM((2, HEAD, TOKENS), F32),
            *[pltpu.VMEM((SEQS, LENGTH, COLS), BF16)] * N_ZH,
            pltpu.VMEM((len(PAIRS), N_ZH, LENGTH, COLS), BF16),
            pltpu.VMEM((len(PAIRS) + 1, N_ZH, LENGTH, COLS), BF16),
            pltpu.VMEM((TOKENS, COLS), BF16),
            pltpu.VMEM((N_X, N_ZH, HALF, COLS), BF16),
            pltpu.VMEM((N_X, N_ZH, HALF, COLS), BF16),
            pltpu.VMEM((N_X, N_ZH, HALF, COLS), BF16),
            pltpu.VMEM((N_X, N_ZH, HALF, COLS), BF16),
            pltpu.VMEM((N_ZH, HALF, COLS), BF16),
            pltpu.VMEM((N_ZH, HALF, COLS), BF16),
            pltpu.VMEM((N_ZL, 64, TOKENS), BF16),
            pltpu.VMEM((N_ZL, 64, TOKENS), BF16),
            pltpu.VMEM((N_Y, N_ZL, 64, TOKENS), BF16),
            pltpu.VMEM((N_CORE, N_X, N_ZH, 2, 16, PADDED), BF16),
            pltpu.VMEM((N_X, N_ZH, 2, 16, PADDED), BF16),
            pltpu.VMEM((N_X, N_ZH, 2, 16, PADDED), BF16),
            pltpu.VMEM((N_X, N_ZH, 2, 16, PADDED), BF16),
            pltpu.VMEM((N_ZH, 2, 16, PADDED), BF16),
            pltpu.VMEM((N_ZH, 2, 16, PADDED), BF16),
            dma((5,)),
            dma((4,)),
            dma((4, 2)),
            dma((4, 2)),
            dma((4, 2)),
            dma((4, 2)),
            dma,
            dma,
            dma((4,)),
            dma((4,)),
            dma((4,)),
            dma((4,)),
            dma((2, 2)),
            dma((2, 2)),
            dma((2,)),
            dma((2,)),
            dma,
            dma,
            dma((2, 2)),
            dma((2, 2)),
            dma((2,)),
            dma((2,)),
            dma,
            dma,
            dma((4,)),
            dma((4,)),
            dma((4,)),
            dma((4,)),
            dma((4, 4)),
            dma((4, 4)),
            dma((4,)),
            dma((4,)),
            dma((4, 4)),
            dma((4, 4)),
            dma((4,)),
            dma((4,)),
            dma((4,)),
            dma((4,)),
            dma((4, 2)),
            dma((4, 2)),
            dma((4,)),
            dma((4,)),
        ],
        compiler_params=pltpu.CompilerParams(
            collective_id=0, has_side_effects=True, vmem_limit_bytes=60 * 1024 * 1024
        ),
        name="train_step",
    )(
        send_table,
        slot_source,
        multiplicity,
        slot_weight,
        pool,
        cotangent,
        w_query,
        w_key,
        w_value,
        query_gain.reshape(1, HEAD),
        key_gain.reshape(1, HEAD),
    )
    attended, grad_query, grad_key, grad_value = pl.pallas_call(
        finish,
        out_shape=out_shape,
        in_specs=[vmem] * 4,
        out_specs=[vmem] * 4,
        compiler_params=pltpu.CompilerParams(vmem_limit_bytes=60 * 1024 * 1024),
        name="results",
    )(*results)
    return attended, grad_query, grad_key.T, grad_value.T


def solution(mesh):
    return jax.shard_map(
        local,
        mesh=mesh,
        in_specs=(
            P("dp", None, "mp"),
            P("dp", None),
            P("dp"),
            P("dp"),
            P("dp"),
            P("dp", None, "mp"),
            P(None, "mp"),
            P("mp", None),
            P("mp", None),
            P(),
            P(),
        ),
        out_specs=(P("dp", None, "mp"), P("dp", "mp"), P("mp", "dp"), P("mp", "dp")),
        check_vma=False,
    )
```

```python
import functools
import math

import jax
import jax.numpy as jnp
from jax import lax
from jax.experimental import pallas as pl
from jax.experimental.pallas import tpu as pltpu
from jax.sharding import PartitionSpec as P

F32, BF16 = jnp.float32, jnp.bfloat16
MESH = pl.DeviceIdType.MESH

N_X, N_ZH, N_CORE, N_Y, N_ZL = 4, 4, 2, 4, 4
N_DP, N_MP = N_X * N_ZH * N_CORE, N_Y * N_ZL
SEQS, LENGTH, WIDTH = 8, 32, 320
TOKENS = SEQS * LENGTH
HEAD, COLS = 128, 256
PADDED = 384
SHARE = WIDTH // N_X
HALF = WIDTH // 2
EPS = 1e-6
PAIRS = ((0, 1), (1, 0), (1, 1), (2, 0), (2, 1), (3, 0), (3, 1))
SCALE = 1.0 / math.sqrt(HEAD)


def dot_nn(a, b):
    return lax.dot_general(a, b, (((1,), (0,)), ((), ())), preferred_element_type=F32)


def dot_tn(a, b):
    return lax.dot_general(a, b, (((0,), (0,)), ((), ())), preferred_element_type=F32)


def dot_nt(a, b):
    return lax.dot_general(a, b, (((1,), (1,)), ((), ())), preferred_element_type=F32)


def rms_back(values, inverse, gain, grad_out):
    scaled = grad_out * gain
    inner = jnp.mean(values * scaled, axis=0, keepdims=True)
    return inverse * scaled - values * (inverse * inverse * inverse) * inner


def kernel(
    table_in,
    source_in,
    drawn_in,
    weight_in,
    pool_in,
    cotangent_in,
    w_query_in,
    w_key_in,
    w_value_in,
    q_gain_in,
    k_gain_in,
    att_out,
    gq_out,
    gk_out,
    gv_out,
    table,
    source,
    drawn,
    weight,
    pool,
    cotangent,
    w_query,
    w_key,
    w_value,
    q_gain,
    k_gain,
    load_s,
    table_row,
    source_row,
    tables,
    sources,
    near_tables,
    near_sources,
    ts_s,
    ts_r,
    x_ref,
    w_mine,
    piece,
    w_kv,
    d_all_0,
    d_all_1,
    d_all_2,
    d_all_3,
    d_send,
    d_slots,
    acc_q,
    acc_kv,
    att_all_0,
    att_all_1,
    att_all_2,
    att_all_3,
    att_send,
    att_slots,
    d_query,
    g_send,
    g_recv,
    g_keep,
    x_recv,
    z_send,
    z_recv,
    z_pass,
    dkv,
    dkv_recv,
    dkv_all,
    kv_part,
    kv_recv,
    kv_sum,
    kv_x,
    kv_zs,
    kv_z,
    tz_s,
    tz_r,
    ty_s,
    ty_r,
    tf_s,
    tf_r,
    w1_s,
    w1_r,
    w2_s,
    w2_r,
    w3_s,
    w3_r,
    c1_s,
    c1_r,
    cf_s,
    cf_r,
    c2_s,
    c2_r,
    a1_s,
    a1_r,
    af_s,
    af_r,
    a2_s,
    a2_r,
    k1_s,
    k1_r,
    k2_s,
    k2_r,
    k3_s,
    k3_r,
    gc_s,
    gc_r,
    gx_s,
    gx_r,
    gp_s,
    gp_r,
    gz_s,
    gz_r,
    vc_s,
    vc_r,
    vx_s,
    vx_r,
    vz_s,
    vz_r,
):
    dp, mp = lax.axis_index("dp"), lax.axis_index("mp")
    x, zh, core = dp // (N_ZH * N_CORE), (dp // N_CORE) % N_ZH, dp % N_CORE
    y, zl = mp // N_ZL, mp % N_ZL
    other = 1 - core

    def pair(step, flip):
        return lax.rem(x + step, N_X) * (N_ZH * N_CORE) + zh * N_CORE + (
            other if flip else core
        )

    def at_mp(step):
        return dp, lax.rem(mp + step, N_MP)

    def at_x(step):
        return lax.rem(dp + step * (N_ZH * N_CORE), N_DP), mp

    def at_zh(step):
        return x * (N_ZH * N_CORE) + lax.rem(zh + step, N_ZH) * N_CORE + core, mp

    def at_y(step):
        return dp, lax.rem(mp + step * N_ZL, N_MP)

    def at_zl(step):
        return dp, y * N_ZL + lax.rem(zl + step, N_ZL)

    sibling = (dp + 1 - 2 * core, mp)
    d_all = (d_all_0, d_all_1, d_all_2, d_all_3)
    att_all = (att_all_0, att_all_1, att_all_2, att_all_3)

    def copy(src, dst, send, recv, device):
        return pltpu.make_async_remote_copy(
            src_ref=src,
            dst_ref=dst,
            send_sem=send,
            recv_sem=recv,
            device_id=device,
            device_id_type=MESH,
        )

    sends = []

    def start(*args):
        made = copy(*args)
        made.start()
        sends.append(made)

    barrier = pltpu.get_barrier_semaphore()
    partners = [at_mp(step) for step in range(1, N_MP)]
    partners += [at_zh(step) for step in range(1, N_ZH)]
    partners += [(pair(step, flip), mp) for step, flip in PAIRS]
    for device in partners:
        pl.semaphore_signal(barrier, inc=1, device_id=device, device_id_type=MESH)

    loads = {}
    for i, (name, src, dst) in enumerate(
        (
            ("pool", pool_in, pool),
            ("w_key", w_key_in, w_key),
            ("w_value", w_value_in, w_value),
            ("table_row", table_in, table_row),
            ("source_row", source_in, source_row),
            ("table", table_in, table),
            ("source", source_in, source),
            ("drawn", drawn_in, drawn),
            ("weight", weight_in, weight),
            ("cotangent", cotangent_in, cotangent),
            ("w_query", w_query_in, w_query),
            ("q_gain", q_gain_in, q_gain),
            ("k_gain", k_gain_in, k_gain),
        )
    ):
        loads[name] = pltpu.make_async_copy(src, dst, load_s.at[i])
        loads[name].start()

    for name in ("pool", "w_key", "w_value"):
        loads[name].wait()
    rows = pool[...].reshape(TOKENS, WIDTH).astype(F32)
    x_ref[:COLS] = rows[:, :COLS].T.astype(BF16)
    rest = [rows[:, COLS:], jnp.zeros((TOKENS, PADDED - WIDTH), F32)]
    x_ref[COLS:] = jnp.concatenate(rest, axis=1).T.astype(BF16)
    rows = pl.ds(pl.multiple_of(x * SHARE, 16), SHARE)
    for which, w_ref in ((0, w_key), (1, w_value)):

        @pl.when(core == which)
        def _():
            for g in range(N_Y):
                w_mine[g] = w_ref[rows, g * HEAD : (g + 1) * HEAD]

    loads["table_row"].wait()
    loads["source_row"].wait()
    pl.semaphore_wait(barrier, len(partners))

    fellow = zl + 1 - 2 * (zl % 2)
    across = N_ZL - 1 - zl
    inner = (zl == 1) | (zl == 2)
    line_of = (
        zl,
        fellow,
        jnp.where(zl < 2, jnp.int32(2), jnp.int32(1)),
        jnp.where(zl < 2, jnp.int32(3), jnp.int32(0)),
    )

    def mine(k):
        return y * N_ZL + line_of[k]

    def near(k, way):
        return lax.rem(y + (N_Y - 1 if way == 0 else 1), N_Y) * N_ZL + line_of[k]

    inner_sends = []

    def start_inner(*args):
        inner_sends.append(args)

        @pl.when(inner)
        def _():
            copy(*args).start()

    def along_y(k):
        spot = piece.at[mine(k)]
        for way, step in ((0, 1), (1, N_Y - 1)):
            start(spot, spot, ty_s.at[k, way], ty_r.at[k, way], at_y(step))

    piece[mp] = x_ref[:WIDTH]
    w_kv[core, mp, rows] = w_mine[y]
    for step in range(1, N_MP):
        dest = at_mp(step)
        start(w_mine.at[dest[1] // N_ZL], w_kv.at[core, mp, rows], w1_s, w1_r, dest)
    tokens = piece.at[mp]
    start(tokens, tokens, tz_s.at[0], tz_r.at[1], (dp, y * N_ZL + fellow))
    start_inner(tokens, tokens, tz_s.at[1], tz_r.at[2], (dp, y * N_ZL + across))
    along_y(0)

    for k in (1, 2, 3):
        start(table_row, tables.at[k], ts_s.at[k, 0], ts_r.at[k, 0], at_zh(N_ZH - k))
        start(source_row, sources.at[k], ts_s.at[k, 1], ts_r.at[k, 1], at_zh(N_ZH - k))

    half_slots = SEQS // 2

    def line_send(buf, send, recv):
        for part in (0, 1):
            for way, step in ((0, 1), (1, N_ZH - 1)):
                some = pl.ds((way ^ part) * half_slots, half_slots)
                start(
                    buf[0].at[some],
                    buf[N_ZH - 1 if way == 0 else 1].at[some],
                    send.at[way, part],
                    recv.at[way, part],
                    at_zh(step),
                )

    def line_wait(buf, send, recv, part, then):
        for way, step in ((0, 1), (1, N_ZH - 1)):
            some = pl.ds((way ^ part) * half_slots, half_slots)
            spot = buf[N_ZH - 1 if way == 0 else 1].at[some]
            copy(
                spot, spot, send.at[way, part], recv.at[way, part], at_zh(step)
            ).wait_recv()
            then(way, step, some, spot)

    def line_pass(buf, send, recv, send_on, recv_on):
        def on(way, step, some, spot):
            start(spot, buf[2].at[some], send_on.at[way], recv_on.at[way], at_zh(step))

        line_wait(buf, send, recv, 0, on)

    def line_rest(buf, send, recv):
        line_wait(buf, send, recv, 1, lambda *args: None)

    def line_end(buf, send_on, recv_on):
        for way in (0, 1):
            spot = buf[2].at[pl.ds(way * (SEQS // 2), SEQS // 2)]
            copy(spot, spot, send_on.at[way], recv_on.at[way], at_zh(1)).wait_recv()

    def deal(buf, k, pick, out, into, send, recv):
        for i, (step, flip) in enumerate(PAIRS):
            to = pair(step, flip)
            out[i, k] = buf[k][pick(k, to)]
            start(out.at[i, k], into.at[i, k], send, recv, (to, mp))
        into[len(PAIRS), k] = buf[k][pick(k, dp)]

    def dealt(into, send, recv):
        spot = into.at[pl.ds(0, len(PAIRS))]
        copy(spot, spot, send, recv, sibling).wait_recv()

    for name in ("drawn", "weight", "cotangent", "table", "source"):
        loads[name].wait()
    for s in range(SEQS):
        factor = drawn[s].astype(F32) * weight[s] * (1.0 / LENGTH)
        d_all[0][s] = (cotangent[s].astype(F32) * factor).astype(BF16)
    for k in range(N_ZH):
        d_all[k][SEQS] = jnp.zeros((LENGTH, COLS), BF16)

    def slot_of(k, rank):
        found = jnp.int32(SEQS)
        for s in range(SEQS):
            have = source[s] if k == 0 else near_sources[k, s]
            found = jnp.where(have == rank, jnp.int32(s), found)
        return found

    deal(d_all, 0, slot_of, d_send, d_slots, c2_s, c2_r)

    acc_q[...] = jnp.zeros_like(acc_q)

    def project(j):
        place = pl.ds(pl.multiple_of(j * WIDTH, WIDTH), WIDTH)
        acc_q[...] += dot_tn(w_query[place], piece[j])

    def wait_near(k, way):
        spot = piece.at[near(k, way)]
        copy(spot, spot, ty_s.at[k, way], ty_r.at[k, way], at_y(1)).wait_recv()

    def pass_on(k):
        for way, step in ((0, 1), (1, N_Y - 1)):
            wait_near(k, way)
            half = piece.at[near(k, way), pl.ds(way * HALF, HALF)]
            start(half, half, tf_s.at[k, way], tf_r.at[k, way], at_y(step))

    def take(k):
        spot = piece.at[mine(k)]
        copy(spot, spot, tz_s.at[k], tz_r.at[k], at_y(1)).wait_recv()
        to = across if k == 1 else fellow
        start_inner(
            spot, spot, tz_s.at[k + 1], tz_r.at[3 if k == 1 else k], (dp, y * N_ZL + to)
        )
        along_y(k)

    def w_rows(step):
        at = lax.rem(x + step, N_X) * SHARE
        return w_kv.at[core, :, pl.ds(pl.multiple_of(at, 16), SHARE)]

    def w_across(step):
        spot = w_rows(step)
        start(spot, spot, w3_s.at[step], w3_r.at[step], sibling)

    def w_arrived(step):
        spot = w_rows(N_X - step)
        copy(spot, spot, w2_s.at[step], w2_r.at[step], at_x(step)).wait_recv()
        w_across(N_X - step)

    def far_arrived(k):
        far = lax.rem(y + 2, N_Y) * N_ZL + line_of[k]
        for way in (0, 1):
            half = piece.at[far, pl.ds(way * HALF, HALF)]
            copy(half, half, tf_s.at[k, way], tf_r.at[k, way], at_y(1)).wait_recv()
        project(far)

    loads["w_query"].wait()
    project(mp)
    take(1)
    pass_on(0)
    got = w_kv.at[0, pl.ds(0, N_MP - 1), pl.ds(0, SHARE)]
    copy(got, got, w1_s, w1_r, at_mp(1)).wait_recv()
    for k in (1, 3, 2):
        start(w_rows(0), w_rows(0), w2_s.at[k], w2_r.at[k], at_x(k))
    w_across(0)
    project(mine(1))
    for way in (0, 1):
        project(near(0, way))
    take(2)
    line_send(d_all, c1_s, c1_r)
    project(mine(2))
    pass_on(1)
    take(3)
    project(mine(3))
    far_arrived(0)
    pass_on(2)
    for k in (1, 2, 3):
        for i, row, rows in ((0, table_row, tables), (1, source_row, sources)):
            copy(
                row, rows.at[k], ts_s.at[k, i], ts_r.at[k, i], at_zh(k)
            ).wait_recv()
    fetches = [
        pltpu.make_async_copy(tables, near_tables, load_s.at[13]),
        pltpu.make_async_copy(sources, near_sources, load_s.at[14]),
    ]
    for fetch in fetches:
        fetch.start()
    for fetch in fetches:
        fetch.wait()
    w_arrived(1)
    w_arrived(3)
    for way in (0, 1):
        project(near(1, way))
    for way in (0, 1):
        project(near(2, way))
    line_pass(d_all, c1_s, c1_r, cf_s, cf_r)
    pass_on(3)
    w_arrived(2)
    for way in (0, 1):
        project(near(3, way))
    far_arrived(1)
    far_arrived(2)
    line_rest(d_all, c1_s, c1_r)
    for k in (1, 3):
        deal(d_all, k, slot_of, d_send, d_slots, c2_s, c2_r)
    far_arrived(3)
    line_end(d_all, cf_s, cf_r)
    deal(d_all, 2, slot_of, d_send, d_slots, c2_s, c2_r)
    for k in range(N_X):
        at = lax.rem(x + k, N_X) * SHARE
        spot = w_kv.at[other, :, pl.ds(pl.multiple_of(at, 16), SHARE)]
        copy(spot, spot, w3_s.at[k], w3_r.at[k], sibling).wait_recv()
    gathered = piece[...].reshape(N_MP * WIDTH, TOKENS)
    for half in (0, 1):
        w_half = w_kv[half].reshape(N_MP * WIDTH, HEAD)
        acc_kv[half] = dot_tn(w_half, gathered)

    loads["q_gain"].wait()
    loads["k_gain"].wait()
    gain_q, gain_k = (
        jnp.broadcast_to(gain[...], (HEAD, HEAD)).T[:, :1] for gain in (q_gain, k_gain)
    )
    key_sum = acc_kv[0]
    k_inverse = lax.rsqrt(jnp.mean(key_sum * key_sum, axis=0, keepdims=True) + EPS)
    k_norm = (key_sum * k_inverse * gain_k).astype(BF16)
    value = acc_kv[1].astype(BF16)
    at_key = lax.broadcasted_iota(jnp.int32, (TOKENS, TOKENS), 0)
    at_query = lax.broadcasted_iota(jnp.int32, (TOKENS, TOKENS), 1)
    seen = ((at_key >> 5) == (at_query >> 5)) & (at_key <= at_query)
    saved = []
    for h in range(COLS // HEAD):
        query = acc_q[h * HEAD : (h + 1) * HEAD]
        inverse = lax.rsqrt(jnp.mean(query * query, axis=0, keepdims=True) + EPS)
        q_norm = (query * inverse * gain_q).astype(BF16)
        scores = jnp.where(seen, dot_tn(k_norm, q_norm) * SCALE, -1e30)
        raised = jnp.exp(scores - jnp.max(scores, axis=0, keepdims=True))
        probs = raised / jnp.sum(raised, axis=0, keepdims=True)
        p_half = probs.astype(BF16)
        out = dot_nn(value, p_half).T.astype(BF16)
        att_all[0][:, :, h * HEAD : (h + 1) * HEAD] = out.reshape(SEQS, LENGTH, HEAD)
        saved.append((query, inverse, q_norm, probs, p_half))
    def sent_to(k, rank):
        have = table[0, rank] if k == 0 else near_tables[k, 0, rank]
        return jnp.maximum(have, 0)

    line_send(att_all, a1_s, a1_r)
    deal(att_all, 0, sent_to, att_send, att_slots, a2_s, a2_r)

    dealt(d_slots, c2_s, c2_r)
    lane = lax.broadcasted_iota(jnp.int32, (1, N_DP * LENGTH), 1)
    target = jnp.zeros_like(lane)

    def sender(step, flip, k):
        of_x = lax.rem(x + N_X - step, N_X)
        of_core = other if flip else core
        return of_x * (N_ZH * N_CORE) + lax.rem(zh + k, N_ZH) * N_CORE + of_core

    for i, (step, flip) in enumerate(PAIRS + ((0, 0),)):
        for k in range(N_ZH):
            entry = table[0, sender(step, flip, k)]
            here = (lane >> 5) == i * N_ZH + k
            target = jnp.where(here, entry * LENGTH, target)
    target = jnp.where(target < 0, -1, target + (lane & (LENGTH - 1)))
    place = lax.broadcasted_iota(jnp.int32, (TOKENS, N_DP * LENGTH), 0)
    chosen = jnp.where(place == target, 1.0, 0.0).astype(BF16)
    d_rows = dot_nn(chosen, d_slots[...].reshape(N_DP * LENGTH, COLS))
    d_cols = d_rows.T.astype(BF16)
    d_knorm = jnp.zeros((HEAD, TOKENS), F32)
    d_value = jnp.zeros((HEAD, TOKENS), F32)
    d_queries = []
    for h in range(COLS // HEAD):
        query, inverse, q_norm, probs, p_half = saved[h]
        out_half = d_cols[h * HEAD : (h + 1) * HEAD]
        d_probs = dot_tn(value, out_half)
        d_value += dot_nt(out_half, p_half)
        centred = d_probs - jnp.sum(d_probs * probs, axis=0, keepdims=True)
        score_half = (probs * centred * SCALE).astype(BF16)
        d_qnorm = dot_nn(k_norm, score_half)
        d_knorm += dot_nt(q_norm, score_half)
        d_queries.append((query, inverse, gain_q, d_qnorm))
    d_key = rms_back(key_sum, k_inverse, gain_k, d_knorm).astype(BF16)
    d_value = d_value.astype(BF16)
    for q in (0, 1):
        dkv[q] = d_key[q * 64 : (q + 1) * 64]
        dkv[2 + q] = d_value[q * 64 : (q + 1) * 64]

    for k in (1, 2, 3):
        start(
            dkv.at[lax.rem(zl + k, N_ZL)],
            dkv_recv.at[k],
            k1_s.at[k],
            k1_r.at[k],
            at_zl(k),
        )

    for h in range(COLS // HEAD):
        d_query[:, h * HEAD : (h + 1) * HEAD] = rms_back(*d_queries[h]).T.astype(BF16)

    def x_at(step):
        return lax.rem(x + step, N_X)

    def zh_at(step):
        return lax.rem(zh + step, N_ZH)

    def partial_rows(to, into, which):
        rows = pl.ds(pl.multiple_of(which * HALF, 16), HALF)
        for i in range(N_X):
            total = dot_nn(piece[i * N_ZH + to, rows], d_query[...])
            into[to, i] = total.astype(BF16)

    def core_step(kz):
        to = zh_at(kz)
        copy(
            g_send.at[to], g_recv.at[to], gc_s.at[kz], gc_r.at[kz], sibling
        ).wait_recv()
        both = g_keep[to].astype(F32) + g_recv[to].astype(F32)
        g_keep[to] = both.astype(BF16)
        for k in (2, 1, 3):
            start(
                g_keep.at[to, x_at(k)],
                x_recv.at[to, k],
                gx_s.at[k, kz],
                gx_r.at[k, kz],
                at_x(k),
            )

    def x_step(kz):
        to = zh_at(kz)
        total = g_keep[to, x].astype(F32)
        for k in (1, 2, 3):
            spot = x_recv.at[to, k]
            copy(spot, spot, gx_s.at[k, kz], gx_r.at[k, kz], at_x(k)).wait_recv()
            total += x_recv[to, k].astype(F32)
        z_send[kz] = total.astype(BF16)
        if kz == 2:
            for way in (1, 3):
                some = part_for(way)
                start(
                    z_send.at[2, some],
                    z_pass.at[way],
                    gp_s.at[way],
                    gp_r.at[way],
                    at_zh(way),
                )
        elif kz:
            some = part_for(kz)
            copy(
                z_pass.at[kz], z_pass.at[kz], gp_s.at[kz], gp_r.at[kz], at_zh(kz)
            ).wait_recv()
            both = z_send[kz, some].astype(F32) + z_pass[kz].astype(F32)
            z_send[kz, some] = both.astype(BF16)
            start(z_send.at[kz], z_recv.at[kz], gz_s.at[kz], gz_r.at[kz], at_zh(kz))

    def part_for(way):
        return pl.ds(0 if way == 1 else HALF // 2, HALF // 2)

    order = (2, 1, 3, 0)

    def kv_place(i):
        step = lax.rem(i + N_ZH - zh, N_ZH)
        return jnp.where(
            step == 0, 3, jnp.where(step == 1, 1, jnp.where(step == 2, 0, 2))
        )

    def kv_core_step(k):
        copy(
            kv_part.at[other, k], kv_recv.at[k], vc_s.at[k], vc_r.at[k], sibling
        ).wait_recv()
        both = kv_part[core, k].astype(F32) + kv_recv[k].astype(F32)
        kv_sum[k] = both.astype(BF16)
        for part in (0, 1) if k else ():
            some = pl.ds(2 * part, 2)
            start(
                kv_sum.at[k, some],
                kv_x.at[k, some],
                vx_s.at[k, part],
                vx_r.at[k, part],
                at_x(k),
            )

    def kv_x_step(part):
        some = pl.ds(2 * part, 2)
        total = kv_sum[0, some].astype(F32)
        for k in (1, 2, 3):
            spot = kv_x.at[k, some]
            copy(
                spot, spot, vx_s.at[k, part], vx_r.at[k, part], at_x(k)
            ).wait_recv()
            total += kv_x[k, some].astype(F32)
        kv_zs[some] = total.astype(BF16)
        for p in (0, 1):
            k = order[2 * part + p]
            if k:
                start(
                    kv_zs.at[2 * part + p],
                    kv_z.at[k],
                    vz_s.at[k],
                    vz_r.at[k],
                    at_zh(k),
                )

    for kz in order:
        to = zh_at(kz)
        partial_rows(to, g_send, other)
        start(g_send.at[to], g_recv.at[to], gc_s.at[kz], gc_r.at[kz], sibling)
    for kz in order:
        partial_rows(zh_at(kz), g_keep, core)
    for k in (1, 2, 3):
        copy(
            dkv.at[0], dkv_recv.at[k], k1_s.at[k], k1_r.at[k], at_zl(k)
        ).wait_recv()
    total = dkv[zl].astype(F32)
    for k in (1, 2, 3):
        total += dkv_recv[k].astype(F32)
    dkv_all[y, zl] = total.astype(BF16)

    def quarter(step_y, k):
        of_y = lax.rem(y + N_Y - step_y, N_Y)
        return dkv_all.at[of_y, lax.rem(zl + N_ZL - k, N_ZL)]

    def quarter_along_y(k):
        spot = quarter(0, k)
        for step in (2, 1, 3):
            start(spot, spot, k3_s.at[k, step], k3_r.at[k, step], at_y(step))

    for k in (1, 2, 3):
        spot = quarter(0, 0)
        start(spot, spot, k2_s.at[k], k2_r.at[k], at_zl(k))
    quarter_along_y(0)
    core_step(2)
    core_step(1)
    for k in (1, 2, 3):
        spot = quarter(0, k)
        copy(spot, spot, k2_s.at[k], k2_r.at[k], at_zl(k)).wait_recv()
        quarter_along_y(k)
    line_pass(att_all, a1_s, a1_r, af_s, af_r)
    core_step(3)
    core_step(0)
    x_step(2)
    line_rest(att_all, a1_s, a1_r)
    for k in (1, 3):
        deal(att_all, k, sent_to, att_send, att_slots, a2_s, a2_r)
    for k in range(N_ZL):
        for step in (1, 2, 3):
            spot = quarter(step, k)
            copy(
                spot, spot, k3_s.at[k, step], k3_r.at[k, step], at_y(step)
            ).wait_recv()
    for step in order:
        rows = dkv_all[x_at(step)].reshape(2 * HEAD, TOKENS)
        product = dot_nt(rows, x_ref[...]).astype(BF16)
        for half in range(2):
            for i in range(N_ZH):
                for c in range(N_CORE):
                    first = half * HEAD + i * 32 + c * 16
                    kv_part[c, step, kv_place(i), half] = product[first : first + 16]
        start(
            kv_part.at[other, step],
            kv_recv.at[step],
            vc_s.at[step],
            vc_r.at[step],
            sibling,
        )
    for k in order:
        kv_core_step(k)
    x_step(1)
    line_end(att_all, af_s, af_r)
    deal(att_all, 2, sent_to, att_send, att_slots, a2_s, a2_r)
    x_step(3)
    kv_x_step(0)
    kv_x_step(1)
    x_step(0)
    total = z_send[0].astype(F32)
    for k in (1, 3):
        spot = z_recv.at[k]
        copy(spot, spot, gz_s.at[k], gz_r.at[k], at_zh(k)).wait_recv()
        total += z_recv[k].astype(F32)
    gq_out[...] = total

    total = kv_zs[3].astype(F32)
    for k in (1, 2, 3):
        copy(kv_zs.at[0], kv_z.at[k], vz_s.at[k], vz_r.at[k], at_zh(k)).wait_recv()
        total += kv_z[k].astype(F32)
    gk_out[...] = total[0][:, :WIDTH]
    gv_out[...] = total[1][:, :WIDTH]

    dealt(att_slots, a2_s, a2_r)
    for s in range(SEQS):
        rank = source[s]
        step = lax.rem(x + N_X - rank // (N_ZH * N_CORE), N_X)
        flip = lax.rem(rank + core, N_CORE)
        k = lax.rem((rank // N_CORE) % N_ZH + N_ZH - zh, N_ZH)
        place = lax.rem(step * N_CORE + flip + len(PAIRS), len(PAIRS) + 1)
        att_out[s] = att_slots[place, k]
    for made in sends:
        made.wait_send()

    @pl.when(inner)
    def _():
        for args in inner_sends:
            copy(*args).wait_send()


def finish(*refs):
    for src, dst in zip(refs[:4], refs[4:]):
        dst[...] = src[...]


def local(
    pool,
    send_table,
    slot_source,
    multiplicity,
    slot_weight,
    cotangent,
    w_query,
    w_key,
    w_value,
    query_gain,
    key_gain,
):
    dma = pltpu.SemaphoreType.DMA
    vmem = pl.BlockSpec(memory_space=pltpu.VMEM)
    out_shape = (
        jax.ShapeDtypeStruct((SEQS, LENGTH, COLS), BF16),
        jax.ShapeDtypeStruct((HALF, COLS), F32),
        jax.ShapeDtypeStruct((16, WIDTH), F32),
        jax.ShapeDtypeStruct((16, WIDTH), F32),
    )
    results = pl.pallas_call(
        kernel,
        out_shape=out_shape,
        in_specs=[pl.BlockSpec(memory_space=pl.ANY)] * 11,
        out_specs=(vmem,) * 4,
        scratch_shapes=[
            pltpu.SMEM((1, N_DP), jnp.int32),
            pltpu.SMEM((SEQS,), jnp.int32),
            pltpu.SMEM((SEQS,), jnp.int32),
            pltpu.SMEM((SEQS,), F32),
            pltpu.VMEM((SEQS, LENGTH, WIDTH), BF16),
            pltpu.VMEM((SEQS, LENGTH, COLS), BF16),
            pltpu.VMEM((N_MP * WIDTH, COLS), BF16),
            pltpu.VMEM((WIDTH, N_Y * HEAD), BF16),
            pltpu.VMEM((WIDTH, N_Y * HEAD), BF16),
            pltpu.VMEM((1, HEAD), F32),
            pltpu.VMEM((1, HEAD), F32),
            dma((15,)),
            pltpu.VMEM((1, N_DP), jnp.int32),
            pltpu.VMEM((SEQS,), jnp.int32),
            pltpu.VMEM((N_ZH, 1, N_DP), jnp.int32),
            pltpu.VMEM((N_ZH, SEQS), jnp.int32),
            pltpu.SMEM((N_ZH, 1, N_DP), jnp.int32),
            pltpu.SMEM((N_ZH, SEQS), jnp.int32),
            dma((4, 2)),
            dma((4, 2)),
            pltpu.VMEM((PADDED, TOKENS), BF16),
            pltpu.VMEM((N_Y, SHARE, HEAD), BF16),
            pltpu.VMEM((N_MP, WIDTH, TOKENS), BF16),
            pltpu.VMEM((2, N_MP, WIDTH, HEAD), BF16),
            *[pltpu.VMEM((SEQS + 1, LENGTH, COLS), BF16)] * N_ZH,
            pltpu.VMEM((len(PAIRS), N_ZH, LENGTH, COLS), BF16),
            pltpu.VMEM((len(PAIRS) + 1, N_ZH, LENGTH, COLS), BF16),
            pltpu.VMEM((COLS, TOKENS), F32),
            pltpu.VMEM((2, HEAD, TOKENS), F32),
            *[pltpu.VMEM((SEQS, LENGTH, COLS), BF16)] * N_ZH,
            pltpu.VMEM((len(PAIRS), N_ZH, LENGTH, COLS), BF16),
            pltpu.VMEM((len(PAIRS) + 1, N_ZH, LENGTH, COLS), BF16),
            pltpu.VMEM((TOKENS, COLS), BF16),
            pltpu.VMEM((N_X, N_ZH, HALF, COLS), BF16),
            pltpu.VMEM((N_X, N_ZH, HALF, COLS), BF16),
            pltpu.VMEM((N_X, N_ZH, HALF, COLS), BF16),
            pltpu.VMEM((N_X, N_ZH, HALF, COLS), BF16),
            pltpu.VMEM((N_ZH, HALF, COLS), BF16),
            pltpu.VMEM((N_ZH, HALF, COLS), BF16),
            pltpu.VMEM((N_ZH, HALF // 2, COLS), BF16),
            pltpu.VMEM((N_ZL, 64, TOKENS), BF16),
            pltpu.VMEM((N_ZL, 64, TOKENS), BF16),
            pltpu.VMEM((N_Y, N_ZL, 64, TOKENS), BF16),
            pltpu.VMEM((N_CORE, N_X, N_ZH, 2, 16, PADDED), BF16),
            pltpu.VMEM((N_X, N_ZH, 2, 16, PADDED), BF16),
            pltpu.VMEM((N_X, N_ZH, 2, 16, PADDED), BF16),
            pltpu.VMEM((N_X, N_ZH, 2, 16, PADDED), BF16),
            pltpu.VMEM((N_ZH, 2, 16, PADDED), BF16),
            pltpu.VMEM((N_ZH, 2, 16, PADDED), BF16),
            dma((5,)),
            dma((4,)),
            dma((4, 2)),
            dma((4, 2)),
            dma((4, 2)),
            dma((4, 2)),
            dma,
            dma,
            dma((4,)),
            dma((4,)),
            dma((4,)),
            dma((4,)),
            dma((2, 2)),
            dma((2, 2)),
            dma((2,)),
            dma((2,)),
            dma,
            dma,
            dma((2, 2)),
            dma((2, 2)),
            dma((2,)),
            dma((2,)),
            dma,
            dma,
            dma((4,)),
            dma((4,)),
            dma((4,)),
            dma((4,)),
            dma((4, 4)),
            dma((4, 4)),
            dma((4,)),
            dma((4,)),
            dma((4, 4)),
            dma((4, 4)),
            dma((4,)),
            dma((4,)),
            dma((4,)),
            dma((4,)),
            dma((4,)),
            dma((4,)),
            dma((4, 2)),
            dma((4, 2)),
            dma((4,)),
            dma((4,)),
        ],
        compiler_params=pltpu.CompilerParams(
            collective_id=0, has_side_effects=True, vmem_limit_bytes=60 * 1024 * 1024
        ),
        name="train_step",
    )(
        send_table,
        slot_source,
        multiplicity,
        slot_weight,
        pool,
        cotangent,
        w_query,
        w_key,
        w_value,
        query_gain.reshape(1, HEAD),
        key_gain.reshape(1, HEAD),
    )
    attended, grad_query, grad_key, grad_value = pl.pallas_call(
        finish,
        out_shape=out_shape,
        in_specs=[vmem] * 4,
        out_specs=[vmem] * 4,
        compiler_params=pltpu.CompilerParams(vmem_limit_bytes=60 * 1024 * 1024),
        name="results",
    )(*results)
    return attended, grad_query, grad_key.T, grad_value.T


def solution(mesh):
    return jax.shard_map(
        local,
        mesh=mesh,
        in_specs=(
            P("dp", None, "mp"),
            P("dp", None),
            P("dp"),
            P("dp"),
            P("dp"),
            P("dp", None, "mp"),
            P(None, "mp"),
            P("mp", None),
            P("mp", None),
            P(),
            P(),
        ),
        out_specs=(P("dp", None, "mp"), P("dp", "mp"), P("mp", "dp"), P("mp", "dp")),
        check_vma=False,
    )
```

```python
import functools
import math

import jax
import jax.numpy as jnp
from jax import lax
from jax.experimental import pallas as pl
from jax.experimental.pallas import tpu as pltpu
from jax.sharding import PartitionSpec as P

F32, BF16 = jnp.float32, jnp.bfloat16
MESH = pl.DeviceIdType.MESH

N_X, N_ZH, N_CORE, N_Y, N_ZL = 4, 4, 2, 4, 4
N_DP, N_MP = N_X * N_ZH * N_CORE, N_Y * N_ZL
SEQS, LENGTH, WIDTH = 8, 32, 320
TOKENS = SEQS * LENGTH
HEAD, COLS = 128, 256
PADDED = 384
SHARE = WIDTH // N_X
HALF = WIDTH // 2
EPS = 1e-6
PAIRS = ((0, 1), (1, 0), (1, 1), (2, 0), (2, 1), (3, 0), (3, 1))
SCALE = 1.0 / math.sqrt(HEAD)


def dot_nn(a, b):
    return lax.dot_general(a, b, (((1,), (0,)), ((), ())), preferred_element_type=F32)


def dot_tn(a, b):
    return lax.dot_general(a, b, (((0,), (0,)), ((), ())), preferred_element_type=F32)


def dot_nt(a, b):
    return lax.dot_general(a, b, (((1,), (1,)), ((), ())), preferred_element_type=F32)


def rms_back(values, inverse, gain, grad_out):
    scaled = grad_out * gain
    inner = jnp.mean(values * scaled, axis=0, keepdims=True)
    return inverse * scaled - values * (inverse * inverse * inverse) * inner


def kernel(
    table_in,
    source_in,
    drawn_in,
    weight_in,
    pool_in,
    cotangent_in,
    w_query_in,
    w_key_in,
    w_value_in,
    q_gain_in,
    k_gain_in,
    att_out,
    gq_out,
    gk_out,
    gv_out,
    table,
    source,
    drawn,
    weight,
    pool,
    cotangent,
    w_query,
    w_key,
    w_value,
    q_gain,
    k_gain,
    load_s,
    table_row,
    source_row,
    tables,
    sources,
    near_tables,
    near_sources,
    ts_s,
    ts_r,
    x_ref,
    w_mine,
    piece,
    w_kv,
    d_all_0,
    d_all_1,
    d_all_2,
    d_all_3,
    d_send,
    d_slots,
    acc_q,
    acc_kv,
    att_all_0,
    att_all_1,
    att_all_2,
    att_all_3,
    att_send,
    att_slots,
    d_query,
    g_send,
    g_recv,
    g_keep,
    x_recv,
    z_send,
    z_recv,
    z_pass,
    dkv,
    dkv_recv,
    dkv_all,
    kv_part,
    kv_recv,
    kv_sum,
    kv_x,
    kv_zs,
    kv_z,
    tz_s,
    tz_r,
    ty_s,
    ty_r,
    tf_s,
    tf_r,
    w1_s,
    w1_r,
    w2_s,
    w2_r,
    w3_s,
    w3_r,
    c1_s,
    c1_r,
    cf_s,
    cf_r,
    c2_s,
    c2_r,
    a1_s,
    a1_r,
    af_s,
    af_r,
    a2_s,
    a2_r,
    k1_s,
    k1_r,
    k2_s,
    k2_r,
    k3_s,
    k3_r,
    gc_s,
    gc_r,
    gx_s,
    gx_r,
    gp_s,
    gp_r,
    gz_s,
    gz_r,
    vc_s,
    vc_r,
    vx_s,
    vx_r,
    vz_s,
    vz_r,
):
    dp, mp = lax.axis_index("dp"), lax.axis_index("mp")
    x, zh, core = dp // (N_ZH * N_CORE), (dp // N_CORE) % N_ZH, dp % N_CORE
    y, zl = mp // N_ZL, mp % N_ZL
    other = 1 - core

    def pair(step, flip):
        return lax.rem(x + step, N_X) * (N_ZH * N_CORE) + zh * N_CORE + (
            other if flip else core
        )

    def at_mp(step):
        return dp, lax.rem(mp + step, N_MP)

    def at_x(step):
        return lax.rem(dp + step * (N_ZH * N_CORE), N_DP), mp

    def at_zh(step):
        return x * (N_ZH * N_CORE) + lax.rem(zh + step, N_ZH) * N_CORE + core, mp

    def at_y(step):
        return dp, lax.rem(mp + step * N_ZL, N_MP)

    def at_zl(step):
        return dp, y * N_ZL + lax.rem(zl + step, N_ZL)

    sibling = (dp + 1 - 2 * core, mp)
    d_all = (d_all_0, d_all_1, d_all_2, d_all_3)
    att_all = (att_all_0, att_all_1, att_all_2, att_all_3)

    def copy(src, dst, send, recv, device):
        return pltpu.make_async_remote_copy(
            src_ref=src,
            dst_ref=dst,
            send_sem=send,
            recv_sem=recv,
            device_id=device,
            device_id_type=MESH,
        )

    sends = []

    def start(*args):
        made = copy(*args)
        made.start()
        sends.append(made)

    barrier = pltpu.get_barrier_semaphore()
    partners = [at_mp(step) for step in range(1, N_MP)]
    partners += [at_zh(step) for step in range(1, N_ZH)]
    partners += [(pair(step, flip), mp) for step, flip in PAIRS]
    for device in partners:
        pl.semaphore_signal(barrier, inc=1, device_id=device, device_id_type=MESH)

    loads = {}
    for i, (name, src, dst) in enumerate(
        (
            ("pool", pool_in, pool),
            ("w_key", w_key_in, w_key),
            ("w_value", w_value_in, w_value),
            ("table_row", table_in, table_row),
            ("source_row", source_in, source_row),
            ("table", table_in, table),
            ("source", source_in, source),
            ("drawn", drawn_in, drawn),
            ("weight", weight_in, weight),
            ("cotangent", cotangent_in, cotangent),
            ("w_query", w_query_in, w_query),
            ("q_gain", q_gain_in, q_gain),
            ("k_gain", k_gain_in, k_gain),
        )
    ):
        loads[name] = pltpu.make_async_copy(src, dst, load_s.at[i])
        loads[name].start()

    for name in ("pool", "w_key", "w_value"):
        loads[name].wait()
    rows = pool[...].reshape(TOKENS, WIDTH).astype(F32)
    x_ref[:COLS] = rows[:, :COLS].T.astype(BF16)
    rest = [rows[:, COLS:], jnp.zeros((TOKENS, PADDED - WIDTH), F32)]
    x_ref[COLS:] = jnp.concatenate(rest, axis=1).T.astype(BF16)
    rows = pl.ds(pl.multiple_of(x * SHARE, 16), SHARE)
    for which, w_ref in ((0, w_key), (1, w_value)):

        @pl.when(core == which)
        def _():
            for g in range(N_Y):
                w_mine[g] = w_ref[rows, g * HEAD : (g + 1) * HEAD]

    loads["table_row"].wait()
    loads["source_row"].wait()
    pl.semaphore_wait(barrier, len(partners))

    fellow = zl + 1 - 2 * (zl % 2)
    across = N_ZL - 1 - zl
    inner = (zl == 1) | (zl == 2)
    line_of = (
        zl,
        fellow,
        jnp.where(zl < 2, jnp.int32(2), jnp.int32(1)),
        jnp.where(zl < 2, jnp.int32(3), jnp.int32(0)),
    )

    def mine(k):
        return y * N_ZL + line_of[k]

    def near(k, way):
        return lax.rem(y + (N_Y - 1 if way == 0 else 1), N_Y) * N_ZL + line_of[k]

    inner_sends = []

    def start_inner(*args):
        inner_sends.append(args)

        @pl.when(inner)
        def _():
            copy(*args).start()

    def along_y(k):
        spot = piece.at[mine(k)]
        for way, step in ((0, 1), (1, N_Y - 1)):
            start(spot, spot, ty_s.at[k, way], ty_r.at[k, way], at_y(step))

    piece[mp] = x_ref[:WIDTH]
    w_kv[core, mp, rows] = w_mine[y]
    for step in range(1, N_MP):
        dest = at_mp(step)
        start(w_mine.at[dest[1] // N_ZL], w_kv.at[core, mp, rows], w1_s, w1_r, dest)
    tokens = piece.at[mp]
    start(tokens, tokens, tz_s.at[0], tz_r.at[1], (dp, y * N_ZL + fellow))
    start_inner(tokens, tokens, tz_s.at[1], tz_r.at[2], (dp, y * N_ZL + across))
    along_y(0)

    for k in (1, 2, 3):
        start(table_row, tables.at[k], ts_s.at[k, 0], ts_r.at[k, 0], at_zh(N_ZH - k))
        start(source_row, sources.at[k], ts_s.at[k, 1], ts_r.at[k, 1], at_zh(N_ZH - k))

    half_slots = SEQS // 2

    def line_send(buf, send, recv):
        for part in (0, 1):
            for way, step in ((0, 1), (1, N_ZH - 1)):
                some = pl.ds((way ^ part) * half_slots, half_slots)
                start(
                    buf[0].at[some],
                    buf[N_ZH - 1 if way == 0 else 1].at[some],
                    send.at[way, part],
                    recv.at[way, part],
                    at_zh(step),
                )

    def line_wait(buf, send, recv, part, then):
        for way, step in ((0, 1), (1, N_ZH - 1)):
            some = pl.ds((way ^ part) * half_slots, half_slots)
            spot = buf[N_ZH - 1 if way == 0 else 1].at[some]
            copy(
                spot, spot, send.at[way, part], recv.at[way, part], at_zh(step)
            ).wait_recv()
            then(way, step, some, spot)

    def line_pass(buf, send, recv, send_on, recv_on):
        def on(way, step, some, spot):
            start(spot, buf[2].at[some], send_on.at[way], recv_on.at[way], at_zh(step))

        line_wait(buf, send, recv, 0, on)

    def line_rest(buf, send, recv):
        line_wait(buf, send, recv, 1, lambda *args: None)

    def line_end(buf, send_on, recv_on):
        for way in (0, 1):
            spot = buf[2].at[pl.ds(way * (SEQS // 2), SEQS // 2)]
            copy(spot, spot, send_on.at[way], recv_on.at[way], at_zh(1)).wait_recv()

    def deal(buf, k, pick, out, into, send, recv):
        for i, (step, flip) in enumerate(PAIRS):
            to = pair(step, flip)
            out[i, k] = buf[k][pick(k, to)]
            start(out.at[i, k], into.at[i, k], send, recv, (to, mp))
        into[len(PAIRS), k] = buf[k][pick(k, dp)]

    def dealt(into, send, recv):
        spot = into.at[pl.ds(0, len(PAIRS))]
        copy(spot, spot, send, recv, sibling).wait_recv()

    for name in ("drawn", "weight", "cotangent", "table", "source"):
        loads[name].wait()
    for s in range(SEQS):
        factor = drawn[s].astype(F32) * weight[s] * (1.0 / LENGTH)
        d_all[0][s] = (cotangent[s].astype(F32) * factor).astype(BF16)
    for k in range(N_ZH):
        d_all[k][SEQS] = jnp.zeros((LENGTH, COLS), BF16)

    def slot_of(k, rank):
        found = jnp.int32(SEQS)
        for s in range(SEQS):
            have = source[s] if k == 0 else near_sources[k, s]
            found = jnp.where(have == rank, jnp.int32(s), found)
        return found

    deal(d_all, 0, slot_of, d_send, d_slots, c2_s, c2_r)

    acc_q[...] = jnp.zeros_like(acc_q)

    def project(j):
        place = pl.ds(pl.multiple_of(j * WIDTH, WIDTH), WIDTH)
        acc_q[...] += dot_tn(w_query[place], piece[j])

    def wait_near(k, way):
        spot = piece.at[near(k, way)]
        copy(spot, spot, ty_s.at[k, way], ty_r.at[k, way], at_y(1)).wait_recv()

    def pass_on(k):
        for way, step in ((0, 1), (1, N_Y - 1)):
            wait_near(k, way)
            half = piece.at[near(k, way), pl.ds(way * HALF, HALF)]
            start(half, half, tf_s.at[k, way], tf_r.at[k, way], at_y(step))

    def take(k):
        spot = piece.at[mine(k)]
        copy(spot, spot, tz_s.at[k], tz_r.at[k], at_y(1)).wait_recv()
        to = across if k == 1 else fellow
        start_inner(
            spot, spot, tz_s.at[k + 1], tz_r.at[3 if k == 1 else k], (dp, y * N_ZL + to)
        )
        along_y(k)

    def w_rows(step):
        at = lax.rem(x + step, N_X) * SHARE
        return w_kv.at[core, :, pl.ds(pl.multiple_of(at, 16), SHARE)]

    def w_across(step):
        spot = w_rows(step)
        start(spot, spot, w3_s.at[step], w3_r.at[step], sibling)

    def w_arrived(step):
        spot = w_rows(N_X - step)
        copy(spot, spot, w2_s.at[step], w2_r.at[step], at_x(step)).wait_recv()
        w_across(N_X - step)

    def far_arrived(k):
        far = lax.rem(y + 2, N_Y) * N_ZL + line_of[k]
        for way in (0, 1):
            half = piece.at[far, pl.ds(way * HALF, HALF)]
            copy(half, half, tf_s.at[k, way], tf_r.at[k, way], at_y(1)).wait_recv()
        project(far)

    loads["w_query"].wait()
    project(mp)
    take(1)
    pass_on(0)
    got = w_kv.at[0, pl.ds(0, N_MP - 1), pl.ds(0, SHARE)]
    copy(got, got, w1_s, w1_r, at_mp(1)).wait_recv()
    for k in (1, 3, 2):
        start(w_rows(0), w_rows(0), w2_s.at[k], w2_r.at[k], at_x(k))
    w_across(0)
    project(mine(1))
    for way in (0, 1):
        project(near(0, way))
    take(2)
    line_send(d_all, c1_s, c1_r)
    project(mine(2))
    pass_on(1)
    take(3)
    project(mine(3))
    far_arrived(0)
    pass_on(2)
    for k in (1, 2, 3):
        for i, row, rows in ((0, table_row, tables), (1, source_row, sources)):
            copy(
                row, rows.at[k], ts_s.at[k, i], ts_r.at[k, i], at_zh(k)
            ).wait_recv()
    fetches = [
        pltpu.make_async_copy(tables, near_tables, load_s.at[13]),
        pltpu.make_async_copy(sources, near_sources, load_s.at[14]),
    ]
    for fetch in fetches:
        fetch.start()
    for fetch in fetches:
        fetch.wait()
    w_arrived(1)
    w_arrived(3)
    for way in (0, 1):
        project(near(1, way))
    for way in (0, 1):
        project(near(2, way))
    line_pass(d_all, c1_s, c1_r, cf_s, cf_r)
    pass_on(3)
    w_arrived(2)
    for way in (0, 1):
        project(near(3, way))
    far_arrived(1)
    far_arrived(2)
    line_rest(d_all, c1_s, c1_r)
    for k in (1, 3):
        deal(d_all, k, slot_of, d_send, d_slots, c2_s, c2_r)
    far_arrived(3)
    line_end(d_all, cf_s, cf_r)
    deal(d_all, 2, slot_of, d_send, d_slots, c2_s, c2_r)
    for k in range(N_X):
        at = lax.rem(x + k, N_X) * SHARE
        spot = w_kv.at[other, :, pl.ds(pl.multiple_of(at, 16), SHARE)]
        copy(spot, spot, w3_s.at[k], w3_r.at[k], sibling).wait_recv()
    gathered = piece[...].reshape(N_MP * WIDTH, TOKENS)
    for half in (0, 1):
        w_half = w_kv[half].reshape(N_MP * WIDTH, HEAD)
        acc_kv[half] = dot_tn(w_half, gathered)

    loads["q_gain"].wait()
    loads["k_gain"].wait()
    gain_q, gain_k = (
        jnp.broadcast_to(gain[...], (HEAD, HEAD)).T[:, :1] for gain in (q_gain, k_gain)
    )
    key_sum = acc_kv[0]
    k_inverse = lax.rsqrt(jnp.mean(key_sum * key_sum, axis=0, keepdims=True) + EPS)
    k_norm = (key_sum * k_inverse * gain_k).astype(BF16)
    value = acc_kv[1].astype(BF16)
    at_key = lax.broadcasted_iota(jnp.int32, (TOKENS, TOKENS), 0)
    at_query = lax.broadcasted_iota(jnp.int32, (TOKENS, TOKENS), 1)
    seen = ((at_key >> 5) == (at_query >> 5)) & (at_key <= at_query)
    saved = []
    for h in range(COLS // HEAD):
        query = acc_q[h * HEAD : (h + 1) * HEAD]
        inverse = lax.rsqrt(jnp.mean(query * query, axis=0, keepdims=True) + EPS)
        q_norm = (query * inverse * gain_q).astype(BF16)
        scores = jnp.where(seen, dot_tn(k_norm, q_norm) * SCALE, -1e30)
        raised = jnp.exp(scores - jnp.max(scores, axis=0, keepdims=True))
        probs = raised / jnp.sum(raised, axis=0, keepdims=True)
        p_half = probs.astype(BF16)
        out = dot_nn(value, p_half).T.astype(BF16)
        att_all[0][:, :, h * HEAD : (h + 1) * HEAD] = out.reshape(SEQS, LENGTH, HEAD)
        saved.append((query, inverse, q_norm, probs, p_half))
    def sent_to(k, rank):
        have = table[0, rank] if k == 0 else near_tables[k, 0, rank]
        return jnp.maximum(have, 0)

    line_send(att_all, a1_s, a1_r)
    deal(att_all, 0, sent_to, att_send, att_slots, a2_s, a2_r)

    dealt(d_slots, c2_s, c2_r)
    lane = lax.broadcasted_iota(jnp.int32, (1, N_DP * LENGTH), 1)
    target = jnp.zeros_like(lane)

    def sender(step, flip, k):
        of_x = lax.rem(x + N_X - step, N_X)
        of_core = other if flip else core
        return of_x * (N_ZH * N_CORE) + lax.rem(zh + k, N_ZH) * N_CORE + of_core

    for i, (step, flip) in enumerate(PAIRS + ((0, 0),)):
        for k in range(N_ZH):
            entry = table[0, sender(step, flip, k)]
            here = (lane >> 5) == i * N_ZH + k
            target = jnp.where(here, entry * LENGTH, target)
    target = jnp.where(target < 0, -1, target + (lane & (LENGTH - 1)))
    place = lax.broadcasted_iota(jnp.int32, (TOKENS, N_DP * LENGTH), 0)
    chosen = jnp.where(place == target, 1.0, 0.0).astype(BF16)
    d_rows = dot_nn(chosen, d_slots[...].reshape(N_DP * LENGTH, COLS))
    d_cols = d_rows.T.astype(BF16)
    d_knorm = jnp.zeros((HEAD, TOKENS), F32)
    d_value = jnp.zeros((HEAD, TOKENS), F32)
    d_queries = []
    for h in range(COLS // HEAD):
        query, inverse, q_norm, probs, p_half = saved[h]
        out_half = d_cols[h * HEAD : (h + 1) * HEAD]
        d_probs = dot_tn(value, out_half)
        d_value += dot_nt(out_half, p_half)
        centred = d_probs - jnp.sum(d_probs * probs, axis=0, keepdims=True)
        score_half = (probs * centred * SCALE).astype(BF16)
        d_qnorm = dot_nn(k_norm, score_half)
        d_knorm += dot_nt(q_norm, score_half)
        d_queries.append((query, inverse, gain_q, d_qnorm))
    d_key = rms_back(key_sum, k_inverse, gain_k, d_knorm).astype(BF16)
    d_value = d_value.astype(BF16)
    for q in (0, 1):
        dkv[q] = d_key[q * 64 : (q + 1) * 64]
        dkv[2 + q] = d_value[q * 64 : (q + 1) * 64]

    for k in (1, 2, 3):
        start(
            dkv.at[lax.rem(zl + k, N_ZL)],
            dkv_recv.at[k],
            k1_s.at[k],
            k1_r.at[k],
            at_zl(k),
        )

    for h in range(COLS // HEAD):
        d_query[:, h * HEAD : (h + 1) * HEAD] = rms_back(*d_queries[h]).T.astype(BF16)

    def x_at(step):
        return lax.rem(x + step, N_X)

    def zh_at(step):
        return lax.rem(zh + step, N_ZH)

    def partial_rows(to, into, which):
        rows = pl.ds(pl.multiple_of(which * HALF, 16), HALF)
        for i in range(N_X):
            total = dot_nn(piece[i * N_ZH + to, rows], d_query[...])
            into[to, i] = total.astype(BF16)

    def core_step(kz):
        to = zh_at(kz)
        copy(
            g_send.at[to], g_recv.at[to], gc_s.at[kz], gc_r.at[kz], sibling
        ).wait_recv()
        both = g_keep[to].astype(F32) + g_recv[to].astype(F32)
        g_keep[to] = both.astype(BF16)
        for k in (2, 1, 3):
            start(
                g_keep.at[to, x_at(k)],
                x_recv.at[to, k],
                gx_s.at[k, kz],
                gx_r.at[k, kz],
                at_x(k),
            )

    def x_step(kz):
        to = zh_at(kz)
        total = g_keep[to, x].astype(F32)
        for k in (1, 2, 3):
            spot = x_recv.at[to, k]
            copy(spot, spot, gx_s.at[k, kz], gx_r.at[k, kz], at_x(k)).wait_recv()
            total += x_recv[to, k].astype(F32)
        z_send[kz] = total.astype(BF16)
        if kz == 2:
            for way in (1, 3):
                some = part_for(way)
                start(
                    z_send.at[2, some],
                    z_pass.at[way],
                    gp_s.at[way],
                    gp_r.at[way],
                    at_zh(way),
                )
        elif kz:
            some = part_for(kz)
            copy(
                z_pass.at[kz], z_pass.at[kz], gp_s.at[kz], gp_r.at[kz], at_zh(kz)
            ).wait_recv()
            both = z_send[kz, some].astype(F32) + z_pass[kz].astype(F32)
            z_send[kz, some] = both.astype(BF16)
            start(z_send.at[kz], z_recv.at[kz], gz_s.at[kz], gz_r.at[kz], at_zh(kz))

    def part_for(way):
        return pl.ds(0 if way == 1 else HALF // 2, HALF // 2)

    order = (2, 1, 3, 0)

    def kv_place(i):
        step = lax.rem(i + N_ZH - zh, N_ZH)
        return jnp.where(
            step == 0, 3, jnp.where(step == 1, 1, jnp.where(step == 2, 0, 2))
        )

    def kv_core_step(k):
        copy(
            kv_part.at[other, k], kv_recv.at[k], vc_s.at[k], vc_r.at[k], sibling
        ).wait_recv()
        both = kv_part[core, k].astype(F32) + kv_recv[k].astype(F32)
        kv_sum[k] = both.astype(BF16)
        for part in (0, 1) if k else ():
            some = pl.ds(2 * part, 2)
            start(
                kv_sum.at[k, some],
                kv_x.at[k, some],
                vx_s.at[k, part],
                vx_r.at[k, part],
                at_x(k),
            )

    def kv_x_step(part):
        some = pl.ds(2 * part, 2)
        total = kv_sum[0, some].astype(F32)
        for k in (1, 2, 3):
            spot = kv_x.at[k, some]
            copy(
                spot, spot, vx_s.at[k, part], vx_r.at[k, part], at_x(k)
            ).wait_recv()
            total += kv_x[k, some].astype(F32)
        kv_zs[some] = total.astype(BF16)
        for p in (0, 1):
            k = order[2 * part + p]
            if k:
                start(
                    kv_zs.at[2 * part + p],
                    kv_z.at[k],
                    vz_s.at[k],
                    vz_r.at[k],
                    at_zh(k),
                )

    for kz in order:
        to = zh_at(kz)
        partial_rows(to, g_send, other)
        start(g_send.at[to], g_recv.at[to], gc_s.at[kz], gc_r.at[kz], sibling)
    for kz in order:
        partial_rows(zh_at(kz), g_keep, core)
    for k in (1, 2, 3):
        copy(
            dkv.at[0], dkv_recv.at[k], k1_s.at[k], k1_r.at[k], at_zl(k)
        ).wait_recv()
    total = dkv[zl].astype(F32)
    for k in (1, 2, 3):
        total += dkv_recv[k].astype(F32)
    dkv_all[y, zl] = total.astype(BF16)

    def quarter(step_y, k):
        of_y = lax.rem(y + N_Y - step_y, N_Y)
        return dkv_all.at[of_y, lax.rem(zl + N_ZL - k, N_ZL)]

    def quarter_along_y(k):
        spot = quarter(0, k)
        for step in (2, 1, 3):
            start(spot, spot, k3_s.at[k, step], k3_r.at[k, step], at_y(step))

    for k in (1, 2, 3):
        spot = quarter(0, 0)
        start(spot, spot, k2_s.at[k], k2_r.at[k], at_zl(k))
    quarter_along_y(0)
    core_step(2)
    core_step(1)
    for k in (1, 2, 3):
        spot = quarter(0, k)
        copy(spot, spot, k2_s.at[k], k2_r.at[k], at_zl(k)).wait_recv()
        quarter_along_y(k)
    line_pass(att_all, a1_s, a1_r, af_s, af_r)
    core_step(3)
    core_step(0)
    x_step(2)
    line_rest(att_all, a1_s, a1_r)
    for k in (1, 3):
        deal(att_all, k, sent_to, att_send, att_slots, a2_s, a2_r)
    for k in range(N_ZL):
        for step in (1, 2, 3):
            spot = quarter(step, k)
            copy(
                spot, spot, k3_s.at[k, step], k3_r.at[k, step], at_y(step)
            ).wait_recv()
    for step in order:
        rows = dkv_all[x_at(step)].reshape(2 * HEAD, TOKENS)
        product = dot_nt(rows, x_ref[...])[:, :WIDTH]
        both = jnp.concatenate([product[:HEAD], product[HEAD:]], axis=1).astype(BF16)
        for i in range(N_ZH):
            for c in range(N_CORE):
                first = i * 32 + c * 16
                kv_part[c, step, kv_place(i)] = both[first : first + 16]
        start(
            kv_part.at[other, step],
            kv_recv.at[step],
            vc_s.at[step],
            vc_r.at[step],
            sibling,
        )
    for k in order:
        kv_core_step(k)
    x_step(1)
    line_end(att_all, af_s, af_r)
    deal(att_all, 2, sent_to, att_send, att_slots, a2_s, a2_r)
    x_step(3)
    kv_x_step(0)
    kv_x_step(1)
    x_step(0)
    total = z_send[0].astype(F32)
    for k in (1, 3):
        spot = z_recv.at[k]
        copy(spot, spot, gz_s.at[k], gz_r.at[k], at_zh(k)).wait_recv()
        total += z_recv[k].astype(F32)
    gq_out[...] = total

    total = kv_zs[3].astype(F32)
    for k in (1, 2, 3):
        copy(kv_zs.at[0], kv_z.at[k], vz_s.at[k], vz_r.at[k], at_zh(k)).wait_recv()
        total += kv_z[k].astype(F32)
    gk_out[...] = total[:, :WIDTH]
    gv_out[...] = total[:, WIDTH:]

    dealt(att_slots, a2_s, a2_r)
    for s in range(SEQS):
        rank = source[s]
        step = lax.rem(x + N_X - rank // (N_ZH * N_CORE), N_X)
        flip = lax.rem(rank + core, N_CORE)
        k = lax.rem((rank // N_CORE) % N_ZH + N_ZH - zh, N_ZH)
        place = lax.rem(step * N_CORE + flip + len(PAIRS), len(PAIRS) + 1)
        att_out[s] = att_slots[place, k]
    for made in sends:
        made.wait_send()

    @pl.when(inner)
    def _():
        for args in inner_sends:
            copy(*args).wait_send()


def finish(*refs):
    for src, dst in zip(refs[:4], refs[4:]):
        dst[...] = src[...]


def local(
    pool,
    send_table,
    slot_source,
    multiplicity,
    slot_weight,
    cotangent,
    w_query,
    w_key,
    w_value,
    query_gain,
    key_gain,
):
    dma = pltpu.SemaphoreType.DMA
    vmem = pl.BlockSpec(memory_space=pltpu.VMEM)
    out_shape = (
        jax.ShapeDtypeStruct((SEQS, LENGTH, COLS), BF16),
        jax.ShapeDtypeStruct((HALF, COLS), F32),
        jax.ShapeDtypeStruct((16, WIDTH), F32),
        jax.ShapeDtypeStruct((16, WIDTH), F32),
    )
    results = pl.pallas_call(
        kernel,
        out_shape=out_shape,
        in_specs=[pl.BlockSpec(memory_space=pl.ANY)] * 11,
        out_specs=(vmem,) * 4,
        scratch_shapes=[
            pltpu.SMEM((1, N_DP), jnp.int32),
            pltpu.SMEM((SEQS,), jnp.int32),
            pltpu.SMEM((SEQS,), jnp.int32),
            pltpu.SMEM((SEQS,), F32),
            pltpu.VMEM((SEQS, LENGTH, WIDTH), BF16),
            pltpu.VMEM((SEQS, LENGTH, COLS), BF16),
            pltpu.VMEM((N_MP * WIDTH, COLS), BF16),
            pltpu.VMEM((WIDTH, N_Y * HEAD), BF16),
            pltpu.VMEM((WIDTH, N_Y * HEAD), BF16),
            pltpu.VMEM((1, HEAD), F32),
            pltpu.VMEM((1, HEAD), F32),
            dma((15,)),
            pltpu.VMEM((1, N_DP), jnp.int32),
            pltpu.VMEM((SEQS,), jnp.int32),
            pltpu.VMEM((N_ZH, 1, N_DP), jnp.int32),
            pltpu.VMEM((N_ZH, SEQS), jnp.int32),
            pltpu.SMEM((N_ZH, 1, N_DP), jnp.int32),
            pltpu.SMEM((N_ZH, SEQS), jnp.int32),
            dma((4, 2)),
            dma((4, 2)),
            pltpu.VMEM((PADDED, TOKENS), BF16),
            pltpu.VMEM((N_Y, SHARE, HEAD), BF16),
            pltpu.VMEM((N_MP, WIDTH, TOKENS), BF16),
            pltpu.VMEM((2, N_MP, WIDTH, HEAD), BF16),
            *[pltpu.VMEM((SEQS + 1, LENGTH, COLS), BF16)] * N_ZH,
            pltpu.VMEM((len(PAIRS), N_ZH, LENGTH, COLS), BF16),
            pltpu.VMEM((len(PAIRS) + 1, N_ZH, LENGTH, COLS), BF16),
            pltpu.VMEM((COLS, TOKENS), F32),
            pltpu.VMEM((2, HEAD, TOKENS), F32),
            *[pltpu.VMEM((SEQS, LENGTH, COLS), BF16)] * N_ZH,
            pltpu.VMEM((len(PAIRS), N_ZH, LENGTH, COLS), BF16),
            pltpu.VMEM((len(PAIRS) + 1, N_ZH, LENGTH, COLS), BF16),
            pltpu.VMEM((TOKENS, COLS), BF16),
            pltpu.VMEM((N_X, N_ZH, HALF, COLS), BF16),
            pltpu.VMEM((N_X, N_ZH, HALF, COLS), BF16),
            pltpu.VMEM((N_X, N_ZH, HALF, COLS), BF16),
            pltpu.VMEM((N_X, N_ZH, HALF, COLS), BF16),
            pltpu.VMEM((N_ZH, HALF, COLS), BF16),
            pltpu.VMEM((N_ZH, HALF, COLS), BF16),
            pltpu.VMEM((N_ZH, HALF // 2, COLS), BF16),
            pltpu.VMEM((N_ZL, 64, TOKENS), BF16),
            pltpu.VMEM((N_ZL, 64, TOKENS), BF16),
            pltpu.VMEM((N_Y, N_ZL, 64, TOKENS), BF16),
            pltpu.VMEM((N_CORE, N_X, N_ZH, 16, 2 * WIDTH), BF16),
            pltpu.VMEM((N_X, N_ZH, 16, 2 * WIDTH), BF16),
            pltpu.VMEM((N_X, N_ZH, 16, 2 * WIDTH), BF16),
            pltpu.VMEM((N_X, N_ZH, 16, 2 * WIDTH), BF16),
            pltpu.VMEM((N_ZH, 16, 2 * WIDTH), BF16),
            pltpu.VMEM((N_ZH, 16, 2 * WIDTH), BF16),
            dma((5,)),
            dma((4,)),
            dma((4, 2)),
            dma((4, 2)),
            dma((4, 2)),
            dma((4, 2)),
            dma,
            dma,
            dma((4,)),
            dma((4,)),
            dma((4,)),
            dma((4,)),
            dma((2, 2)),
            dma((2, 2)),
            dma((2,)),
            dma((2,)),
            dma,
            dma,
            dma((2, 2)),
            dma((2, 2)),
            dma((2,)),
            dma((2,)),
            dma,
            dma,
            dma((4,)),
            dma((4,)),
            dma((4,)),
            dma((4,)),
            dma((4, 4)),
            dma((4, 4)),
            dma((4,)),
            dma((4,)),
            dma((4, 4)),
            dma((4, 4)),
            dma((4,)),
            dma((4,)),
            dma((4,)),
            dma((4,)),
            dma((4,)),
            dma((4,)),
            dma((4, 2)),
            dma((4, 2)),
            dma((4,)),
            dma((4,)),
        ],
        compiler_params=pltpu.CompilerParams(
            collective_id=0, has_side_effects=True, vmem_limit_bytes=60 * 1024 * 1024
        ),
        name="train_step",
    )(
        send_table,
        slot_source,
        multiplicity,
        slot_weight,
        pool,
        cotangent,
        w_query,
        w_key,
        w_value,
        query_gain.reshape(1, HEAD),
        key_gain.reshape(1, HEAD),
    )
    attended, grad_query, grad_key, grad_value = pl.pallas_call(
        finish,
        out_shape=out_shape,
        in_specs=[vmem] * 4,
        out_specs=[vmem] * 4,
        compiler_params=pltpu.CompilerParams(vmem_limit_bytes=60 * 1024 * 1024),
        name="results",
    )(*results)
    return attended, grad_query, grad_key.T, grad_value.T


def solution(mesh):
    return jax.shard_map(
        local,
        mesh=mesh,
        in_specs=(
            P("dp", None, "mp"),
            P("dp", None),
            P("dp"),
            P("dp"),
            P("dp"),
            P("dp", None, "mp"),
            P(None, "mp"),
            P("mp", None),
            P("mp", None),
            P(),
            P(),
        ),
        out_specs=(P("dp", None, "mp"), P("dp", "mp"), P("mp", "dp"), P("mp", "dp")),
        check_vma=False,
    )
```
